32 devices in a mesh: chan: 2 (over y), dp: 16 (over z, x, core).
Axes of the slice: x: 2, y: 2, z: 4, core: 2. Of those that a mesh axis runs over, the one named last changes fastest.
Arguments:
- volume: bfloat16 [32, 32, 32, 256], P('dp', None, None, 'chan'), may hold values from -6 to 6
- filter_one: bfloat16 [3, 3, 3, 256, 256], P(None, None, None, 'chan'), may hold values from -0.078125 to 0.078125
- filter_two: bfloat16 [3, 3, 3, 256, 256], P(None, None, None, 'chan'), may hold values from -0.078125 to 0.078125
- cotangent: bfloat16 [32, 32, 32, 256], P('dp', None, None, 'chan'), may hold values from -6 to 6
Outputs:
- output: bfloat16 [32, 32, 32, 256], P('dp', None, None, 'chan')
- input_grad: bfloat16 [32, 32, 32, 256], P('dp', None, None, 'chan')
- grad_one: float32 [3, 3, 3, 256, 256], P(None, None, None, 'chan')
- grad_two: float32 [3, 3, 3, 256, 256], P(None, None, None, 'chan')
The draws below stay inside these ranges and needn't reach their ends.
All inputs are finite; a program needn't handle non-finite values.
Results may differ from the reference program's by a relative error of at most 0.02525.
The reference program's roundings to bfloat16 on the way (of `act_one`, `delta_two` and `delta_one`) count: a program that leaves them out, or rounds other values in their place, can miss the bound.
Values may be sent and summed in bfloat16 or wider, within the bound.
No kernel may reach another device: no remote copies, remote signals or barrier semaphores. Data moves between devices by JAX's collectives and lax.ppermute only.
A program may use at most 128 MiB of HBM per device.

```python
import math
import jax
import jax.numpy as jnp
from jax import lax

C = 256
VOX = 32
ROWS = 32
SAMPLES = 1


def block_levels(own_key, extent, cuts, smallest, high):
    factor_of = 1.0
    for axis_at, shards_of in cuts:
        steps = jax.random.uniform(jax.random.fold_in(jax.random.fold_in(own_key, 6), axis_at), (shards_of,), jnp.float32, smallest / len(cuts), high / len(cuts))
        factor_of = factor_of * jnp.repeat(jnp.exp(steps), extent[axis_at] // shards_of).reshape((-1,) + (1,) * (len(extent) - 1 - axis_at))
    return factor_of


def scatter_about(rng, extent, scale, limit, shards=(), dtype=jnp.bfloat16):
    loudness = block_levels(rng, extent, shards, -0.22, 0.18) if shards else 1.0
    drawn = jax.random.normal(rng, extent, jnp.float32) * scale * loudness
    return jnp.minimum(jnp.maximum(drawn, -limit), limit).astype(dtype)


def setup_inputs(seed: int = 0) -> dict:
    keys = jax.random.split(jax.random.key(seed), 5)
    volume = scatter_about(keys[0], (ROWS, VOX, VOX, C), 1.0, 6.0, ((0, 16), (3, 2)))
    filter_one = scatter_about(keys[1], (3, 3, 3, C, C), (27 * C) ** -0.5, 0.078125, ((3, 2),))
    filter_two = scatter_about(keys[2], (3, 3, 3, C, C), (27 * C) ** -0.5, 0.078125, ((3, 2),))
    cotangent = scatter_about(keys[3], (ROWS, VOX, VOX, C), 1.0, 6.0, ((0, 16), (3, 2)))
    return dict(volume=volume, filter_one=filter_one, filter_two=filter_two, cotangent=cotangent)


SLOPE = 0.3

def leaky(values):
    return jnp.where(values > 0, values, SLOPE * values)

def slope_of(values):
    return jnp.where(values > 0, jnp.float32(1.0), jnp.float32(SLOPE))

def padded(cubes):
    return jnp.pad(cubes.astype(jnp.float32), ((0, 0), (1, 1), (1, 1), (1, 1), (0, 0)))

def conv(cubes, weight):
    samples, depth, height, width_w, inner = cubes.shape
    source = padded(cubes)
    weights = weight.astype(jnp.float32)
    total = jnp.zeros((samples * depth * height * width_w, weight.shape[4]), jnp.float32)
    for a in range(3):
        for b in range(3):
            for c in range(3):
                piece = source[:, a:a + depth, b:b + height, c:c + width_w, :].reshape(-1, inner)
                total = total + jnp.dot(piece, weights[a, b, c], precision=lax.Precision.HIGHEST)
    return total

def conv_back(delta, weight):
    samples, depth, height, width_w, outer = delta.shape
    source = padded(delta)
    weights = weight.astype(jnp.float32)
    total = jnp.zeros((samples * depth * height * width_w, weight.shape[3]), jnp.float32)
    for a in range(3):
        for b in range(3):
            for c in range(3):
                piece = source[:, 2 - a:2 - a + depth, 2 - b:2 - b + height, 2 - c:2 - c + width_w, :].reshape(-1, outer)
                total = total + jnp.dot(piece, weights[a, b, c].T, precision=lax.Precision.HIGHEST)
    return total

def filter_grad(cubes, delta):
    samples, depth, height, width_w, inner = cubes.shape
    source = padded(cubes)
    flat = delta.astype(jnp.float32).reshape(-1, delta.shape[4])
    taps = []
    for a in range(3):
        for b in range(3):
            for c in range(3):
                piece = source[:, a:a + depth, b:b + height, c:c + width_w, :].reshape(-1, inner)
                taps.append(jnp.dot(piece.T, flat, precision=lax.Precision.HIGHEST))
    return jnp.stack(taps).reshape(3, 3, 3, inner, flat.shape[1])

def reference(volume, filter_one, filter_two, cotangent):
    shape = (SAMPLES, VOX, VOX, VOX, C)
    cubes = jnp.roll(volume, -1, axis=0).reshape(shape)
    cot = jnp.roll(cotangent, -1, axis=0)
    scale = 1.0 / math.sqrt(SAMPLES * VOX * VOX * VOX)
    pre_one = conv(cubes, filter_one)
    act_one = leaky(pre_one).astype(jnp.bfloat16)
    pre_two = conv(act_one.reshape(shape), filter_two)
    output = leaky(pre_two).astype(jnp.bfloat16)
    delta_two = (cot.reshape(-1, C).astype(jnp.float32) * slope_of(pre_two)).astype(jnp.bfloat16)
    grad_two = filter_grad(act_one.reshape(shape), delta_two.reshape(shape)) * scale
    back_two = conv_back(delta_two.reshape(shape), filter_two)
    delta_one = (back_two * slope_of(pre_one)).astype(jnp.bfloat16)
    grad_one = filter_grad(cubes, delta_one.reshape(shape)) * scale
    input_grad = conv_back(delta_one.reshape(shape), filter_one).astype(jnp.bfloat16)
    output = jnp.roll(output.reshape(volume.shape), 1, axis=0)
    input_grad = jnp.roll(input_grad.reshape(volume.shape), 1, axis=0)
    return (output, input_grad, grad_one, grad_two)
```

```python
import math

import jax
import jax.numpy as jnp
from jax import lax
from jax.sharding import PartitionSpec as P

VOX = 32


SLOPE = 0.3


def extended(block, sides, width):
    for axis, dim in sides:
        count = lax.axis_size(axis)
        forward = [(i, i + 1) for i in range(count - 1)]
        forward.append((count - 1, 0))
        backward = [(target, source) for source, target in forward]
        low = lax.ppermute(
            lax.slice_in_dim(block, block.shape[dim] - width, None, axis=dim), axis, forward
        )
        high = lax.ppermute(lax.slice_in_dim(block, 0, width, axis=dim), axis, backward)
        block = jnp.concatenate([low, block, high], axis=dim)
    return block


def leaky(values):
    return jnp.where(values > 0, values, SLOPE * values)


def slope_of(values):
    return jnp.where(values > 0, jnp.float32(1.0), jnp.float32(SLOPE))


def tap_mask(rows, offset):
    base = lax.axis_index("dp") * rows
    total_rows = lax.axis_size("dp") * rows
    planes = jnp.mod(base + jnp.arange(rows, dtype=jnp.int32) - 1, total_rows)
    depth = jnp.mod(planes, VOX) + offset
    inside = jnp.logical_and(depth >= 0, depth < VOX)
    return inside[:, None, None, None]


def pad_plane(values):
    return jnp.pad(values, ((0, 0), (1, 1), (1, 1), (0, 0)))


def columns(plane, rows, height, breadth):
    taps = []
    for a in range(3):
        inside = tap_mask(rows, a - 1)
        depth_slab = plane[a : a + rows]
        depth_slab = jnp.where(inside, depth_slab, jnp.zeros_like(depth_slab))
        for b in range(3):
            for c in range(3):
                taps.append(depth_slab[:, b : b + height, c : c + breadth, :])
    stacked = jnp.concatenate(taps, axis=-1)
    return stacked.reshape(rows * height * breadth, stacked.shape[-1])


def local(volume, filter_one, filter_two, cotangent):
    rows, height, breadth, narrow = volume.shape
    full = filter_one.shape[4]
    voxels = rows * height * breadth
    scale = 1.0 / math.sqrt(lax.axis_size("dp") * voxels)

    def forward(activity, weight):
        rim = extended(activity, (("dp", 0),), 1)
        plane = pad_plane(rim)
        stacked = columns(plane, rows, height, breadth)
        partial_value = jnp.dot(
            stacked, weight.reshape(27 * narrow, full), preferred_element_type=jnp.float32
        )
        summed = lax.psum_scatter(partial_value, "chan", scatter_dimension=1, tiled=True)
        return (plane, summed)

    def backward(plane, delta, weight):
        wide = lax.all_gather(delta, "chan", axis=3, tiled=True)
        rim = extended(wide, (("dp", 0),), 1)
        centre = rim[1 : rows + 1].reshape(voxels, full)
        stacked = columns(plane, rows, height, breadth)
        weight_grad = lax.dot_general(
            stacked, centre, (((0,), (0,)), ((), ())), preferred_element_type=jnp.float32
        )
        weight_grad = weight_grad.reshape(3, 3, 3, narrow, full)
        source = pad_plane(rim)
        total = jnp.zeros((rows, height, breadth, narrow), jnp.float32)
        for a in range(3):
            depth_slab = source[2 - a : 2 - a + rows]
            flat = depth_slab.reshape(-1, full)
            product = lax.dot_general(
                flat,
                weight[a].reshape(9 * narrow, full),
                (((1,), (1,)), ((), ())),
                preferred_element_type=jnp.float32,
            )
            product = product.reshape(rows, height + 2, breadth + 2, 9, narrow)
            part = jnp.zeros((rows, height, breadth, narrow), jnp.float32)
            for b in range(3):
                for c in range(3):
                    part = (
                        part
                        + product[:, 2 - b : 2 - b + height, 2 - c : 2 - c + breadth, b * 3 + c, :]
                    )
            inside = tap_mask(rows, 1 - a)
            total = total + jnp.where(inside, part, jnp.zeros_like(part))
        return (weight_grad, total.reshape(voxels, narrow))

    def layer_sum(weight_grad):
        return lax.psum(weight_grad.astype(jnp.bfloat16), "dp")

    plane_one, pre_one = forward(volume, filter_one)
    act_one = leaky(pre_one).astype(jnp.bfloat16).reshape(rows, height, breadth, narrow)
    plane_two, pre_two = forward(act_one, filter_two)
    output = leaky(pre_two).astype(jnp.bfloat16).reshape(rows, height, breadth, narrow)
    delta_two = (cotangent.reshape(voxels, narrow).astype(jnp.float32) * slope_of(pre_two)).astype(
        jnp.bfloat16
    )
    local_two, back_two = backward(
        plane_two, delta_two.reshape(rows, height, breadth, narrow), filter_two
    )
    summed_two = layer_sum(local_two)
    delta_one = (back_two * slope_of(pre_one)).astype(jnp.bfloat16)
    local_one, back_one = backward(
        plane_one, delta_one.reshape(rows, height, breadth, narrow), filter_one
    )
    local_one, summed_two = lax.optimization_barrier((local_one, summed_two))
    summed_one = layer_sum(local_one)
    input_grad = back_one.astype(jnp.bfloat16).reshape(rows, height, breadth, narrow)
    grad_one = summed_one.astype(jnp.float32) * scale
    grad_two = summed_two.astype(jnp.float32) * scale
    return (output, input_grad, grad_one, grad_two)


def solution(mesh):
    in_specs = (
        P("dp", None, None, "chan"),
        P(None, None, None, "chan", None),
        P(None, None, None, "chan", None),
        P("dp", None, None, "chan"),
    )
    out_specs = (
        P("dp", None, None, "chan"),
        P("dp", None, None, "chan"),
        P(None, None, None, "chan", None),
        P(None, None, None, "chan", None),
    )
    return jax.shard_map(local, mesh=mesh, in_specs=in_specs, out_specs=out_specs, check_vma=False)
```

```python
import functools
import math

import jax
import jax.numpy as jnp
from jax import lax
from jax.experimental import pallas as pl
from jax.experimental.pallas import tpu as pltpu
from jax.sharding import PartitionSpec as P

VOX = 32
SLOPE = 0.3
HALF = 128
FULL = 256
TILE = 16
VMEM_LIMIT = 40 * 1024 * 1024


def extended(block, sides, width):
    for axis, dim in sides:
        count = lax.axis_size(axis)
        forward = [(i, i + 1) for i in range(count - 1)]
        forward.append((count - 1, 0))
        backward = [(target, source) for source, target in forward]
        low = lax.ppermute(
            lax.slice_in_dim(block, block.shape[dim] - width, None, axis=dim), axis, forward
        )
        high = lax.ppermute(lax.slice_in_dim(block, 0, width, axis=dim), axis, backward)
        block = jnp.concatenate([low, block, high], axis=dim)
    return block


def leaky(values):
    return jnp.where(values > 0, values, SLOPE * values)


def slope_of(values):
    return jnp.where(values > 0, jnp.float32(1.0), jnp.float32(SLOPE))


def tap_mask(rows, offset):
    base = lax.axis_index("dp") * rows
    total_rows = lax.axis_size("dp") * rows
    planes = jnp.mod(base + jnp.arange(rows, dtype=jnp.int32) - 1, total_rows)
    depth = jnp.mod(planes, VOX) + offset
    inside = jnp.logical_and(depth >= 0, depth < VOX)
    return inside[:, None, None, None]


def pad_plane(values):
    return jnp.pad(values, ((0, 0), (1, 1), (1, 1), (0, 0)))


def columns(plane, rows, height, breadth):
    taps = []
    for a in range(3):
        inside = tap_mask(rows, a - 1)
        depth_slab = plane[a : a + rows]
        depth_slab = jnp.where(inside, depth_slab, jnp.zeros_like(depth_slab))
        for b in range(3):
            for c in range(3):
                taps.append(depth_slab[:, b : b + height, c : c + breadth, :])
    stacked = jnp.concatenate(taps, axis=-1)
    return stacked.reshape(rows * height * breadth, stacked.shape[-1])


def plain(volume, filter_one, filter_two, cotangent):
    rows, height, breadth, narrow = volume.shape
    full = filter_one.shape[4]
    voxels = rows * height * breadth
    scale = 1.0 / math.sqrt(lax.axis_size("dp") * voxels)

    def forward(activity, weight):
        rim = extended(activity, (("dp", 0),), 1)
        plane = pad_plane(rim)
        stacked = columns(plane, rows, height, breadth)
        partial_value = jnp.dot(
            stacked, weight.reshape(27 * narrow, full), preferred_element_type=jnp.float32
        )
        summed = lax.psum_scatter(partial_value, "chan", scatter_dimension=1, tiled=True)
        return (plane, summed)

    def backward(plane, delta, weight):
        wide = lax.all_gather(delta, "chan", axis=3, tiled=True)
        rim = extended(wide, (("dp", 0),), 1)
        centre = rim[1 : rows + 1].reshape(voxels, full)
        stacked = columns(plane, rows, height, breadth)
        weight_grad = lax.dot_general(
            stacked, centre, (((0,), (0,)), ((), ())), preferred_element_type=jnp.float32
        )
        weight_grad = weight_grad.reshape(3, 3, 3, narrow, full)
        source = pad_plane(rim)
        total = jnp.zeros((rows, height, breadth, narrow), jnp.float32)
        for a in range(3):
            depth_slab = source[2 - a : 2 - a + rows]
            flat = depth_slab.reshape(-1, full)
            product = lax.dot_general(
                flat,
                weight[a].reshape(9 * narrow, full),
                (((1,), (1,)), ((), ())),
                preferred_element_type=jnp.float32,
            )
            product = product.reshape(rows, height + 2, breadth + 2, 9, narrow)
            part = jnp.zeros((rows, height, breadth, narrow), jnp.float32)
            for b in range(3):
                for c in range(3):
                    part = (
                        part
                        + product[:, 2 - b : 2 - b + height, 2 - c : 2 - c + breadth, b * 3 + c, :]
                    )
            inside = tap_mask(rows, 1 - a)
            total = total + jnp.where(inside, part, jnp.zeros_like(part))
        return (weight_grad, total.reshape(voxels, narrow))

    def layer_sum(weight_grad):
        return lax.psum(weight_grad, "dp")

    plane_one, pre_one = forward(volume, filter_one)
    act_one = leaky(pre_one).astype(jnp.bfloat16).reshape(rows, height, breadth, narrow)
    plane_two, pre_two = forward(act_one, filter_two)
    output = leaky(pre_two).astype(jnp.bfloat16).reshape(rows, height, breadth, narrow)
    delta_two = (cotangent.reshape(voxels, narrow).astype(jnp.float32) * slope_of(pre_two)).astype(
        jnp.bfloat16
    )
    local_two, back_two = backward(
        plane_two, delta_two.reshape(rows, height, breadth, narrow), filter_two
    )
    summed_two = layer_sum(local_two)
    delta_one = (back_two * slope_of(pre_one)).astype(jnp.bfloat16)
    local_one, back_one = backward(
        plane_one, delta_one.reshape(rows, height, breadth, narrow), filter_one
    )
    summed_one = layer_sum(local_one)
    input_grad = back_one.astype(jnp.bfloat16).reshape(rows, height, breadth, narrow)
    return (output, input_grad, summed_one * scale, summed_two * scale)


def copy_weights(own_ref, same_ref, swap_ref, full_ref, sems):
    me = lax.axis_index("chan")
    core = lax.rem(lax.axis_index("dp"), 2)
    quarter = HALF // 2
    sources = [(own_ref, HALF, 0)]
    if same_ref is not None:
        sources.append((same_ref, quarter, HALF + core * quarter))
        sources.append((swap_ref, quarter, HALF + (1 - core) * quarter))
    copies = []
    for source, height, row in sources:
        for side in range(2):
            column = pl.multiple_of((me if side == 0 else 1 - me) * HALF, HALF)
            if not isinstance(row, int):
                row = pl.multiple_of(row, quarter)
            copies.append(
                pltpu.make_async_copy(
                    source.at[:, :, pl.ds(column, HALF)],
                    full_ref.at[:, pl.ds(row, height), pl.ds(side * HALF, HALF)],
                    sems.at[len(copies)],
                )
            )
    for copy in copies:
        copy.start()
    return copies


def is_seam():
    return lax.rem(lax.axis_index("dp") * 2, VOX) == 0


def fill_planes(planes, store):
    for slot in range(6):
        store[slot, 0] = jnp.zeros(store.shape[2:], store.dtype)
        store[slot, VOX + 1] = jnp.zeros(store.shape[2:], store.dtype)
    for slot, plane in ((0, 0), (1, 1), (4, 2), (5, 3)):
        for lane, ref, at in planes[plane]:
            store[slot, 1 : VOX + 1, :, lane : lane + ref.shape[3]] = ref[at]
    seam = is_seam()
    for slot, plane in ((2, 2), (3, 1)):

        @pl.when(seam)
        def _():
            store[slot] = jnp.zeros(store.shape[1:], store.dtype)

        @pl.when(jnp.logical_not(seam))
        def _():
            for lane, ref, at in planes[plane]:
                store[slot, 1 : VOX + 1, :, lane : lane + ref.shape[3]] = ref[at]


def conv_rows(store, weights, plane, row, flipped):
    pieces = []
    for a in range(3):
        for b in range(3):
            piece = store[3 * plane + a, pl.ds(row + b, TILE)]
            pieces.append(piece.reshape(TILE * VOX, FULL))
    stacked = jnp.concatenate(pieces, axis=1)
    products = []
    for c in range(3):
        if flipped:
            taps = [weights[(2 - a) * 9 + (2 - b) * 3 + 2 - c] for a in range(3) for b in range(3)]
            dims = (((1,), (1,)), ((), ()))
            taps = jnp.concatenate(taps, axis=1)
        else:
            taps = [weights[a * 9 + b * 3 + c] for a in range(3) for b in range(3)]
            dims = (((1,), (0,)), ((), ()))
            taps = jnp.concatenate(taps, axis=0)
        products.append(
            lax.dot_general(stacked, taps, dims, preferred_element_type=jnp.float32)
        )
    left, middle, right = products
    column = lax.rem(lax.broadcasted_iota(jnp.int32, left.shape, 0), VOX)
    left = jnp.where(column > 0, pltpu.roll(left, 1, 0), 0.0)
    right = jnp.where(column < VOX - 1, pltpu.roll(right, TILE * VOX - 1, 0), 0.0)
    return middle + left + right


def over_tiles(body):
    for plane in range(2):

        @pl.loop(0, VOX // TILE)
        def _(step):
            body(plane, pl.multiple_of(step * TILE, TILE))


def shaped(values):
    return values.reshape(TILE, VOX, values.shape[1])


def first_kernel(
    mid_own, mid_other, low_own, high_own, low_other, high_other, own, same, swap,
    act_0, act_1, weights, store, sems,
):
    copies = copy_weights(own, same, swap, weights, sems)
    fill_planes(
        [
            ((0, low_own, 0), (HALF, low_other, 0)),
            ((0, mid_own, 0), (HALF, mid_other, 0)),
            ((0, mid_own, 1), (HALF, mid_other, 1)),
            ((0, high_own, 0), (HALF, high_other, 0)),
        ],
        store,
    )
    for copy in copies:
        copy.wait()

    def body(plane, row):
        value = leaky(conv_rows(store, weights, plane, row, False))
        target = (act_0, act_1)[plane]
        target[0, pl.ds(row, TILE)] = shaped(value.astype(jnp.bfloat16))

    over_tiles(body)


def second_kernel(
    act_0, act_1, low, high, cot_own, cot_other, own, same, swap,
    output, delta_0, delta_1, weights, store, sems,
):
    copies = copy_weights(own, same, swap, weights, sems)
    fill_planes(
        [((0, low, 0),), ((0, act_0, 0),), ((0, act_1, 0),), ((0, high, 0),)], store
    )
    for copy in copies:
        copy.wait()

    def body(plane, row):
        value = conv_rows(store, weights, plane, row, False)
        output[plane, pl.ds(row, TILE)] = shaped(leaky(value[:, :HALF]).astype(jnp.bfloat16))
        slope = slope_of(value)
        target = (delta_0, delta_1)[plane]
        for lane, cot in ((0, cot_own), (HALF, cot_other)):
            grad = cot[plane, pl.ds(row, TILE)].astype(jnp.float32)
            delta = grad * shaped(slope[:, lane : lane + HALF])
            target[0, pl.ds(row, TILE), :, lane : lane + HALF] = delta.astype(jnp.bfloat16)

    over_tiles(body)


def back_kernel(
    delta_0, delta_1, low, high, act_0, act_1, own, same, swap,
    prior_0, prior_1, weights, store, sems,
):
    copies = copy_weights(own, same, swap, weights, sems)
    fill_planes(
        [((0, low, 0),), ((0, delta_0, 0),), ((0, delta_1, 0),), ((0, high, 0),)], store
    )
    for copy in copies:
        copy.wait()

    def body(plane, row):
        value = shaped(conv_rows(store, weights, plane, row, True))
        act = (act_0, act_1)[plane][0, pl.ds(row, TILE)].astype(jnp.float32)
        target = (prior_0, prior_1)[plane]
        target[0, pl.ds(row, TILE)] = (value * slope_of(act)).astype(jnp.bfloat16)

    over_tiles(body)


def last_kernel(delta_0, delta_1, low, high, own, grad, weights, store, sems):
    copies = copy_weights(own, None, None, weights, sems)
    fill_planes(
        [((0, low, 0),), ((0, delta_0, 0),), ((0, delta_1, 0),), ((0, high, 0),)], store
    )
    for copy in copies:
        copy.wait()

    def body(plane, row):
        value = conv_rows(store, weights, plane, row, True)
        grad[plane, pl.ds(row, TILE)] = shaped(value.astype(jnp.bfloat16))

    over_tiles(body)


def filter_kernel(low, mid_0, mid_1, high, delta_0, delta_1, grad, turned, moved):
    pixels = VOX * VOX
    seam = is_seam()
    sources = ((0, low), (1, mid_0), (2, mid_1), (3, high))
    for plane, ref in sources:
        flipped = ref[0].reshape(pixels, HALF).T
        for output_plane in range(2):
            tap = plane - output_plane
            if not 0 <= tap < 3:
                continue
            rows = slice(tap * HALF, (tap + 1) * HALF)
            columns = slice(output_plane * pixels, (output_plane + 1) * pixels)
            if plane in (1, 2) and tap != 1:
                turned[rows, columns] = jnp.where(seam, jnp.zeros_like(flipped), flipped)
            else:
                turned[rows, columns] = flipped
    for plane, ref in ((0, delta_0), (1, delta_1)):
        for c in range(3):
            moved[c, plane, 0] = jnp.zeros(moved.shape[3:], moved.dtype)
            moved[c, plane, VOX + 1] = jnp.zeros(moved.shape[3:], moved.dtype)
        moved[1, plane, 1 : VOX + 1] = ref[0]

        @pl.loop(0, VOX // TILE)
        def _(step):
            row = step * TILE
            values = ref[0, pl.ds(row, TILE)].reshape(TILE * VOX, FULL).astype(jnp.float32)
            column = lax.rem(lax.broadcasted_iota(jnp.int32, values.shape, 0), VOX)
            ahead = jnp.where(column < VOX - 1, pltpu.roll(values, TILE * VOX - 1, 0), 0.0)
            behind = jnp.where(column > 0, pltpu.roll(values, 1, 0), 0.0)
            moved[0, plane, pl.ds(row + 1, TILE)] = shaped(ahead.astype(jnp.bfloat16))
            moved[2, plane, pl.ds(row + 1, TILE)] = shaped(behind.astype(jnp.bfloat16))

    me = lax.axis_index("chan")
    for b in range(3):

        @pl.loop(0, 3)
        def _(c):
            right = moved[c, :, 2 - b : 2 - b + VOX].reshape(2 * pixels, FULL)
            product = jnp.dot(turned[...], right, preferred_element_type=jnp.float32)
            first = jnp.where(me == 0, product[:, :HALF], product[:, HALF:])
            second = jnp.where(me == 0, product[:, HALF:], product[:, :HALF])
            for a in range(3):
                rows = slice(a * HALF, (a + 1) * HALF)
                grad[a * 9 + b * 3 + c, :, :HALF] = first[rows].astype(grad.dtype)
                grad[a * 9 + b * 3 + c, :, HALF:] = second[rows].astype(grad.dtype)


def conv_call(kernel, outs, operands, weight_rows, name):
    flops = 2 * 2 * VOX * VOX * 27 * FULL * weight_rows
    count = sum(ref.size * 2 for ref in operands)
    narrow = weight_rows == HALF
    specs = [pl.BlockSpec(memory_space=pltpu.VMEM)] * (len(operands) - (1 if narrow else 3))
    specs += [pl.BlockSpec(memory_space=pl.ANY)] * (1 if narrow else 3)
    return pl.pallas_call(
        kernel,
        out_shape=[jax.ShapeDtypeStruct(shape, jnp.bfloat16) for shape in outs],
        in_specs=specs,
        out_specs=[pl.BlockSpec(memory_space=pltpu.VMEM)] * len(outs),
        scratch_shapes=[
            pltpu.VMEM((27, weight_rows, FULL), jnp.bfloat16),
            pltpu.VMEM((6, VOX + 2, VOX, FULL), jnp.bfloat16),
            pltpu.SemaphoreType.DMA((6,)),
        ],
        compiler_params=pltpu.CompilerParams(vmem_limit_bytes=VMEM_LIMIT),
        cost_estimate=pl.CostEstimate(flops=flops, bytes_accessed=count, transcendentals=0),
        name=name,
    )(*operands)


def filter_call(planes, mid_at, deltas, dtype, name):
    narrow = (1, VOX, VOX, HALF)
    specs = [
        pl.BlockSpec(narrow, functools.partial(lambda at, i: (at, 0, 0, 0), at)) for at in mid_at
    ]
    specs += [pl.BlockSpec((1, VOX, VOX, FULL), lambda i: (0, 0, 0, 0))] * 2
    return pl.pallas_call(
        filter_kernel,
        grid=(1,),
        out_shape=jax.ShapeDtypeStruct((27, HALF, FULL), dtype),
        in_specs=specs,
        out_specs=pl.BlockSpec((27, HALF, FULL), lambda i: (0, 0, 0)),
        scratch_shapes=[
            pltpu.VMEM((3 * HALF, 2 * VOX * VOX), jnp.bfloat16),
            pltpu.VMEM((3, 2, VOX + 2, VOX, FULL), jnp.bfloat16),
        ],
        compiler_params=pltpu.CompilerParams(vmem_limit_bytes=VMEM_LIMIT),
        cost_estimate=pl.CostEstimate(
            flops=2 * 2 * VOX * VOX * 27 * HALF * FULL, bytes_accessed=8 << 20, transcendentals=0
        ),
        name=name,
    )(*planes, *deltas)


def after(value, *earlier):
    return lax.optimization_barrier((value,) + earlier)[0]


def paired(volume, filter_one, filter_two, cotangent):
    count = lax.axis_size("dp")
    ahead = [(i, (i + 1) % count) for i in range(count)]
    behind = [(target, source) for source, target in ahead]
    cores = [(i, i ^ 1) for i in range(count)]
    across = [(0, 1), (1, 0)]
    core = lax.rem(lax.axis_index("dp"), 2)
    scale = 1.0 / math.sqrt(count * 2 * VOX * VOX)
    one = filter_one.reshape(27, HALF, FULL)
    two = filter_two.reshape(27, HALF, FULL)

    def other(values):
        return lax.ppermute(values, "chan", across)

    def rims(first, last):
        return lax.ppermute(last, "dp", ahead), lax.ppermute(first, "dp", behind)

    def my_part(weight):
        return lax.dynamic_slice_in_dim(weight, core * (HALF // 2), HALF // 2, axis=1)

    volume_other = other(volume)
    low_own, high_own = rims(volume[:1], volume[1:])
    one_same = other(my_part(one))
    low_other, high_other = rims(volume_other[:1], volume_other[1:])
    one_swap = lax.ppermute(one_same, "dp", cores)
    two_same = other(after(my_part(two), one_same))
    cot_other = other(after(cotangent, one_same))
    two_swap = lax.ppermute(two_same, "dp", cores)

    wide = (1, VOX, VOX, FULL)
    narrow = (2, VOX, VOX, HALF)
    act_0, act_1 = conv_call(
        first_kernel,
        [wide, wide],
        [volume, volume_other, low_own, high_own, low_other, high_other, one, one_same, one_swap],
        FULL,
        "first_layer",
    )
    low_act, high_act = rims(act_0, act_1)
    output, delta_0, delta_1 = conv_call(
        second_kernel,
        [narrow, wide, wide],
        [act_0, act_1, low_act, high_act, cotangent, cot_other, two, two_same, two_swap],
        FULL,
        "second_layer",
    )
    low_delta, high_delta = rims(delta_0, delta_1)
    local_two = filter_call(
        [low_act, act_0, act_1, high_act], (0, 0, 0, 0), [delta_0, delta_1], jnp.float32, "grad_two"
    )
    summed_two = lax.psum(local_two, "dp")
    prior_0, prior_1 = conv_call(
        back_kernel,
        [wide, wide],
        [delta_0, delta_1, low_delta, high_delta, act_0, act_1, two, two_same, two_swap],
        FULL,
        "second_back",
    )
    low_prior, high_prior = rims(prior_0, prior_1)
    local_one = filter_call(
        [low_own, volume, volume, high_own], (0, 0, 1, 0), [prior_0, prior_1], jnp.float32, "grad_one"
    )
    local_one, summed_two = lax.optimization_barrier((local_one, summed_two))
    summed_one = lax.psum(local_one, "dp")
    (input_grad,) = conv_call(
        last_kernel, [narrow], [prior_0, prior_1, low_prior, high_prior, one], HALF, "first_back"
    )
    shape = filter_one.shape
    return (
        output,
        input_grad,
        (summed_one * scale).reshape(shape),
        (summed_two * scale).reshape(shape),
    )


def local(volume, filter_one, filter_two, cotangent):
    pair = lax.axis_size("chan") == 2 and lax.axis_size("dp") % 2 == 0
    if pair and volume.shape == (2, VOX, VOX, HALF):
        return paired(volume, filter_one, filter_two, cotangent)
    return plain(volume, filter_one, filter_two, cotangent)


def solution(mesh):
    in_specs = (
        P("dp", None, None, "chan"),
        P(None, None, None, "chan", None),
        P(None, None, None, "chan", None),
        P("dp", None, None, "chan"),
    )
    out_specs = (
        P("dp", None, None, "chan"),
        P("dp", None, None, "chan"),
        P(None, None, None, "chan", None),
        P(None, None, None, "chan", None),
    )
    return jax.shard_map(local, mesh=mesh, in_specs=in_specs, out_specs=out_specs, check_vma=False)
```

```python
import functools
import math

import jax
import jax.numpy as jnp
from jax import lax
from jax.experimental import pallas as pl
from jax.experimental.pallas import tpu as pltpu
from jax.sharding import PartitionSpec as P

VOX = 32
SLOPE = 0.3
HALF = 128
FULL = 256
TILE = 16
VMEM_LIMIT = 40 * 1024 * 1024


def extended(block, sides, width):
    for axis, dim in sides:
        count = lax.axis_size(axis)
        forward = [(i, i + 1) for i in range(count - 1)]
        forward.append((count - 1, 0))
        backward = [(target, source) for source, target in forward]
        low = lax.ppermute(
            lax.slice_in_dim(block, block.shape[dim] - width, None, axis=dim), axis, forward
        )
        high = lax.ppermute(lax.slice_in_dim(block, 0, width, axis=dim), axis, backward)
        block = jnp.concatenate([low, block, high], axis=dim)
    return block


def leaky(values):
    return jnp.where(values > 0, values, SLOPE * values)


def slope_of(values):
    return jnp.where(values > 0, jnp.float32(1.0), jnp.float32(SLOPE))


def tap_mask(rows, offset):
    base = lax.axis_index("dp") * rows
    total_rows = lax.axis_size("dp") * rows
    planes = jnp.mod(base + jnp.arange(rows, dtype=jnp.int32) - 1, total_rows)
    depth = jnp.mod(planes, VOX) + offset
    inside = jnp.logical_and(depth >= 0, depth < VOX)
    return inside[:, None, None, None]


def pad_plane(values):
    return jnp.pad(values, ((0, 0), (1, 1), (1, 1), (0, 0)))


def columns(plane, rows, height, breadth):
    taps = []
    for a in range(3):
        inside = tap_mask(rows, a - 1)
        depth_slab = plane[a : a + rows]
        depth_slab = jnp.where(inside, depth_slab, jnp.zeros_like(depth_slab))
        for b in range(3):
            for c in range(3):
                taps.append(depth_slab[:, b : b + height, c : c + breadth, :])
    stacked = jnp.concatenate(taps, axis=-1)
    return stacked.reshape(rows * height * breadth, stacked.shape[-1])


def plain(volume, filter_one, filter_two, cotangent):
    rows, height, breadth, narrow = volume.shape
    full = filter_one.shape[4]
    voxels = rows * height * breadth
    scale = 1.0 / math.sqrt(lax.axis_size("dp") * voxels)

    def forward(activity, weight):
        rim = extended(activity, (("dp", 0),), 1)
        plane = pad_plane(rim)
        stacked = columns(plane, rows, height, breadth)
        partial_value = jnp.dot(
            stacked, weight.reshape(27 * narrow, full), preferred_element_type=jnp.float32
        )
        summed = lax.psum_scatter(partial_value, "chan", scatter_dimension=1, tiled=True)
        return (plane, summed)

    def backward(plane, delta, weight):
        wide = lax.all_gather(delta, "chan", axis=3, tiled=True)
        rim = extended(wide, (("dp", 0),), 1)
        centre = rim[1 : rows + 1].reshape(voxels, full)
        stacked = columns(plane, rows, height, breadth)
        weight_grad = lax.dot_general(
            stacked, centre, (((0,), (0,)), ((), ())), preferred_element_type=jnp.float32
        )
        weight_grad = weight_grad.reshape(3, 3, 3, narrow, full)
        source = pad_plane(rim)
        total = jnp.zeros((rows, height, breadth, narrow), jnp.float32)
        for a in range(3):
            depth_slab = source[2 - a : 2 - a + rows]
            flat = depth_slab.reshape(-1, full)
            product = lax.dot_general(
                flat,
                weight[a].reshape(9 * narrow, full),
                (((1,), (1,)), ((), ())),
                preferred_element_type=jnp.float32,
            )
            product = product.reshape(rows, height + 2, breadth + 2, 9, narrow)
            part = jnp.zeros((rows, height, breadth, narrow), jnp.float32)
            for b in range(3):
                for c in range(3):
                    part = (
                        part
                        + product[:, 2 - b : 2 - b + height, 2 - c : 2 - c + breadth, b * 3 + c, :]
                    )
            inside = tap_mask(rows, 1 - a)
            total = total + jnp.where(inside, part, jnp.zeros_like(part))
        return (weight_grad, total.reshape(voxels, narrow))

    def layer_sum(weight_grad):
        return lax.psum(weight_grad, "dp")

    plane_one, pre_one = forward(volume, filter_one)
    act_one = leaky(pre_one).astype(jnp.bfloat16).reshape(rows, height, breadth, narrow)
    plane_two, pre_two = forward(act_one, filter_two)
    output = leaky(pre_two).astype(jnp.bfloat16).reshape(rows, height, breadth, narrow)
    delta_two = (cotangent.reshape(voxels, narrow).astype(jnp.float32) * slope_of(pre_two)).astype(
        jnp.bfloat16
    )
    local_two, back_two = backward(
        plane_two, delta_two.reshape(rows, height, breadth, narrow), filter_two
    )
    summed_two = layer_sum(local_two)
    delta_one = (back_two * slope_of(pre_one)).astype(jnp.bfloat16)
    local_one, back_one = backward(
        plane_one, delta_one.reshape(rows, height, breadth, narrow), filter_one
    )
    summed_one = layer_sum(local_one)
    input_grad = back_one.astype(jnp.bfloat16).reshape(rows, height, breadth, narrow)
    return (output, input_grad, summed_one * scale, summed_two * scale)


def copy_weights(own_ref, same_ref, swap_ref, full_ref, sems):
    me = lax.axis_index("chan")
    core = lax.rem(lax.axis_index("dp"), 2)
    quarter = HALF // 2
    sources = [(own_ref, HALF, 0)]
    if same_ref is not None:
        sources.append((same_ref, quarter, HALF + core * quarter))
        sources.append((swap_ref, quarter, HALF + (1 - core) * quarter))
    copies = []
    for source, height, row in sources:
        for side in range(2):
            column = pl.multiple_of((me if side == 0 else 1 - me) * HALF, HALF)
            if not isinstance(row, int):
                row = pl.multiple_of(row, quarter)
            copies.append(
                pltpu.make_async_copy(
                    source.at[:, :, pl.ds(column, HALF)],
                    full_ref.at[:, pl.ds(row, height), pl.ds(side * HALF, HALF)],
                    sems.at[len(copies)],
                )
            )
    for copy in copies:
        copy.start()
    return copies


def is_seam():
    return lax.rem(lax.axis_index("dp") * 2, VOX) == 0


def fill_planes(planes, store):
    for slot in range(6):
        store[slot, 0] = jnp.zeros(store.shape[2:], store.dtype)
        store[slot, VOX + 1] = jnp.zeros(store.shape[2:], store.dtype)
    for slot, plane in ((0, 0), (1, 1), (4, 2), (5, 3)):
        for lane, ref, at in planes[plane]:
            store[slot, 1 : VOX + 1, :, lane : lane + ref.shape[3]] = ref[at]
    seam = is_seam()
    for slot, plane in ((2, 2), (3, 1)):

        @pl.when(seam)
        def _():
            store[slot] = jnp.zeros(store.shape[1:], store.dtype)

        @pl.when(jnp.logical_not(seam))
        def _():
            for lane, ref, at in planes[plane]:
                store[slot, 1 : VOX + 1, :, lane : lane + ref.shape[3]] = ref[at]


def conv_rows(store, weights, plane, row, flipped):
    pieces = []
    for a in range(3):
        for b in range(3):
            piece = store[3 * plane + a, pl.ds(row + b, TILE)]
            pieces.append(piece.reshape(TILE * VOX, FULL))
    stacked = jnp.concatenate(pieces, axis=1)
    products = []
    for c in range(3):
        if flipped:
            taps = [weights[(2 - a) * 9 + (2 - b) * 3 + 2 - c] for a in range(3) for b in range(3)]
            dims = (((1,), (1,)), ((), ()))
            taps = jnp.concatenate(taps, axis=1)
        else:
            taps = [weights[a * 9 + b * 3 + c] for a in range(3) for b in range(3)]
            dims = (((1,), (0,)), ((), ()))
            taps = jnp.concatenate(taps, axis=0)
        products.append(
            lax.dot_general(stacked, taps, dims, preferred_element_type=jnp.float32)
        )
    left, middle, right = products
    column = lax.rem(lax.broadcasted_iota(jnp.int32, left.shape, 0), VOX)
    left = jnp.where(column > 0, pltpu.roll(left, 1, 0), 0.0)
    right = jnp.where(column < VOX - 1, pltpu.roll(right, TILE * VOX - 1, 0), 0.0)
    return middle + left + right


def over_tiles(body):
    for plane in range(2):

        @pl.loop(0, VOX // TILE)
        def _(step):
            body(plane, pl.multiple_of(step * TILE, TILE))


def shaped(values):
    return values.reshape(TILE, VOX, values.shape[1])


def first_kernel(
    mid_own, mid_other, low_own, high_own, low_other, high_other, own, same, swap,
    act_0, act_1, weights, store, sems,
):
    copies = copy_weights(own, same, swap, weights, sems)
    fill_planes(
        [
            ((0, low_own, 0), (HALF, low_other, 0)),
            ((0, mid_own, 0), (HALF, mid_other, 0)),
            ((0, mid_own, 1), (HALF, mid_other, 1)),
            ((0, high_own, 0), (HALF, high_other, 0)),
        ],
        store,
    )
    for copy in copies:
        copy.wait()

    def body(plane, row):
        value = leaky(conv_rows(store, weights, plane, row, False))
        target = (act_0, act_1)[plane]
        target[0, pl.ds(row, TILE)] = shaped(value.astype(jnp.bfloat16))

    over_tiles(body)


def second_kernel(
    act_0, act_1, low, high, cot_own, cot_other, own, same, swap,
    output, delta_0, delta_1, weights, store, sems,
):
    copies = copy_weights(own, same, swap, weights, sems)
    fill_planes(
        [((0, low, 0),), ((0, act_0, 0),), ((0, act_1, 0),), ((0, high, 0),)], store
    )
    for copy in copies:
        copy.wait()

    def body(plane, row):
        value = conv_rows(store, weights, plane, row, False)
        output[plane, pl.ds(row, TILE)] = shaped(leaky(value[:, :HALF]).astype(jnp.bfloat16))
        slope = slope_of(value)
        target = (delta_0, delta_1)[plane]
        for lane, cot in ((0, cot_own), (HALF, cot_other)):
            grad = cot[plane, pl.ds(row, TILE)].astype(jnp.float32)
            delta = grad * shaped(slope[:, lane : lane + HALF])
            target[0, pl.ds(row, TILE), :, lane : lane + HALF] = delta.astype(jnp.bfloat16)

    over_tiles(body)


def back_kernel(
    delta_0, delta_1, low, high, act_0, act_1, own, same, swap,
    prior_0, prior_1, weights, store, sems,
):
    copies = copy_weights(own, same, swap, weights, sems)
    fill_planes(
        [((0, low, 0),), ((0, delta_0, 0),), ((0, delta_1, 0),), ((0, high, 0),)], store
    )
    for copy in copies:
        copy.wait()

    def body(plane, row):
        value = shaped(conv_rows(store, weights, plane, row, True))
        act = (act_0, act_1)[plane][0, pl.ds(row, TILE)].astype(jnp.float32)
        target = (prior_0, prior_1)[plane]
        target[0, pl.ds(row, TILE)] = (value * slope_of(act)).astype(jnp.bfloat16)

    over_tiles(body)


def last_kernel(delta_0, delta_1, low, high, own, grad, weights, store, sems):
    copies = copy_weights(own, None, None, weights, sems)
    fill_planes(
        [((0, low, 0),), ((0, delta_0, 0),), ((0, delta_1, 0),), ((0, high, 0),)], store
    )
    for copy in copies:
        copy.wait()

    def body(plane, row):
        value = conv_rows(store, weights, plane, row, True)
        grad[plane, pl.ds(row, TILE)] = shaped(value.astype(jnp.bfloat16))

    over_tiles(body)


def filter_kernel(low, mid_0, mid_1, high, delta_0, delta_1, keep, send, turned, moved):
    pixels = VOX * VOX
    seam = is_seam()
    sources = ((0, low), (1, mid_0), (2, mid_1), (3, high))
    for plane, ref in sources:
        flipped = ref[0].reshape(pixels, HALF).T
        for output_plane in range(2):
            tap = plane - output_plane
            if not 0 <= tap < 3:
                continue
            rows = slice(tap * HALF, (tap + 1) * HALF)
            columns = slice(output_plane * pixels, (output_plane + 1) * pixels)
            if plane in (1, 2) and tap != 1:
                turned[rows, columns] = jnp.where(seam, jnp.zeros_like(flipped), flipped)
            else:
                turned[rows, columns] = flipped
    for plane, ref in ((0, delta_0), (1, delta_1)):
        for c in range(3):
            moved[c, plane, 0] = jnp.zeros(moved.shape[3:], moved.dtype)
            moved[c, plane, VOX + 1] = jnp.zeros(moved.shape[3:], moved.dtype)
        moved[1, plane, 1 : VOX + 1] = ref[0]

        @pl.loop(0, VOX // TILE)
        def _(step):
            row = step * TILE
            values = ref[0, pl.ds(row, TILE)].reshape(TILE * VOX, FULL).astype(jnp.float32)
            column = lax.rem(lax.broadcasted_iota(jnp.int32, values.shape, 0), VOX)
            ahead = jnp.where(column < VOX - 1, pltpu.roll(values, TILE * VOX - 1, 0), 0.0)
            behind = jnp.where(column > 0, pltpu.roll(values, 1, 0), 0.0)
            moved[0, plane, pl.ds(row + 1, TILE)] = shaped(ahead.astype(jnp.bfloat16))
            moved[2, plane, pl.ds(row + 1, TILE)] = shaped(behind.astype(jnp.bfloat16))

    mine = lax.axis_index("chan") == lax.rem(lax.axis_index("dp"), 2)
    for b in range(3):

        @pl.loop(0, 3)
        def _(c):
            right = moved[c, :, 2 - b : 2 - b + VOX].reshape(2 * pixels, FULL)
            product = jnp.dot(turned[...], right, preferred_element_type=jnp.float32)
            kept = jnp.where(mine, product[:, :HALF], product[:, HALF:])
            sent = jnp.where(mine, product[:, HALF:], product[:, :HALF])
            for a in range(3):
                rows = slice(a * HALF, (a + 1) * HALF)
                tap = a * 9 + b * 3 + c
                keep[:, tap] = kept[rows].reshape(8, 16, HALF)
                send[:, tap] = sent[rows].reshape(8, 16, HALF).astype(send.dtype)


def place():
    at = lax.axis_index("dp")
    return at // 4, lax.rem(at // 2, 2), lax.rem(at, 2)


def add_core_kernel(keep, came, kept, sent):
    _, side, _ = place()
    for target, first in ((kept, side * 4), (sent, (1 - side) * 4)):

        @pl.loop(0, 4)
        def _(block):
            total = keep[first + block] + came[first + block].astype(jnp.float32)
            target[block] = total.astype(target.dtype)


def add_side_kernel(keep, came, kept, *sent):
    level, _, _ = place()
    for step, target in enumerate((kept,) + sent):
        block = lax.rem(level + step, 4)
        total = keep[block] + came[block].astype(jnp.float32)
        target[...] = total.astype(target.dtype)


def add_level_kernel(scale, keep, *rest):
    total = keep[...]
    for came in rest[:-1]:
        total = total + came[...].astype(jnp.float32)
    rest[-1][...] = (total * scale).astype(rest[-1].dtype)


def join_level_kernel(own, *rest):
    level, _, _ = place()
    target = rest[-1]
    target[level] = own[...]
    for step, came in enumerate(rest[:-1], 1):
        target[lax.rem(level + 4 - step, 4)] = came[...]


def join_side_kernel(own, came, target):
    _, side, _ = place()
    target[pl.ds(side * 4, 4)] = own[...]
    target[pl.ds((1 - side) * 4, 4)] = came[...]


def join_core_kernel(own, came, grad):
    _, _, core = place()

    @pl.loop(0, 8)
    def _(block):
        row = pl.multiple_of(block * 16, 16)
        first = jnp.where(core == 0, own[block], came[block])
        second = jnp.where(core == 0, came[block], own[block])
        grad[:, pl.ds(row, 16), :HALF] = first.astype(jnp.float32)
        grad[:, pl.ds(row, 16), HALF:] = second.astype(jnp.float32)


def small_call(kernel, outs, operands, name):
    moved = sum(ref.size * ref.dtype.itemsize for ref in operands)
    moved += sum(math.prod(shape) * jnp.dtype(dtype).itemsize for shape, dtype in outs)
    return pl.pallas_call(
        kernel,
        out_shape=[jax.ShapeDtypeStruct(shape, dtype) for shape, dtype in outs],
        in_specs=[pl.BlockSpec(memory_space=pltpu.VMEM)] * len(operands),
        out_specs=[pl.BlockSpec(memory_space=pltpu.VMEM)] * len(outs),
        compiler_params=pltpu.CompilerParams(vmem_limit_bytes=VMEM_LIMIT),
        cost_estimate=pl.CostEstimate(flops=0, bytes_accessed=moved, transcendentals=0),
        name=name,
    )(*operands)


def layer_sum(keep, send, scale, name):
    count = lax.axis_size("dp")
    wide, thin = jnp.float32, jnp.bfloat16
    cores = [(i, i ^ 1) for i in range(count)]
    sides = [(i, i ^ 2) for i in range(count)]
    levels = [[(i, (i + 4 * step) % count) for i in range(count)] for step in (1, 2, 3)]
    part = (27, 16, HALF)

    came = lax.ppermute(send, "dp", cores)
    keep, send = small_call(
        add_core_kernel, [((4,) + part, wide), ((4,) + part, thin)], [keep, came], name + "_core"
    )
    came = lax.ppermute(send, "dp", sides)
    keep, *sends = small_call(
        add_side_kernel, [(part, wide)] + [(part, thin)] * 3, [keep, came], name + "_side"
    )
    came = [lax.ppermute(block, "dp", pairs) for block, pairs in zip(sends, levels)]
    (own,) = small_call(
        functools.partial(add_level_kernel, scale), [(part, thin)], [keep, *came], name + "_level"
    )
    came = [lax.ppermute(own, "dp", pairs) for pairs in levels]
    (own,) = small_call(join_level_kernel, [((4,) + part, thin)], [own, *came], name + "_levels")
    came = lax.ppermute(own, "dp", sides)
    (own,) = small_call(join_side_kernel, [((8,) + part, thin)], [own, came], name + "_sides")
    came = lax.ppermute(own, "dp", cores)
    (grad,) = small_call(join_core_kernel, [((27, HALF, FULL), wide)], [own, came], name + "_cores")
    return grad


def conv_call(kernel, outs, operands, weight_rows, name):
    flops = 2 * 2 * VOX * VOX * 27 * FULL * weight_rows
    count = sum(ref.size * 2 for ref in operands)
    narrow = weight_rows == HALF
    specs = [pl.BlockSpec(memory_space=pltpu.VMEM)] * (len(operands) - (1 if narrow else 3))
    specs += [pl.BlockSpec(memory_space=pl.ANY)] * (1 if narrow else 3)
    return pl.pallas_call(
        kernel,
        out_shape=[jax.ShapeDtypeStruct(shape, jnp.bfloat16) for shape in outs],
        in_specs=specs,
        out_specs=[pl.BlockSpec(memory_space=pltpu.VMEM)] * len(outs),
        scratch_shapes=[
            pltpu.VMEM((27, weight_rows, FULL), jnp.bfloat16),
            pltpu.VMEM((6, VOX + 2, VOX, FULL), jnp.bfloat16),
            pltpu.SemaphoreType.DMA((6,)),
        ],
        compiler_params=pltpu.CompilerParams(vmem_limit_bytes=VMEM_LIMIT),
        cost_estimate=pl.CostEstimate(flops=flops, bytes_accessed=count, transcendentals=0),
        name=name,
    )(*operands)


def filter_call(planes, mid_at, deltas, name):
    narrow = (1, VOX, VOX, HALF)
    specs = [
        pl.BlockSpec(narrow, functools.partial(lambda at, i: (at, 0, 0, 0), at)) for at in mid_at
    ]
    specs += [pl.BlockSpec((1, VOX, VOX, FULL), lambda i: (0, 0, 0, 0))] * 2
    return pl.pallas_call(
        filter_kernel,
        grid=(1,),
        out_shape=[
            jax.ShapeDtypeStruct((8, 27, 16, HALF), jnp.float32),
            jax.ShapeDtypeStruct((8, 27, 16, HALF), jnp.bfloat16),
        ],
        in_specs=specs,
        out_specs=[pl.BlockSpec((8, 27, 16, HALF), lambda i: (0, 0, 0, 0))] * 2,
        scratch_shapes=[
            pltpu.VMEM((3 * HALF, 2 * VOX * VOX), jnp.bfloat16),
            pltpu.VMEM((3, 2, VOX + 2, VOX, FULL), jnp.bfloat16),
        ],
        compiler_params=pltpu.CompilerParams(vmem_limit_bytes=VMEM_LIMIT),
        cost_estimate=pl.CostEstimate(
            flops=2 * 2 * VOX * VOX * 27 * HALF * FULL, bytes_accessed=8 << 20, transcendentals=0
        ),
        name=name,
    )(*planes, *deltas)


def after(value, *earlier):
    return lax.optimization_barrier((value,) + earlier)[0]


def paired(volume, filter_one, filter_two, cotangent):
    count = lax.axis_size("dp")
    ahead = [(i, (i + 1) % count) for i in range(count)]
    behind = [(target, source) for source, target in ahead]
    cores = [(i, i ^ 1) for i in range(count)]
    across = [(0, 1), (1, 0)]
    core = lax.rem(lax.axis_index("dp"), 2)
    scale = 1.0 / math.sqrt(count * 2 * VOX * VOX)
    one = filter_one.reshape(27, HALF, FULL)
    two = filter_two.reshape(27, HALF, FULL)

    def other(values):
        return lax.ppermute(values, "chan", across)

    def rims(first, last):
        return lax.ppermute(last, "dp", ahead), lax.ppermute(first, "dp", behind)

    def my_part(weight):
        return lax.dynamic_slice_in_dim(weight, core * (HALF // 2), HALF // 2, axis=1)

    volume_other = other(volume)
    low_own, high_own = rims(volume[:1], volume[1:])
    one_same = other(my_part(one))
    low_other, high_other = rims(volume_other[:1], volume_other[1:])
    one_swap = lax.ppermute(one_same, "dp", cores)
    two_same = other(after(my_part(two), one_same))
    cot_other = other(after(cotangent, one_same))
    wide = (1, VOX, VOX, FULL)
    narrow = (2, VOX, VOX, HALF)
    act_0, act_1 = conv_call(
        first_kernel,
        [wide, wide],
        [volume, volume_other, low_own, high_own, low_other, high_other, one, one_same, one_swap],
        FULL,
        "first_layer",
    )
    low_act, high_act = rims(act_0, act_1)
    two_swap = lax.ppermute(after(two_same, act_0), "dp", cores)
    output, delta_0, delta_1 = conv_call(
        second_kernel,
        [narrow, wide, wide],
        [act_0, act_1, low_act, high_act, cotangent, cot_other, two, two_same, two_swap],
        FULL,
        "second_layer",
    )
    low_delta, high_delta = rims(delta_0, delta_1)
    local_two = filter_call(
        [low_act, act_0, act_1, high_act], (0, 0, 0, 0), [delta_0, delta_1], "grad_two"
    )
    summed_two = layer_sum(*local_two, scale, "sum_two")
    prior_0, prior_1 = conv_call(
        back_kernel,
        [wide, wide],
        [delta_0, delta_1, low_delta, high_delta, act_0, act_1, two, two_same, two_swap],
        FULL,
        "second_back",
    )
    low_prior, high_prior = rims(prior_0, prior_1)
    local_one = filter_call(
        [low_own, volume, volume, high_own], (0, 0, 1, 0), [prior_0, prior_1], "grad_one"
    )
    summed_one = layer_sum(*local_one, scale, "sum_one")
    (input_grad,) = conv_call(
        last_kernel, [narrow], [prior_0, prior_1, low_prior, high_prior, one], HALF, "first_back"
    )
    shape = filter_one.shape
    return (
        output,
        input_grad,
        summed_one.reshape(shape),
        summed_two.reshape(shape),
    )


def local(volume, filter_one, filter_two, cotangent):
    pair = lax.axis_size("chan") == 2 and lax.axis_size("dp") == 16
    if pair and volume.shape == (2, VOX, VOX, HALF):
        return paired(volume, filter_one, filter_two, cotangent)
    return plain(volume, filter_one, filter_two, cotangent)


def solution(mesh):
    in_specs = (
        P("dp", None, None, "chan"),
        P(None, None, None, "chan", None),
        P(None, None, None, "chan", None),
        P("dp", None, None, "chan"),
    )
    out_specs = (
        P("dp", None, None, "chan"),
        P("dp", None, None, "chan"),
        P(None, None, None, "chan", None),
        P(None, None, None, "chan", None),
    )
    return jax.shard_map(local, mesh=mesh, in_specs=in_specs, out_specs=out_specs, check_vma=False)
```

```python
import functools
import math

import jax
import jax.numpy as jnp
from jax import lax
from jax.experimental import pallas as pl
from jax.experimental.pallas import tpu as pltpu
from jax.sharding import PartitionSpec as P

VOX = 32
SLOPE = 0.3
HALF = 128
FULL = 256
TILE = 16
VMEM_LIMIT = 32 * 1024 * 1024


def extended(block, sides, width):
    for axis, dim in sides:
        count = lax.axis_size(axis)
        forward = [(i, i + 1) for i in range(count - 1)]
        forward.append((count - 1, 0))
        backward = [(target, source) for source, target in forward]
        low = lax.ppermute(
            lax.slice_in_dim(block, block.shape[dim] - width, None, axis=dim), axis, forward
        )
        high = lax.ppermute(lax.slice_in_dim(block, 0, width, axis=dim), axis, backward)
        block = jnp.concatenate([low, block, high], axis=dim)
    return block


def leaky(values):
    return jnp.where(values > 0, values, SLOPE * values)


def slope_of(values):
    return jnp.where(values > 0, jnp.float32(1.0), jnp.float32(SLOPE))


def tap_mask(rows, offset):
    base = lax.axis_index("dp") * rows
    total_rows = lax.axis_size("dp") * rows
    planes = jnp.mod(base + jnp.arange(rows, dtype=jnp.int32) - 1, total_rows)
    depth = jnp.mod(planes, VOX) + offset
    inside = jnp.logical_and(depth >= 0, depth < VOX)
    return inside[:, None, None, None]


def pad_plane(values):
    return jnp.pad(values, ((0, 0), (1, 1), (1, 1), (0, 0)))


def columns(plane, rows, height, breadth):
    taps = []
    for a in range(3):
        inside = tap_mask(rows, a - 1)
        depth_slab = plane[a : a + rows]
        depth_slab = jnp.where(inside, depth_slab, jnp.zeros_like(depth_slab))
        for b in range(3):
            for c in range(3):
                taps.append(depth_slab[:, b : b + height, c : c + breadth, :])
    stacked = jnp.concatenate(taps, axis=-1)
    return stacked.reshape(rows * height * breadth, stacked.shape[-1])


def plain(volume, filter_one, filter_two, cotangent):
    rows, height, breadth, narrow = volume.shape
    full = filter_one.shape[4]
    voxels = rows * height * breadth
    scale = 1.0 / math.sqrt(lax.axis_size("dp") * voxels)

    def forward(activity, weight):
        rim = extended(activity, (("dp", 0),), 1)
        plane = pad_plane(rim)
        stacked = columns(plane, rows, height, breadth)
        partial_value = jnp.dot(
            stacked, weight.reshape(27 * narrow, full), preferred_element_type=jnp.float32
        )
        summed = lax.psum_scatter(partial_value, "chan", scatter_dimension=1, tiled=True)
        return (plane, summed)

    def backward(plane, delta, weight):
        wide = lax.all_gather(delta, "chan", axis=3, tiled=True)
        rim = extended(wide, (("dp", 0),), 1)
        centre = rim[1 : rows + 1].reshape(voxels, full)
        stacked = columns(plane, rows, height, breadth)
        weight_grad = lax.dot_general(
            stacked, centre, (((0,), (0,)), ((), ())), preferred_element_type=jnp.float32
        )
        weight_grad = weight_grad.reshape(3, 3, 3, narrow, full)
        source = pad_plane(rim)
        total = jnp.zeros((rows, height, breadth, narrow), jnp.float32)
        for a in range(3):
            depth_slab = source[2 - a : 2 - a + rows]
            flat = depth_slab.reshape(-1, full)
            product = lax.dot_general(
                flat,
                weight[a].reshape(9 * narrow, full),
                (((1,), (1,)), ((), ())),
                preferred_element_type=jnp.float32,
            )
            product = product.reshape(rows, height + 2, breadth + 2, 9, narrow)
            part = jnp.zeros((rows, height, breadth, narrow), jnp.float32)
            for b in range(3):
                for c in range(3):
                    part = (
                        part
                        + product[:, 2 - b : 2 - b + height, 2 - c : 2 - c + breadth, b * 3 + c, :]
                    )
            inside = tap_mask(rows, 1 - a)
            total = total + jnp.where(inside, part, jnp.zeros_like(part))
        return (weight_grad, total.reshape(voxels, narrow))

    def layer_sum(weight_grad):
        return lax.psum(weight_grad, "dp")

    plane_one, pre_one = forward(volume, filter_one)
    act_one = leaky(pre_one).astype(jnp.bfloat16).reshape(rows, height, breadth, narrow)
    plane_two, pre_two = forward(act_one, filter_two)
    output = leaky(pre_two).astype(jnp.bfloat16).reshape(rows, height, breadth, narrow)
    delta_two = (cotangent.reshape(voxels, narrow).astype(jnp.float32) * slope_of(pre_two)).astype(
        jnp.bfloat16
    )
    local_two, back_two = backward(
        plane_two, delta_two.reshape(rows, height, breadth, narrow), filter_two
    )
    summed_two = layer_sum(local_two)
    delta_one = (back_two * slope_of(pre_one)).astype(jnp.bfloat16)
    local_one, back_one = backward(
        plane_one, delta_one.reshape(rows, height, breadth, narrow), filter_one
    )
    summed_one = layer_sum(local_one)
    input_grad = back_one.astype(jnp.bfloat16).reshape(rows, height, breadth, narrow)
    return (output, input_grad, summed_one * scale, summed_two * scale)


def is_seam():
    return lax.rem(lax.axis_index("dp") * 2, VOX) == 0


def place():
    at = lax.axis_index("dp")
    return at // 4, lax.rem(at // 2, 2), lax.rem(at, 2)


def shaped(values):
    return values.reshape(TILE, VOX, values.shape[1])


PARTS = {
    "all": dict(
        slots=((0, True), (1, True), (2, False), (1, False), (2, True), (3, True)),
        taps=(((0, 0), (1, 1), (2, 2)), ((0, 3), (1, 4), (2, 5))),
        depths=(0, 1, 2),
    ),
    "local": dict(
        slots=((0, True), (1, True), (0, False), (1, False)),
        taps=(((1, 0), (2, 3)), ((0, 2), (1, 1))),
        depths=(0, 1, 2),
    ),
    "rim": dict(
        slots=((0, True), (1, True)),
        taps=(((0, 0),), ((2, 1),)),
        depths=(0, 2),
    ),
}


def filter_rows(kind):
    _, side, core = place()
    if kind == "own":
        return [(HALF, 0)]
    if kind == "quarters":
        return [
            (32, (2 * along + unit) * 32)
            for unit in (core, 1 - core)
            for along in (side, 1 - side)
        ]
    return [(HALF, 0), (64, HALF + core * 64), (64, HALF + (1 - core) * 64)]


def copy_weights(kind, part, pieces, store, sems):
    me = lax.axis_index("chan")
    copies = []
    for (height, row), piece in zip(filter_rows(kind), pieces):
        if not isinstance(row, int):
            row = pl.multiple_of(row, 32)
        spans = ((0, 27),) if part != "rim" else ((0, 9), (18, 9))
        for side in range(2):
            column = pl.multiple_of((me if side == 0 else 1 - me) * HALF, HALF)
            for first, length in spans:
                taps = pl.ds(first, length)
                copies.append(
                    pltpu.make_async_copy(
                        piece.at[taps, :, pl.ds(column, HALF)],
                        store.at[taps, pl.ds(row, height), pl.ds(side * HALF, HALF)],
                        sems.at[len(copies)],
                    )
                )
    for copy in copies:
        copy.start()
    return copies


def fill_planes(part, planes, store):
    edge = jnp.zeros(store.shape[2:], store.dtype)
    seam = is_seam()
    for slot, (plane, always) in enumerate(PARTS[part]["slots"]):
        ref, at = planes[plane]
        store[slot, 0] = edge
        store[slot, VOX + 1] = edge
        if always:
            store[slot, 1 : VOX + 1] = ref[at]
            continue

        @pl.when(seam)
        def _():
            store[slot] = jnp.zeros(store.shape[1:], store.dtype)

        @pl.when(jnp.logical_not(seam))
        def _():
            store[slot, 1 : VOX + 1] = ref[at]


def conv_rows(store, weights, taps, row, flipped):
    pieces = []
    for _, slot in taps:
        for b in range(3):
            piece = store[slot, pl.ds(row + b, TILE)]
            pieces.append(piece.reshape(TILE * VOX, store.shape[3]))
    stacked = jnp.concatenate(pieces, axis=1)
    products = []
    for c in range(3):
        if flipped:
            tiles = [weights[(2 - a) * 9 + (2 - b) * 3 + 2 - c] for a, _ in taps for b in range(3)]
            dims = (((1,), (1,)), ((), ()))
            tiles = jnp.concatenate(tiles, axis=1)
        else:
            tiles = [weights[a * 9 + b * 3 + c] for a, _ in taps for b in range(3)]
            dims = (((1,), (0,)), ((), ()))
            tiles = jnp.concatenate(tiles, axis=0)
        products.append(
            lax.dot_general(stacked, tiles, dims, preferred_element_type=jnp.float32)
        )
    left, middle, right = products
    column = lax.rem(lax.broadcasted_iota(jnp.int32, left.shape, 0), VOX)
    left = jnp.where(column > 0, pltpu.roll(left, 1, 0), 0.0)
    right = jnp.where(column < VOX - 1, pltpu.roll(right, TILE * VOX - 1, 0), 0.0)
    return middle + left + right


def conv_kernel(part, kind, flipped, finish, counts, *refs):
    refs = list(refs)
    groups = []
    for count in counts:
        groups.append(refs[:count])
        refs = refs[count:]
    planes, pieces, begun, extra, outs = groups
    weights, store, sems = refs
    copies = copy_weights(kind, part, pieces, weights, sems)
    views = []
    for ref in planes:
        views += [(ref, at) for at in range(ref.shape[0])]
    fill_planes(part, views, store)
    for copy in copies:
        copy.wait()
    for plane in range(2):
        taps = PARTS[part]["taps"][plane]

        @pl.loop(0, VOX // TILE)
        def _(step):
            rows = pl.ds(pl.multiple_of(step * TILE, TILE), TILE)
            value = shaped(conv_rows(store, weights, taps, step * TILE, flipped))
            if begun:
                value = value + begun[0][plane, rows]
            finish(value, plane, rows, extra, outs)


def finish_partial(value, plane, rows, extra, outs):
    outs[0][plane, rows] = value


def finish_first(value, plane, rows, extra, outs):
    outs[plane][0, rows] = leaky(value).astype(jnp.bfloat16)


def finish_second(value, plane, rows, extra, outs):
    output, deltas = outs[0], outs[1:]
    output[plane, rows] = leaky(value[:, :, :HALF]).astype(jnp.bfloat16)
    slope = slope_of(value)
    for lane, cot in ((0, extra[0]), (HALF, extra[1])):
        delta = cot[plane, rows].astype(jnp.float32) * slope[:, :, lane : lane + HALF]
        deltas[plane][0, rows, :, lane : lane + HALF] = delta.astype(jnp.bfloat16)


def finish_back(value, plane, rows, extra, outs):
    act = extra[plane][0, rows].astype(jnp.float32)
    outs[plane][0, rows] = (value * slope_of(act)).astype(jnp.bfloat16)


def finish_last(value, plane, rows, extra, outs):
    outs[0][plane, rows] = value.astype(jnp.bfloat16)


def filter_kernel(low, mid_0, mid_1, high, delta_0, delta_1, keep, send, turned, moved):
    pixels = VOX * VOX
    seam = is_seam()
    sources = ((0, low), (1, mid_0), (2, mid_1), (3, high))
    for plane, ref in sources:
        flipped = ref[0].reshape(pixels, HALF).T
        for output_plane in range(2):
            tap = plane - output_plane
            if not 0 <= tap < 3:
                continue
            rows = slice(tap * HALF, (tap + 1) * HALF)
            columns = slice(output_plane * pixels, (output_plane + 1) * pixels)
            if plane in (1, 2) and tap != 1:
                turned[rows, columns] = jnp.where(seam, jnp.zeros_like(flipped), flipped)
            else:
                turned[rows, columns] = flipped
    for plane, ref in ((0, delta_0), (1, delta_1)):
        for c in range(3):
            moved[c, plane, 0] = jnp.zeros(moved.shape[3:], moved.dtype)
            moved[c, plane, VOX + 1] = jnp.zeros(moved.shape[3:], moved.dtype)
        moved[1, plane, 1 : VOX + 1] = ref[0]

        @pl.loop(0, VOX // TILE)
        def _(step):
            row = step * TILE
            values = ref[0, pl.ds(row, TILE)].reshape(TILE * VOX, FULL).astype(jnp.float32)
            column = lax.rem(lax.broadcasted_iota(jnp.int32, values.shape, 0), VOX)
            ahead = jnp.where(column < VOX - 1, pltpu.roll(values, TILE * VOX - 1, 0), 0.0)
            behind = jnp.where(column > 0, pltpu.roll(values, 1, 0), 0.0)
            moved[0, plane, pl.ds(row + 1, TILE)] = shaped(ahead.astype(jnp.bfloat16))
            moved[2, plane, pl.ds(row + 1, TILE)] = shaped(behind.astype(jnp.bfloat16))

    mine = lax.axis_index("chan") == lax.rem(lax.axis_index("dp"), 2)
    for b in range(3):

        @pl.loop(0, 3)
        def _(c):
            right = moved[c, :, 2 - b : 2 - b + VOX].reshape(2 * pixels, FULL)
            product = jnp.dot(turned[...], right, preferred_element_type=jnp.float32)
            kept = jnp.where(mine, product[:, :HALF], product[:, HALF:])
            sent = jnp.where(mine, product[:, HALF:], product[:, :HALF])
            for a in range(3):
                rows = slice(a * HALF, (a + 1) * HALF)
                tap = a * 9 + b * 3 + c
                keep[:, tap] = kept[rows].reshape(8, 16, HALF)
                send[:, tap] = sent[rows].reshape(8, 16, HALF).astype(send.dtype)


def add_core_kernel(keep, came, kept, sent):
    _, side, _ = place()
    for target, first in ((kept, side * 4), (sent, (1 - side) * 4)):

        @pl.loop(0, 4)
        def _(block):
            total = keep[first + block] + came[first + block].astype(jnp.float32)
            target[block] = total.astype(target.dtype)


def add_side_kernel(keep, came, kept, *sent):
    level, _, _ = place()
    for step, target in enumerate((kept,) + sent):
        block = lax.rem(level + step, 4)
        total = keep[block] + came[block].astype(jnp.float32)
        target[...] = total.astype(target.dtype)


def add_level_kernel(scale, keep, *rest):
    total = keep[...]
    for came in rest[:-1]:
        total = total + came[...].astype(jnp.float32)
    rest[-1][...] = (total * scale).astype(rest[-1].dtype)


def join_level_kernel(own, *rest):
    level, _, _ = place()
    target = rest[-1]
    target[level] = own[...]
    for step, came in enumerate(rest[:-1], 1):
        target[lax.rem(level + 4 - step, 4)] = came[...]


def join_side_kernel(own, came, target):
    _, side, _ = place()
    target[pl.ds(side * 4, 4)] = own[...]
    target[pl.ds((1 - side) * 4, 4)] = came[...]


def join_core_kernel(own, came, grad):
    _, _, core = place()

    @pl.loop(0, 8)
    def _(block):
        row = pl.multiple_of(block * 16, 16)
        first = jnp.where(core == 0, own[block], came[block])
        second = jnp.where(core == 0, came[block], own[block])
        grad[:, pl.ds(row, 16), :HALF] = first.astype(jnp.float32)
        grad[:, pl.ds(row, 16), HALF:] = second.astype(jnp.float32)


def small_call(kernel, outs, operands, name):
    moved = sum(ref.size * ref.dtype.itemsize for ref in operands)
    moved += sum(math.prod(shape) * jnp.dtype(dtype).itemsize for shape, dtype in outs)
    return pl.pallas_call(
        kernel,
        out_shape=[jax.ShapeDtypeStruct(shape, dtype) for shape, dtype in outs],
        in_specs=[pl.BlockSpec(memory_space=pltpu.VMEM)] * len(operands),
        out_specs=[pl.BlockSpec(memory_space=pltpu.VMEM)] * len(outs),
        compiler_params=pltpu.CompilerParams(vmem_limit_bytes=VMEM_LIMIT),
        cost_estimate=pl.CostEstimate(flops=0, bytes_accessed=moved, transcendentals=0),
        name=name,
    )(*operands)


PART = (27, 16, HALF)


def to_levels(blocks):
    count = lax.axis_size("dp")
    return [
        lax.ppermute(block, "dp", [(i, (i + 4 * step) % count) for i in range(count)])
        for step, block in enumerate(blocks, 1)
    ]


def sum_core(keep, came, name):
    outs = [((4,) + PART, jnp.float32), ((4,) + PART, jnp.bfloat16)]
    return small_call(add_core_kernel, outs, [keep, came], name + "_core")


def sum_side(keep, came, name):
    outs = [(PART, jnp.float32)] + [(PART, jnp.bfloat16)] * 3
    return small_call(add_side_kernel, outs, [keep, came], name + "_side")


def sum_level(keep, came, scale, name):
    kernel = functools.partial(add_level_kernel, scale)
    return small_call(kernel, [(PART, jnp.bfloat16)], [keep, *came], name + "_level")[0]


def join_level(own, came, name):
    outs = [((4,) + PART, jnp.bfloat16)]
    return small_call(join_level_kernel, outs, [own, *came], name + "_levels")[0]


def join_side(own, came, name):
    outs = [((8,) + PART, jnp.bfloat16)]
    return small_call(join_side_kernel, outs, [own, came], name + "_sides")[0]


def join_core(own, came, name):
    outs = [((27, HALF, FULL), jnp.float32)]
    return small_call(join_core_kernel, outs, [own, came], name + "_cores")[0]


def conv_call(name, part, kind, finish, outs, planes, pieces, begun=(), extra=(), flipped=False):
    lanes = planes[0].shape[3]
    height = {"own": HALF, "quarters": HALF, "both": FULL}[kind]
    depths = len(PARTS[part]["taps"][0])
    flops = 2 * 2 * VOX * VOX * 9 * depths * FULL * height
    operands = [*planes, *pieces, *begun, *extra]
    moved = sum(ref.size * ref.dtype.itemsize for ref in operands)
    counts = (len(planes), len(pieces), len(begun), len(extra), len(outs))
    specs = [pl.BlockSpec(memory_space=pltpu.VMEM) for _ in operands]
    for at in range(len(planes), len(planes) + len(pieces)):
        specs[at] = pl.BlockSpec(memory_space=pl.ANY)
    return pl.pallas_call(
        functools.partial(conv_kernel, part, kind, flipped, finish, counts),
        out_shape=[jax.ShapeDtypeStruct(shape, dtype) for shape, dtype in outs],
        in_specs=specs,
        out_specs=[pl.BlockSpec(memory_space=pltpu.VMEM)] * len(outs),
        scratch_shapes=[
            pltpu.VMEM((27, height, FULL), jnp.bfloat16),
            pltpu.VMEM((len(PARTS[part]["slots"]), VOX + 2, VOX, lanes), jnp.bfloat16),
            pltpu.SemaphoreType.DMA((16,)),
        ],
        compiler_params=pltpu.CompilerParams(vmem_limit_bytes=VMEM_LIMIT),
        cost_estimate=pl.CostEstimate(flops=flops, bytes_accessed=moved, transcendentals=0),
        name=name,
    )(*operands)


def filter_call(planes, mid_at, deltas, name):
    narrow = (1, VOX, VOX, HALF)
    specs = [
        pl.BlockSpec(narrow, functools.partial(lambda at, i: (at, 0, 0, 0), at)) for at in mid_at
    ]
    specs += [pl.BlockSpec((1, VOX, VOX, FULL), lambda i: (0, 0, 0, 0))] * 2
    return pl.pallas_call(
        filter_kernel,
        grid=(1,),
        out_shape=[
            jax.ShapeDtypeStruct((8, 27, 16, HALF), jnp.float32),
            jax.ShapeDtypeStruct((8, 27, 16, HALF), jnp.bfloat16),
        ],
        in_specs=specs,
        out_specs=[pl.BlockSpec((8, 27, 16, HALF), lambda i: (0, 0, 0, 0))] * 2,
        scratch_shapes=[
            pltpu.VMEM((3 * HALF, 2 * VOX * VOX), jnp.bfloat16),
            pltpu.VMEM((3, 2, VOX + 2, VOX, FULL), jnp.bfloat16),
        ],
        compiler_params=pltpu.CompilerParams(vmem_limit_bytes=VMEM_LIMIT),
        cost_estimate=pl.CostEstimate(
            flops=2 * 2 * VOX * VOX * 27 * HALF * FULL, bytes_accessed=8 << 20, transcendentals=0
        ),
        name=name,
    )(*planes, *deltas)


def after(value, *earlier):
    return lax.optimization_barrier((value,) + earlier)[0]


def paired(volume, filter_one, filter_two, cotangent):
    count = lax.axis_size("dp")
    ahead = [(i, (i + 1) % count) for i in range(count)]
    behind = [(target, source) for source, target in ahead]
    scale = 1.0 / math.sqrt(count * 2 * VOX * VOX)
    one = filter_one.reshape(27, HALF, FULL)
    two = filter_two.reshape(27, HALF, FULL)
    _, side, core = place()

    def other(values):
        return lax.ppermute(values, "chan", [(0, 1), (1, 0)])

    def to_core(values):
        return lax.ppermute(values, "dp", [(i, i ^ 1) for i in range(count)])

    def to_side(values):
        return lax.ppermute(values, "dp", [(i, i ^ 2) for i in range(count)])

    def rims(first, last):
        return lax.ppermute(last, "dp", ahead), lax.ppermute(first, "dp", behind)

    wide = ((1, VOX, VOX, FULL), jnp.bfloat16)
    narrow = ((2, VOX, VOX, HALF), jnp.bfloat16)
    partial = ((2, VOX, VOX, FULL), jnp.float32)

    one_0 = other(lax.dynamic_slice_in_dim(one, (2 * side + core) * 32, 32, axis=1))
    low_own, high_own = rims(volume[:1], volume[1:])
    one_1 = to_side(one_0)
    one_2 = to_core(one_0)
    volume_other = other(after(volume, one_0))
    two_same = other(
        after(lax.dynamic_slice_in_dim(two, core * 64, 64, axis=1), volume_other)
    )
    low_other, high_other = rims(volume_other[:1], volume_other[1:])
    one_3 = to_core(one_1)
    quarters = [one_0, one_1, one_2, one_3]

    (begun,) = conv_call(
        "first_own", "all", "own", finish_partial, [partial], [low_own, volume, high_own], [one]
    )
    (begun,) = conv_call(
        "first_other", "local", "quarters", finish_partial, [partial], [volume_other], quarters,
        [begun],
    )
    cot_other = other(after(cotangent, low_other))
    act_0, act_1 = conv_call(
        "first_rim", "rim", "quarters", finish_first, [wide, wide], [low_other, high_other],
        quarters, [begun],
    )
    low_act, high_act = rims(act_0, act_1)
    two_swap = to_core(after(two_same, act_0))
    pieces = [two, two_same, two_swap]
    (begun,) = conv_call(
        "second_local", "local", "both", finish_partial, [partial], [act_0, act_1], pieces
    )
    output, delta_0, delta_1 = conv_call(
        "second_rim", "rim", "both", finish_second, [narrow, wide, wide], [low_act, high_act],
        pieces, [begun], [cotangent, cot_other],
    )
    low_delta, high_delta = rims(delta_0, delta_1)
    keep, send = filter_call(
        [low_act, act_0, act_1, high_act], (0, 0, 0, 0), [delta_0, delta_1], "grad_two"
    )
    came_two = to_core(send)
    (begun,) = conv_call(
        "back_local", "local", "both", finish_partial, [partial], [delta_0, delta_1], pieces,
        flipped=True,
    )
    keep_two, send_two = sum_core(keep, came_two, "sum_two")
    prior_0, prior_1 = conv_call(
        "back_rim", "rim", "both", finish_back, [wide, wide], [after(low_delta, keep_two), high_delta],
        pieces, [begun], [act_0, act_1], flipped=True,
    )
    came_two = to_side(send_two)
    low_prior, high_prior = rims(prior_0, prior_1)
    keep, send = filter_call(
        [low_own, volume, volume, high_own], (0, 0, 1, 0), [prior_0, prior_1], "grad_one"
    )
    came_one = to_core(send)
    keep_two, *sends_two = sum_side(keep_two, came_two, "sum_two")
    keep_one, send_one = sum_core(keep, after(came_one, keep_two), "sum_one")
    came_two = to_levels(sends_two)
    came_one = to_side(send_one)
    own_two = sum_level(keep_two, came_two, scale, "sum_two")
    keep_one, *sends_one = sum_side(keep_one, after(came_one, own_two), "sum_one")
    came_one = to_levels(sends_one)
    came_two = to_levels([own_two] * 3)
    (input_grad,) = conv_call(
        "first_back", "all", "own", finish_last, [narrow], [low_prior, prior_0, prior_1, high_prior],
        [one], flipped=True,
    )
    own_one = sum_level(after(keep_one, input_grad), came_one, scale, "sum_one")
    own_two = join_level(own_two, came_two, "sum_two")
    came_one = to_levels([after(own_one, own_two)] * 3)
    came_two = to_side(own_two)
    own_two = join_side(own_two, came_two, "sum_two")
    own_one = join_level(own_one, [after(came_one[0], own_two)] + came_one[1:], "sum_one")
    came_one = to_side(own_one)
    came_two = to_core(own_two)
    summed_two = join_core(own_two, came_two, "sum_two")
    own_one = join_side(own_one, after(came_one, summed_two), "sum_one")
    summed_one = join_core(own_one, to_core(own_one), "sum_one")
    shape = filter_one.shape
    return output, input_grad, summed_one.reshape(shape), summed_two.reshape(shape)


def local(volume, filter_one, filter_two, cotangent):
    pair = lax.axis_size("chan") == 2 and lax.axis_size("dp") == 16
    if pair and volume.shape == (2, VOX, VOX, HALF):
        return paired(volume, filter_one, filter_two, cotangent)
    return plain(volume, filter_one, filter_two, cotangent)


def solution(mesh):
    in_specs = (
        P("dp", None, None, "chan"),
        P(None, None, None, "chan", None),
        P(None, None, None, "chan", None),
        P("dp", None, None, "chan"),
    )
    out_specs = (
        P("dp", None, None, "chan"),
        P("dp", None, None, "chan"),
        P(None, None, None, "chan", None),
        P(None, None, None, "chan", None),
    )
    return jax.shard_map(local, mesh=mesh, in_specs=in_specs, out_specs=out_specs, check_vma=False)
```

```python
import functools
import math

import jax
import jax.numpy as jnp
from jax import lax
from jax.experimental import pallas as pl
from jax.experimental.pallas import tpu as pltpu
from jax.sharding import PartitionSpec as P

VOX = 32
SLOPE = 0.3
HALF = 128
FULL = 256
TILE = 16
VMEM_LIMIT = 32 * 1024 * 1024


def extended(block, sides, width):
    for axis, dim in sides:
        count = lax.axis_size(axis)
        forward = [(i, i + 1) for i in range(count - 1)]
        forward.append((count - 1, 0))
        backward = [(target, source) for source, target in forward]
        low = lax.ppermute(
            lax.slice_in_dim(block, block.shape[dim] - width, None, axis=dim), axis, forward
        )
        high = lax.ppermute(lax.slice_in_dim(block, 0, width, axis=dim), axis, backward)
        block = jnp.concatenate([low, block, high], axis=dim)
    return block


def leaky(values):
    return jnp.where(values > 0, values, SLOPE * values)


def slope_of(values):
    return jnp.where(values > 0, jnp.float32(1.0), jnp.float32(SLOPE))


def tap_mask(rows, offset):
    base = lax.axis_index("dp") * rows
    total_rows = lax.axis_size("dp") * rows
    planes = jnp.mod(base + jnp.arange(rows, dtype=jnp.int32) - 1, total_rows)
    depth = jnp.mod(planes, VOX) + offset
    inside = jnp.logical_and(depth >= 0, depth < VOX)
    return inside[:, None, None, None]


def pad_plane(values):
    return jnp.pad(values, ((0, 0), (1, 1), (1, 1), (0, 0)))


def columns(plane, rows, height, breadth):
    taps = []
    for a in range(3):
        inside = tap_mask(rows, a - 1)
        depth_slab = plane[a : a + rows]
        depth_slab = jnp.where(inside, depth_slab, jnp.zeros_like(depth_slab))
        for b in range(3):
            for c in range(3):
                taps.append(depth_slab[:, b : b + height, c : c + breadth, :])
    stacked = jnp.concatenate(taps, axis=-1)
    return stacked.reshape(rows * height * breadth, stacked.shape[-1])


def plain(volume, filter_one, filter_two, cotangent):
    rows, height, breadth, narrow = volume.shape
    full = filter_one.shape[4]
    voxels = rows * height * breadth
    scale = 1.0 / math.sqrt(lax.axis_size("dp") * voxels)

    def forward(activity, weight):
        rim = extended(activity, (("dp", 0),), 1)
        plane = pad_plane(rim)
        stacked = columns(plane, rows, height, breadth)
        partial_value = jnp.dot(
            stacked, weight.reshape(27 * narrow, full), preferred_element_type=jnp.float32
        )
        summed = lax.psum_scatter(partial_value, "chan", scatter_dimension=1, tiled=True)
        return (plane, summed)

    def backward(plane, delta, weight):
        wide = lax.all_gather(delta, "chan", axis=3, tiled=True)
        rim = extended(wide, (("dp", 0),), 1)
        centre = rim[1 : rows + 1].reshape(voxels, full)
        stacked = columns(plane, rows, height, breadth)
        weight_grad = lax.dot_general(
            stacked, centre, (((0,), (0,)), ((), ())), preferred_element_type=jnp.float32
        )
        weight_grad = weight_grad.reshape(3, 3, 3, narrow, full)
        source = pad_plane(rim)
        total = jnp.zeros((rows, height, breadth, narrow), jnp.float32)
        for a in range(3):
            depth_slab = source[2 - a : 2 - a + rows]
            flat = depth_slab.reshape(-1, full)
            product = lax.dot_general(
                flat,
                weight[a].reshape(9 * narrow, full),
                (((1,), (1,)), ((), ())),
                preferred_element_type=jnp.float32,
            )
            product = product.reshape(rows, height + 2, breadth + 2, 9, narrow)
            part = jnp.zeros((rows, height, breadth, narrow), jnp.float32)
            for b in range(3):
                for c in range(3):
                    part = (
                        part
                        + product[:, 2 - b : 2 - b + height, 2 - c : 2 - c + breadth, b * 3 + c, :]
                    )
            inside = tap_mask(rows, 1 - a)
            total = total + jnp.where(inside, part, jnp.zeros_like(part))
        return (weight_grad, total.reshape(voxels, narrow))

    def layer_sum(weight_grad):
        return lax.psum(weight_grad, "dp")

    plane_one, pre_one = forward(volume, filter_one)
    act_one = leaky(pre_one).astype(jnp.bfloat16).reshape(rows, height, breadth, narrow)
    plane_two, pre_two = forward(act_one, filter_two)
    output = leaky(pre_two).astype(jnp.bfloat16).reshape(rows, height, breadth, narrow)
    delta_two = (cotangent.reshape(voxels, narrow).astype(jnp.float32) * slope_of(pre_two)).astype(
        jnp.bfloat16
    )
    local_two, back_two = backward(
        plane_two, delta_two.reshape(rows, height, breadth, narrow), filter_two
    )
    summed_two = layer_sum(local_two)
    delta_one = (back_two * slope_of(pre_one)).astype(jnp.bfloat16)
    local_one, back_one = backward(
        plane_one, delta_one.reshape(rows, height, breadth, narrow), filter_one
    )
    summed_one = layer_sum(local_one)
    input_grad = back_one.astype(jnp.bfloat16).reshape(rows, height, breadth, narrow)
    return (output, input_grad, summed_one * scale, summed_two * scale)


def is_seam():
    return lax.rem(lax.axis_index("dp") * 2, VOX) == 0


def place():
    at = lax.axis_index("dp")
    return at // 4, lax.rem(at // 2, 2), lax.rem(at, 2)


def shaped(values):
    return values.reshape(TILE, VOX, values.shape[1])


PARTS = {
    "all": dict(
        slots=((0, True), (1, True), (2, False), (1, False), (2, True), (3, True)),
        taps=(((0, 0), (1, 1), (2, 2)), ((0, 3), (1, 4), (2, 5))),
        depths=(0, 1, 2),
    ),
    "local": dict(
        slots=((0, True), (1, True), (0, False), (1, False)),
        taps=(((1, 0), (2, 3)), ((0, 2), (1, 1))),
        depths=(0, 1, 2),
    ),
    "rim": dict(
        slots=((0, True), (1, True)),
        taps=(((0, 0),), ((2, 1),)),
        depths=(0, 2),
    ),
}


def filter_rows(kind):
    level, side, core = place()
    along, first = (side, 0) if kind == "quarters" else (lax.rem(level, 2), HALF)
    rows = [] if kind == "quarters" else [(HALF, 0)]
    if kind != "own":
        for unit in (core, 1 - core):
            rows += [(32, first + (2 * at + unit) * 32) for at in (along, 1 - along)]
    return rows


def copy_weights(kind, part, pieces, store, sems):
    me = lax.axis_index("chan")
    copies = []
    for (height, row), piece in zip(filter_rows(kind), pieces):
        if not isinstance(row, int):
            row = pl.multiple_of(row, 32)
        spans = ((0, 27),) if part != "rim" else ((0, 9), (18, 9))
        for side in range(2):
            column = pl.multiple_of((me if side == 0 else 1 - me) * HALF, HALF)
            for first, length in spans:
                taps = pl.ds(first, length)
                copies.append(
                    pltpu.make_async_copy(
                        piece.at[taps, :, pl.ds(column, HALF)],
                        store.at[taps, pl.ds(row, height), pl.ds(side * HALF, HALF)],
                        sems.at[len(copies)],
                    )
                )
    for copy in copies:
        copy.start()
    return copies


def fill_planes(part, planes, store):
    edge = jnp.zeros(store.shape[2:], store.dtype)
    seam = is_seam()
    for slot, (plane, always) in enumerate(PARTS[part]["slots"]):
        ref, at = planes[plane]
        store[slot, 0] = edge
        store[slot, VOX + 1] = edge
        if always:
            store[slot, 1 : VOX + 1] = ref[at]
            continue

        @pl.when(seam)
        def _():
            store[slot] = jnp.zeros(store.shape[1:], store.dtype)

        @pl.when(jnp.logical_not(seam))
        def _():
            store[slot, 1 : VOX + 1] = ref[at]


def conv_rows(store, weights, taps, row, flipped):
    pieces = []
    for _, slot in taps:
        for b in range(3):
            piece = store[slot, pl.ds(row + b, TILE)]
            pieces.append(piece.reshape(TILE * VOX, store.shape[3]))
    stacked = jnp.concatenate(pieces, axis=1)
    products = []
    for c in range(3):
        if flipped:
            tiles = [weights[(2 - a) * 9 + (2 - b) * 3 + 2 - c] for a, _ in taps for b in range(3)]
            dims = (((1,), (1,)), ((), ()))
            tiles = jnp.concatenate(tiles, axis=1)
        else:
            tiles = [weights[a * 9 + b * 3 + c] for a, _ in taps for b in range(3)]
            dims = (((1,), (0,)), ((), ()))
            tiles = jnp.concatenate(tiles, axis=0)
        products.append(
            lax.dot_general(stacked, tiles, dims, preferred_element_type=jnp.float32)
        )
    left, middle, right = products
    column = lax.rem(lax.broadcasted_iota(jnp.int32, left.shape, 0), VOX)
    left = jnp.where(column > 0, pltpu.roll(left, 1, 0), 0.0)
    right = jnp.where(column < VOX - 1, pltpu.roll(right, TILE * VOX - 1, 0), 0.0)
    return middle + left + right


def conv_kernel(part, kind, flipped, finish, counts, *refs):
    refs = list(refs)
    groups = []
    for count in counts:
        groups.append(refs[:count])
        refs = refs[count:]
    planes, pieces, begun, extra, outs = groups
    weights, store, sems = refs
    copies = copy_weights(kind, part, pieces, weights, sems)
    views = []
    for ref in planes:
        views += [(ref, at) for at in range(ref.shape[0])]
    fill_planes(part, views, store)
    for copy in copies:
        copy.wait()
    for plane in range(2):
        taps = PARTS[part]["taps"][plane]

        @pl.loop(0, VOX // TILE)
        def _(step):
            rows = pl.ds(pl.multiple_of(step * TILE, TILE), TILE)
            value = shaped(conv_rows(store, weights, taps, step * TILE, flipped))
            if begun:
                value = value + begun[0][plane, rows]
            finish(value, plane, rows, extra, outs)


def finish_partial(value, plane, rows, extra, outs):
    outs[0][plane, rows] = value


def finish_first(value, plane, rows, extra, outs):
    outs[plane][0, rows] = leaky(value).astype(jnp.bfloat16)


def finish_second(value, plane, rows, extra, outs):
    output, deltas = outs[0], outs[1:]
    output[plane, rows] = leaky(value[:, :, :HALF]).astype(jnp.bfloat16)
    slope = slope_of(value)
    for lane, cot in ((0, extra[0]), (HALF, extra[1])):
        delta = cot[plane, rows].astype(jnp.float32) * slope[:, :, lane : lane + HALF]
        deltas[plane][0, rows, :, lane : lane + HALF] = delta.astype(jnp.bfloat16)


def finish_back(value, plane, rows, extra, outs):
    act = extra[plane][0, rows].astype(jnp.float32)
    outs[plane][0, rows] = (value * slope_of(act)).astype(jnp.bfloat16)


def finish_last(value, plane, rows, extra, outs):
    outs[0][plane, rows] = value.astype(jnp.bfloat16)


def filter_kernel(low, mid_0, mid_1, high, delta_0, delta_1, keep, far, near, turned, moved):
    _, side, core = place()
    pixels = VOX * VOX
    seam = is_seam()
    sources = ((0, low), (1, mid_0), (2, mid_1), (3, high))
    for plane, ref in sources:
        flipped = ref[0].reshape(pixels, HALF).T
        for output_plane in range(2):
            tap = plane - output_plane
            if not 0 <= tap < 3:
                continue
            rows = slice(tap * HALF, (tap + 1) * HALF)
            columns = slice(output_plane * pixels, (output_plane + 1) * pixels)
            if plane in (1, 2) and tap != 1:
                turned[rows, columns] = jnp.where(seam, jnp.zeros_like(flipped), flipped)
            else:
                turned[rows, columns] = flipped
    for plane, ref in ((0, delta_0), (1, delta_1)):
        for c in range(3):
            moved[c, plane, 0] = jnp.zeros(moved.shape[3:], moved.dtype)
            moved[c, plane, VOX + 1] = jnp.zeros(moved.shape[3:], moved.dtype)
        moved[1, plane, 1 : VOX + 1] = ref[0]

        @pl.loop(0, VOX // TILE)
        def _(step):
            row = step * TILE
            values = ref[0, pl.ds(row, TILE)].reshape(TILE * VOX, FULL).astype(jnp.float32)
            column = lax.rem(lax.broadcasted_iota(jnp.int32, values.shape, 0), VOX)
            ahead = jnp.where(column < VOX - 1, pltpu.roll(values, TILE * VOX - 1, 0), 0.0)
            behind = jnp.where(column > 0, pltpu.roll(values, 1, 0), 0.0)
            moved[0, plane, pl.ds(row + 1, TILE)] = shaped(ahead.astype(jnp.bfloat16))
            moved[2, plane, pl.ds(row + 1, TILE)] = shaped(behind.astype(jnp.bfloat16))

    mine = lax.axis_index("chan") == core
    for b in range(3):

        @pl.loop(0, 3)
        def _(c):
            right = moved[c, :, 2 - b : 2 - b + VOX].reshape(2 * pixels, FULL)
            product = jnp.dot(turned[...], right, preferred_element_type=jnp.float32)
            kept = jnp.where(mine, product[:, :HALF], product[:, HALF:])
            sent = jnp.where(mine, product[:, HALF:], product[:, :HALF])
            for a in range(3):
                rows = slice(a * HALF, (a + 1) * HALF)
                tap = a * 9 + b * 3 + c
                keep[:, tap] = kept[rows].reshape(8, 16, HALF)
                blocks = sent[rows].reshape(2, 4, 16, HALF).astype(far.dtype)
                far[:, tap] = jnp.where(side == 0, blocks[1], blocks[0])
                near[:, tap] = jnp.where(side == 0, blocks[0], blocks[1])


def add_core_kernel(keep, far, near, kept, sent):
    _, side, _ = place()
    for target, came, first in ((kept, near, side * 4), (sent, far, (1 - side) * 4)):

        @pl.loop(0, 4)
        def _(block):
            total = keep[first + block] + came[block].astype(jnp.float32)
            target[block] = total.astype(target.dtype)


def add_side_kernel(keep, came, kept, *sent):
    level, _, _ = place()
    for step, target in enumerate((kept,) + sent):
        block = lax.rem(level + step, 4)
        total = keep[block] + came[block].astype(jnp.float32)
        target[...] = total.astype(target.dtype)


def add_level_kernel(scale, keep, *rest):
    total = keep[...]
    for came in rest[:-1]:
        total = total + came[...].astype(jnp.float32)
    rest[-1][...] = (total * scale).astype(rest[-1].dtype)


def join_level_kernel(own, *rest):
    level, _, _ = place()
    target = rest[-1]
    target[level] = own[...]
    for step, came in enumerate(rest[:-1], 1):
        target[lax.rem(level + 4 - step, 4)] = came[...]


def join_side_kernel(own, came, target):
    _, side, _ = place()
    target[pl.ds(side * 4, 4)] = own[...]
    target[pl.ds((1 - side) * 4, 4)] = came[...]


def join_core_kernel(own, came, grad):
    _, _, core = place()

    @pl.loop(0, 8)
    def _(block):
        row = pl.multiple_of(block * 16, 16)
        first = jnp.where(core == 0, own[block], came[block])
        second = jnp.where(core == 0, came[block], own[block])
        grad[:, pl.ds(row, 16), :HALF] = first.astype(jnp.float32)
        grad[:, pl.ds(row, 16), HALF:] = second.astype(jnp.float32)


def hint(flops, moved):
    return pl.CostEstimate(flops=0, bytes_accessed=0, transcendentals=0)


def small_call(kernel, outs, operands, name):
    moved = sum(ref.size * ref.dtype.itemsize for ref in operands)
    moved += sum(math.prod(shape) * jnp.dtype(dtype).itemsize for shape, dtype in outs)
    return pl.pallas_call(
        kernel,
        out_shape=[jax.ShapeDtypeStruct(shape, dtype) for shape, dtype in outs],
        in_specs=[pl.BlockSpec(memory_space=pltpu.VMEM)] * len(operands),
        out_specs=[pl.BlockSpec(memory_space=pltpu.VMEM)] * len(outs),
        compiler_params=pltpu.CompilerParams(vmem_limit_bytes=VMEM_LIMIT),
        cost_estimate=hint(0, moved),
        name=name,
    )(*operands)


PART = (27, 16, HALF)


def to_levels(blocks):
    count = lax.axis_size("dp")
    return [
        lax.ppermute(block, "dp", [(i, (i + 4 * step) % count) for i in range(count)])
        for step, block in enumerate(blocks, 1)
    ]


def sum_core(keep, far, near, name):
    outs = [((4,) + PART, jnp.float32), ((4,) + PART, jnp.bfloat16)]
    return small_call(add_core_kernel, outs, [keep, far, near], name + "_core")


def sum_side(keep, came, name):
    outs = [(PART, jnp.float32)] + [(PART, jnp.bfloat16)] * 3
    return small_call(add_side_kernel, outs, [keep, came], name + "_side")


def sum_level(keep, came, scale, name):
    kernel = functools.partial(add_level_kernel, scale)
    return small_call(kernel, [(PART, jnp.bfloat16)], [keep, *came], name + "_level")[0]


def join_level(own, came, name):
    outs = [((4,) + PART, jnp.bfloat16)]
    return small_call(join_level_kernel, outs, [own, *came], name + "_levels")[0]


def join_side(own, came, name):
    outs = [((8,) + PART, jnp.bfloat16)]
    return small_call(join_side_kernel, outs, [own, came], name + "_sides")[0]


def join_core(own, came, name):
    outs = [((27, HALF, FULL), jnp.float32)]
    return small_call(join_core_kernel, outs, [own, came], name + "_cores")[0]


def conv_call(name, part, kind, finish, outs, planes, pieces, begun=(), extra=(), flipped=False):
    lanes = planes[0].shape[3]
    height = {"own": HALF, "quarters": HALF, "both": FULL}[kind]
    depths = len(PARTS[part]["taps"][0])
    flops = 2 * 2 * VOX * VOX * 9 * depths * FULL * height
    operands = [*planes, *pieces, *begun, *extra]
    moved = sum(ref.size * ref.dtype.itemsize for ref in operands)
    counts = (len(planes), len(pieces), len(begun), len(extra), len(outs))
    specs = [pl.BlockSpec(memory_space=pltpu.VMEM) for _ in operands]
    for at in range(len(planes), len(planes) + len(pieces)):
        specs[at] = pl.BlockSpec(memory_space=pl.ANY)
    return pl.pallas_call(
        functools.partial(conv_kernel, part, kind, flipped, finish, counts),
        out_shape=[jax.ShapeDtypeStruct(shape, dtype) for shape, dtype in outs],
        in_specs=specs,
        out_specs=[pl.BlockSpec(memory_space=pltpu.VMEM)] * len(outs),
        scratch_shapes=[
            pltpu.VMEM((27, height, FULL), jnp.bfloat16),
            pltpu.VMEM((len(PARTS[part]["slots"]), VOX + 2, VOX, lanes), jnp.bfloat16),
            pltpu.SemaphoreType.DMA((20,)),
        ],
        compiler_params=pltpu.CompilerParams(vmem_limit_bytes=VMEM_LIMIT),
        cost_estimate=hint(flops, moved),
        name=name,
    )(*operands)


def filter_call(planes, mid_at, deltas, name):
    narrow = (1, VOX, VOX, HALF)
    specs = [
        pl.BlockSpec(narrow, functools.partial(lambda at, i: (at, 0, 0, 0), at)) for at in mid_at
    ]
    specs += [pl.BlockSpec((1, VOX, VOX, FULL), lambda i: (0, 0, 0, 0))] * 2
    return pl.pallas_call(
        filter_kernel,
        grid=(1,),
        out_shape=[
            jax.ShapeDtypeStruct((8, 27, 16, HALF), jnp.float32),
            jax.ShapeDtypeStruct((4, 27, 16, HALF), jnp.bfloat16),
            jax.ShapeDtypeStruct((4, 27, 16, HALF), jnp.bfloat16),
        ],
        in_specs=specs,
        out_specs=[
            pl.BlockSpec((size, 27, 16, HALF), lambda i: (0, 0, 0, 0)) for size in (8, 4, 4)
        ],
        scratch_shapes=[
            pltpu.VMEM((3 * HALF, 2 * VOX * VOX), jnp.bfloat16),
            pltpu.VMEM((3, 2, VOX + 2, VOX, FULL), jnp.bfloat16),
        ],
        compiler_params=pltpu.CompilerParams(vmem_limit_bytes=VMEM_LIMIT),
        cost_estimate=hint(2 * 2 * VOX * VOX * 27 * HALF * FULL, 8 << 20),
        name=name,
    )(*planes, *deltas)


def after(value, *earlier):
    return lax.optimization_barrier((value,) + earlier)[0]


def paired(volume, filter_one, filter_two, cotangent):
    count = lax.axis_size("dp")
    ahead = [(i, (i + 1) % count) for i in range(count)]
    behind = [(target, source) for source, target in ahead]
    scale = 1.0 / math.sqrt(count * 2 * VOX * VOX)
    one = filter_one.reshape(27, HALF, FULL)
    two = filter_two.reshape(27, HALF, FULL)
    level, side, core = place()

    def other(values):
        return lax.ppermute(values, "chan", [(0, 1), (1, 0)])

    def to_core(values):
        return lax.ppermute(values, "dp", [(i, i ^ 1) for i in range(count)])

    def to_side(values):
        return lax.ppermute(values, "dp", [(i, i ^ 2) for i in range(count)])

    def rims(first, last):
        return lax.ppermute(last, "dp", ahead), lax.ppermute(first, "dp", behind)

    wide = ((1, VOX, VOX, FULL), jnp.bfloat16)
    narrow = ((2, VOX, VOX, HALF), jnp.bfloat16)
    partial = ((2, VOX, VOX, FULL), jnp.float32)

    low_own, high_own = rims(volume[:1], volume[1:])
    one_0 = other(lax.dynamic_slice_in_dim(one, (2 * side + core) * 32, 32, axis=1))
    volume_other = other(after(volume, one_0, low_own, high_own))
    one_1 = to_side(one_0)
    one_2 = to_core(one_0)
    one_3 = to_core(one_1)
    quarters = [one_0, one_1, one_2, one_3]
    (begun,) = conv_call(
        "first_own", "all", "own", finish_partial, [partial],
        [after(low_own, volume_other), volume, high_own], [one],
    )
    two_0 = other(
        after(
            lax.dynamic_slice_in_dim(two, (2 * lax.rem(level, 2) + core) * 32, 32, axis=1),
            volume_other,
        )
    )
    low_other, high_other = rims(volume_other[:1], volume_other[1:])
    (begun,) = conv_call(
        "first_other", "local", "quarters", finish_partial, [partial], [volume_other], quarters,
        [begun],
    )
    cot_other = other(after(cotangent, two_0))
    act_0, act_1 = conv_call(
        "first_rim", "rim", "quarters", finish_first, [wide, wide],
        [low_other, high_other], quarters, [begun],
    )
    low_act, high_act = rims(act_0, act_1)
    two_0 = after(two_0, act_0)
    two_1 = lax.ppermute(two_0, "dp", [(i, i ^ 4) for i in range(count)])
    two_2 = to_core(two_0)
    two_3 = to_core(two_1)
    pieces = [two, two_0, two_1, two_2, two_3]
    (begun,) = conv_call(
        "second_local", "local", "both", finish_partial, [partial], [act_0, act_1], pieces
    )
    output, delta_0, delta_1 = conv_call(
        "second_rim", "rim", "both", finish_second, [narrow, wide, wide], [low_act, high_act],
        pieces, [begun], [cotangent, cot_other],
    )
    low_delta, high_delta = rims(delta_0, delta_1)
    keep, far, near = filter_call(
        [low_act, act_0, act_1, high_act], (0, 0, 0, 0), [delta_0, delta_1], "grad_two"
    )
    far, near = to_core(far), to_core(near)
    (begun,) = conv_call(
        "back_local", "local", "both", finish_partial, [partial], [delta_0, delta_1], pieces,
        flipped=True,
    )
    keep_two, send_two = sum_core(after(keep, begun, low_delta, high_delta), far, near, "sum_two")
    prior_0, prior_1 = conv_call(
        "back_rim", "rim", "both", finish_back, [wide, wide], [after(low_delta, keep_two), high_delta],
        pieces, [begun], [act_0, act_1], flipped=True,
    )
    side_two = to_side(send_two)
    keep, far, near = filter_call(
        [low_own, volume, volume, high_own], (0, 0, 1, 0), [prior_0, prior_1], "grad_one"
    )
    far, near = to_core(far), to_core(near)
    keep_two, *sends = sum_side(after(keep_two, keep), side_two, "sum_two")
    levels_two = to_levels(sends)
    keep_one, send_one = sum_core(after(keep, keep_two), far, near, "sum_one")
    side_one = to_side(send_one)
    own_two = sum_level(after(keep_two, keep_one), levels_two, scale, "sum_two")
    levels_two = to_levels([own_two] * 3)
    keep_one, *sends = sum_side(after(keep_one, own_two), side_one, "sum_one")
    low_prior, high_prior = rims(after(prior_0, keep_one), after(prior_1, keep_one))
    levels_one = to_levels(sends)
    own_two = join_level(after(own_two, keep_one), levels_two, "sum_two")
    side_two = to_side(own_two)
    own_one = sum_level(after(keep_one, own_two), levels_one, scale, "sum_one")
    levels_one = to_levels([own_one] * 3)
    (input_grad,) = conv_call(
        "first_back", "all", "own", finish_last, [narrow],
        [low_prior, after(prior_0, own_one), prior_1, high_prior], [one], flipped=True,
    )
    own_two = join_side(after(own_two, own_one), side_two, "sum_two")
    core_two = to_core(own_two)
    own_one = join_level(after(own_one, own_two, input_grad), levels_one, "sum_one")
    side_one = to_side(own_one)
    summed_two = join_core(after(own_two, own_one), core_two, "sum_two")
    own_one = join_side(after(own_one, summed_two), side_one, "sum_one")
    summed_one = join_core(own_one, to_core(own_one), "sum_one")
    shape = filter_one.shape
    return output, input_grad, summed_one.reshape(shape), summed_two.reshape(shape)


def local(volume, filter_one, filter_two, cotangent):
    pair = lax.axis_size("chan") == 2 and lax.axis_size("dp") == 16
    if pair and volume.shape == (2, VOX, VOX, HALF):
        return paired(volume, filter_one, filter_two, cotangent)
    return plain(volume, filter_one, filter_two, cotangent)


def solution(mesh):
    in_specs = (
        P("dp", None, None, "chan"),
        P(None, None, None, "chan", None),
        P(None, None, None, "chan", None),
        P("dp", None, None, "chan"),
    )
    out_specs = (
        P("dp", None, None, "chan"),
        P("dp", None, None, "chan"),
        P(None, None, None, "chan", None),
        P(None, None, None, "chan", None),
    )
    return jax.shard_map(local, mesh=mesh, in_specs=in_specs, out_specs=out_specs, check_vma=False)
```

```python
import functools
import math

import jax
import jax.numpy as jnp
from jax import lax
from jax.experimental import pallas as pl
from jax.experimental.pallas import tpu as pltpu
from jax.sharding import PartitionSpec as P

VOX = 32
SLOPE = 0.3
HALF = 128
FULL = 256
TILE = 16
VMEM_LIMIT = 32 * 1024 * 1024


def extended(block, sides, width):
    for axis, dim in sides:
        count = lax.axis_size(axis)
        forward = [(i, i + 1) for i in range(count - 1)]
        forward.append((count - 1, 0))
        backward = [(target, source) for source, target in forward]
        low = lax.ppermute(
            lax.slice_in_dim(block, block.shape[dim] - width, None, axis=dim), axis, forward
        )
        high = lax.ppermute(lax.slice_in_dim(block, 0, width, axis=dim), axis, backward)
        block = jnp.concatenate([low, block, high], axis=dim)
    return block


def leaky(values):
    return jnp.where(values > 0, values, SLOPE * values)


def slope_of(values):
    return jnp.where(values > 0, jnp.float32(1.0), jnp.float32(SLOPE))


def tap_mask(rows, offset):
    base = lax.axis_index("dp") * rows
    total_rows = lax.axis_size("dp") * rows
    planes = jnp.mod(base + jnp.arange(rows, dtype=jnp.int32) - 1, total_rows)
    depth = jnp.mod(planes, VOX) + offset
    inside = jnp.logical_and(depth >= 0, depth < VOX)
    return inside[:, None, None, None]


def pad_plane(values):
    return jnp.pad(values, ((0, 0), (1, 1), (1, 1), (0, 0)))


def columns(plane, rows, height, breadth):
    taps = []
    for a in range(3):
        inside = tap_mask(rows, a - 1)
        depth_slab = plane[a : a + rows]
        depth_slab = jnp.where(inside, depth_slab, jnp.zeros_like(depth_slab))
        for b in range(3):
            for c in range(3):
                taps.append(depth_slab[:, b : b + height, c : c + breadth, :])
    stacked = jnp.concatenate(taps, axis=-1)
    return stacked.reshape(rows * height * breadth, stacked.shape[-1])


def plain(volume, filter_one, filter_two, cotangent):
    rows, height, breadth, narrow = volume.shape
    full = filter_one.shape[4]
    voxels = rows * height * breadth
    scale = 1.0 / math.sqrt(lax.axis_size("dp") * voxels)

    def forward(activity, weight):
        rim = extended(activity, (("dp", 0),), 1)
        plane = pad_plane(rim)
        stacked = columns(plane, rows, height, breadth)
        partial_value = jnp.dot(
            stacked, weight.reshape(27 * narrow, full), preferred_element_type=jnp.float32
        )
        summed = lax.psum_scatter(partial_value, "chan", scatter_dimension=1, tiled=True)
        return (plane, summed)

    def backward(plane, delta, weight):
        wide = lax.all_gather(delta, "chan", axis=3, tiled=True)
        rim = extended(wide, (("dp", 0),), 1)
        centre = rim[1 : rows + 1].reshape(voxels, full)
        stacked = columns(plane, rows, height, breadth)
        weight_grad = lax.dot_general(
            stacked, centre, (((0,), (0,)), ((), ())), preferred_element_type=jnp.float32
        )
        weight_grad = weight_grad.reshape(3, 3, 3, narrow, full)
        source = pad_plane(rim)
        total = jnp.zeros((rows, height, breadth, narrow), jnp.float32)
        for a in range(3):
            depth_slab = source[2 - a : 2 - a + rows]
            flat = depth_slab.reshape(-1, full)
            product = lax.dot_general(
                flat,
                weight[a].reshape(9 * narrow, full),
                (((1,), (1,)), ((), ())),
                preferred_element_type=jnp.float32,
            )
            product = product.reshape(rows, height + 2, breadth + 2, 9, narrow)
            part = jnp.zeros((rows, height, breadth, narrow), jnp.float32)
            for b in range(3):
                for c in range(3):
                    part = (
                        part
                        + product[:, 2 - b : 2 - b + height, 2 - c : 2 - c + breadth, b * 3 + c, :]
                    )
            inside = tap_mask(rows, 1 - a)
            total = total + jnp.where(inside, part, jnp.zeros_like(part))
        return (weight_grad, total.reshape(voxels, narrow))

    def layer_sum(weight_grad):
        return lax.psum(weight_grad, "dp")

    plane_one, pre_one = forward(volume, filter_one)
    act_one = leaky(pre_one).astype(jnp.bfloat16).reshape(rows, height, breadth, narrow)
    plane_two, pre_two = forward(act_one, filter_two)
    output = leaky(pre_two).astype(jnp.bfloat16).reshape(rows, height, breadth, narrow)
    delta_two = (cotangent.reshape(voxels, narrow).astype(jnp.float32) * slope_of(pre_two)).astype(
        jnp.bfloat16
    )
    local_two, back_two = backward(
        plane_two, delta_two.reshape(rows, height, breadth, narrow), filter_two
    )
    summed_two = layer_sum(local_two)
    delta_one = (back_two * slope_of(pre_one)).astype(jnp.bfloat16)
    local_one, back_one = backward(
        plane_one, delta_one.reshape(rows, height, breadth, narrow), filter_one
    )
    summed_one = layer_sum(local_one)
    input_grad = back_one.astype(jnp.bfloat16).reshape(rows, height, breadth, narrow)
    return (output, input_grad, summed_one * scale, summed_two * scale)


def is_seam():
    return lax.rem(lax.axis_index("dp") * 2, VOX) == 0


def place():
    at = lax.axis_index("dp")
    return at // 4, lax.rem(at // 2, 2), lax.rem(at, 2)


def shaped(values):
    return values.reshape(TILE, VOX, values.shape[1])


PARTS = {
    "all": dict(
        slots=((0, True), (1, True), (2, False), (1, False), (2, True), (3, True)),
        taps=(((0, 0), (1, 1), (2, 2)), ((0, 3), (1, 4), (2, 5))),
    ),
    "local": dict(
        slots=((0, True), (1, True), (0, False), (1, False)),
        taps=(((1, 0), (2, 3)), ((0, 2), (1, 1))),
    ),
    "rim": dict(
        slots=((0, True), (1, True)),
        taps=(((0, 0),), ((2, 1),)),
    ),
}


def filter_rows(kind):
    level, side, core = place()
    along, first = (side, 0) if kind == "quarters" else (lax.rem(level, 2), HALF)
    rows = [] if kind == "quarters" else [(HALF, 0)]
    if kind != "own":
        for unit in (core, 1 - core):
            rows += [(32, first + (2 * at + unit) * 32) for at in (along, 1 - along)]
    return rows


def copy_weights(kind, part, pieces, store, sems):
    me = lax.axis_index("chan")
    copies = []
    for (height, row), piece in zip(filter_rows(kind), pieces):
        if not isinstance(row, int):
            row = pl.multiple_of(row, 32)
        spans = ((0, 27),) if part != "rim" else ((0, 9), (18, 9))
        for side in range(2):
            column = pl.multiple_of((me if side == 0 else 1 - me) * HALF, HALF)
            for first, length in spans:
                taps = pl.ds(first, length)
                copies.append(
                    pltpu.make_async_copy(
                        piece.at[taps, :, pl.ds(column, HALF)],
                        store.at[taps, pl.ds(row, height), pl.ds(side * HALF, HALF)],
                        sems.at[len(copies)],
                    )
                )
    for copy in copies:
        copy.start()
    return copies


def fill_planes(part, planes, store):
    edge = jnp.zeros(store.shape[2:], store.dtype)
    seam = is_seam()
    for slot, (plane, always) in enumerate(PARTS[part]["slots"]):
        ref, at = planes[plane]
        store[slot, 0] = edge
        store[slot, VOX + 1] = edge
        if always:
            store[slot, 1 : VOX + 1] = ref[at]
            continue

        @pl.when(seam)
        def _():
            store[slot] = jnp.zeros(store.shape[1:], store.dtype)

        @pl.when(jnp.logical_not(seam))
        def _():
            store[slot, 1 : VOX + 1] = ref[at]


def conv_rows(store, weights, taps, row, flipped):
    pieces = []
    for _, slot in taps:
        for b in range(3):
            piece = store[slot, pl.ds(row + b, TILE)]
            pieces.append(piece.reshape(TILE * VOX, store.shape[3]))
    stacked = jnp.concatenate(pieces, axis=1)
    products = []
    for c in range(3):
        if flipped:
            tiles = [weights[(2 - a) * 9 + (2 - b) * 3 + 2 - c] for a, _ in taps for b in range(3)]
            dims = (((1,), (1,)), ((), ()))
            tiles = jnp.concatenate(tiles, axis=1)
        else:
            tiles = [weights[a * 9 + b * 3 + c] for a, _ in taps for b in range(3)]
            dims = (((1,), (0,)), ((), ()))
            tiles = jnp.concatenate(tiles, axis=0)
        products.append(
            lax.dot_general(stacked, tiles, dims, preferred_element_type=jnp.float32)
        )
    left, middle, right = products
    column = lax.rem(lax.broadcasted_iota(jnp.int32, left.shape, 0), VOX)
    left = jnp.where(column > 0, pltpu.roll(left, 1, 0), 0.0)
    right = jnp.where(column < VOX - 1, pltpu.roll(right, TILE * VOX - 1, 0), 0.0)
    return middle + left + right


def conv_kernel(part, kind, flipped, finish, counts, *refs):
    refs = list(refs)
    groups = []
    for count in counts:
        groups.append(refs[:count])
        refs = refs[count:]
    planes, pieces, begun, extra, outs = groups
    if kind == "ready":
        (weights,), copies = pieces, []
        (store,) = refs
    else:
        store, sems = refs
        weights = outs.pop()
        copies = copy_weights(kind, part, pieces, weights, sems)
    views = []
    for ref in planes:
        views += [(ref, at) for at in range(ref.shape[0])]
    fill_planes(part, views, store)
    for copy in copies:
        copy.wait()
    for plane in range(2):
        taps = PARTS[part]["taps"][plane]

        @pl.loop(0, VOX // TILE)
        def _(step):
            rows = pl.ds(pl.multiple_of(step * TILE, TILE), TILE)
            value = shaped(conv_rows(store, weights, taps, step * TILE, flipped))
            if begun:
                value = value + begun[0][plane, rows]
            finish(value, plane, rows, extra, outs)


def finish_partial(value, plane, rows, extra, outs):
    outs[0][plane, rows] = value


def finish_first(value, plane, rows, extra, outs):
    outs[plane][0, rows] = leaky(value).astype(jnp.bfloat16)


def finish_second(value, plane, rows, extra, outs):
    output, deltas = outs[0], outs[1:]
    output[plane, rows] = leaky(value[:, :, :HALF]).astype(jnp.bfloat16)
    slope = slope_of(value)
    for lane, cot in ((0, extra[0]), (HALF, extra[1])):
        delta = cot[plane, rows].astype(jnp.float32) * slope[:, :, lane : lane + HALF]
        deltas[plane][0, rows, :, lane : lane + HALF] = delta.astype(jnp.bfloat16)


def finish_back(value, plane, rows, extra, outs):
    act = extra[plane][0, rows].astype(jnp.float32)
    outs[plane][0, rows] = (value * slope_of(act)).astype(jnp.bfloat16)


def finish_last(value, plane, rows, extra, outs):
    outs[0][plane, rows] = value.astype(jnp.bfloat16)


def filter_kernel(low, mid_0, mid_1, high, delta_0, delta_1, keep, far, near, turned, moved):
    _, side, core = place()
    pixels = VOX * VOX
    seam = is_seam()
    sources = ((0, low), (1, mid_0), (2, mid_1), (3, high))
    for plane, ref in sources:
        flipped = ref[0].reshape(pixels, HALF).T
        for output_plane in range(2):
            tap = plane - output_plane
            if not 0 <= tap < 3:
                continue
            rows = slice(tap * HALF, (tap + 1) * HALF)
            columns = slice(output_plane * pixels, (output_plane + 1) * pixels)
            if plane in (1, 2) and tap != 1:
                turned[rows, columns] = jnp.where(seam, jnp.zeros_like(flipped), flipped)
            else:
                turned[rows, columns] = flipped
    for plane, ref in ((0, delta_0), (1, delta_1)):
        for c in range(3):
            moved[c, plane, 0] = jnp.zeros(moved.shape[3:], moved.dtype)
            moved[c, plane, VOX + 1] = jnp.zeros(moved.shape[3:], moved.dtype)
        moved[1, plane, 1 : VOX + 1] = ref[0]

        @pl.loop(0, VOX // TILE)
        def _(step):
            row = step * TILE
            values = ref[0, pl.ds(row, TILE)].reshape(TILE * VOX, FULL).astype(jnp.float32)
            column = lax.rem(lax.broadcasted_iota(jnp.int32, values.shape, 0), VOX)
            ahead = jnp.where(column < VOX - 1, pltpu.roll(values, TILE * VOX - 1, 0), 0.0)
            behind = jnp.where(column > 0, pltpu.roll(values, 1, 0), 0.0)
            moved[0, plane, pl.ds(row + 1, TILE)] = shaped(ahead.astype(jnp.bfloat16))
            moved[2, plane, pl.ds(row + 1, TILE)] = shaped(behind.astype(jnp.bfloat16))

    mine = lax.axis_index("chan") == core
    for b in range(3):

        @pl.loop(0, 3)
        def _(c):
            right = moved[c, :, 2 - b : 2 - b + VOX].reshape(2 * pixels, FULL)
            product = jnp.dot(turned[...], right, preferred_element_type=jnp.float32)
            kept = jnp.where(mine, product[:, :HALF], product[:, HALF:])
            sent = jnp.where(mine, product[:, HALF:], product[:, :HALF])
            for a in range(3):
                rows = slice(a * HALF, (a + 1) * HALF)
                tap = a * 9 + b * 3 + c
                keep[:, tap] = kept[rows].reshape(8, 16, HALF)
                blocks = sent[rows].reshape(2, 4, 16, HALF).astype(far.dtype)
                far[:, tap] = jnp.where(side == 0, blocks[1], blocks[0])
                near[:, tap] = jnp.where(side == 0, blocks[0], blocks[1])


def add_core_kernel(keep, far, near, kept, sent):
    _, side, _ = place()
    for target, came, first in ((kept, near, side * 4), (sent, far, (1 - side) * 4)):

        @pl.loop(0, 4)
        def _(block):
            total = keep[first + block] + came[block].astype(jnp.float32)
            target[block] = total.astype(target.dtype)


def add_side_kernel(keep, came, kept, *sent):
    level, _, _ = place()
    for step, target in enumerate((kept,) + sent):
        block = lax.rem(level + step, 4)
        total = keep[block] + came[block].astype(jnp.float32)
        target[...] = total.astype(target.dtype)


def add_level_kernel(scale, keep, *rest):
    total = keep[...]
    for came in rest[:-1]:
        total = total + came[...].astype(jnp.float32)
    rest[-1][...] = (total * scale).astype(rest[-1].dtype)


def add_core_level_kernel(keep, far, near, kept, *sent):
    level, side, _ = place()
    for step, target in enumerate((kept,) + sent):
        block = lax.rem(level + step, 4)
        for at, (came, first) in enumerate(((near, side * 4), (far, (1 - side) * 4))):
            total = keep[first + block] + came[block].astype(jnp.float32)
            target[at] = total.astype(target.dtype)


def add_level_far_kernel(keep, *rest):
    came, (near, far) = rest[:-2], rest[-2:]
    for at, target in ((0, near), (1, far)):
        total = keep[at]
        for block in came:
            total = total + block[at].astype(jnp.float32)
        target[...] = total.astype(target.dtype)


def join_level_kernel(own, *rest):
    level, _, _ = place()
    target = rest[-1]
    target[level] = own[...]
    for step, came in enumerate(rest[:-1], 1):
        target[lax.rem(level + 4 - step, 4)] = came[...]


def join_side_kernel(own, came, target):
    _, side, _ = place()
    target[pl.ds(side * 4, 4)] = own[...]
    target[pl.ds((1 - side) * 4, 4)] = came[...]


def join_core_kernel(own, came, grad):
    _, _, core = place()

    @pl.loop(0, 8)
    def _(block):
        row = pl.multiple_of(block * 16, 16)
        first = jnp.where(core == 0, own[block], came[block])
        second = jnp.where(core == 0, came[block], own[block])
        grad[:, pl.ds(row, 16), :HALF] = first.astype(jnp.float32)
        grad[:, pl.ds(row, 16), HALF:] = second.astype(jnp.float32)


WEIGHT = {"sum_two_core": 0, "sum_one_level": 10**10, "sum_one_levels": 10**10}


def hint(flops):
    return pl.CostEstimate(flops=flops, bytes_accessed=0, transcendentals=0)


def small_call(kernel, outs, operands, name):
    return pl.pallas_call(
        kernel,
        out_shape=[jax.ShapeDtypeStruct(shape, dtype) for shape, dtype in outs],
        in_specs=[pl.BlockSpec(memory_space=pltpu.VMEM)] * len(operands),
        out_specs=[pl.BlockSpec(memory_space=pltpu.VMEM)] * len(outs),
        compiler_params=pltpu.CompilerParams(vmem_limit_bytes=VMEM_LIMIT),
        cost_estimate=hint(WEIGHT.get(name, 3 * 10**9)),
        name=name,
    )(*operands)


PART = (27, 16, HALF)


def to_levels(blocks):
    count = lax.axis_size("dp")
    return [
        lax.ppermute(block, "dp", [(i, (i + 4 * step) % count) for i in range(count)])
        for step, block in enumerate(blocks, 1)
    ]


def sum_core(keep, far, near, name):
    outs = [((4,) + PART, jnp.float32), ((4,) + PART, jnp.bfloat16)]
    return small_call(add_core_kernel, outs, [keep, far, near], name + "_core")


def sum_side(keep, came, name):
    outs = [(PART, jnp.float32)] + [(PART, jnp.bfloat16)] * 3
    return small_call(add_side_kernel, outs, [keep, came], name + "_side")


def sum_level(keep, came, scale, name):
    kernel = functools.partial(add_level_kernel, scale)
    return small_call(kernel, [(PART, jnp.bfloat16)], [keep, *came], name + "_level")[0]


def sum_core_level(keep, far, near, name):
    pair = (2,) + PART
    outs = [(pair, jnp.float32)] + [(pair, jnp.bfloat16)] * 3
    return small_call(add_core_level_kernel, outs, [keep, far, near], name + "_core")


def sum_level_far(keep, came, name):
    outs = [(PART, jnp.float32), (PART, jnp.bfloat16)]
    return small_call(add_level_far_kernel, outs, [keep, *came], name + "_level")


def join_level(own, came, name):
    outs = [((4,) + PART, jnp.bfloat16)]
    return small_call(join_level_kernel, outs, [own, *came], name + "_levels")[0]


def join_side(own, came, name):
    outs = [((8,) + PART, jnp.bfloat16)]
    return small_call(join_side_kernel, outs, [own, came], name + "_sides")[0]


def join_core(own, came, name):
    outs = [((27, HALF, FULL), jnp.float32)]
    return small_call(join_core_kernel, outs, [own, came], name + "_cores")[0]


def conv_call(name, part, kind, finish, outs, planes, pieces, begun=(), extra=(), flipped=False):
    lanes = planes[0].shape[3]
    height = {"own": HALF, "quarters": HALF, "both": FULL, "ready": pieces[0].shape[1]}[kind]
    ready = kind == "ready"
    if not ready:
        outs = outs + [((27, height, FULL), jnp.bfloat16)]
    operands = [*planes, *pieces, *begun, *extra]
    counts = (len(planes), len(pieces), len(begun), len(extra), len(outs))
    specs = [pl.BlockSpec(memory_space=pltpu.VMEM) for _ in operands]
    if not ready:
        for at in range(len(planes), len(planes) + len(pieces)):
            own = kind != "quarters" and at == len(planes)
            specs[at] = pl.BlockSpec(memory_space=pltpu.HBM if own else pl.ANY)
    scratch = [pltpu.VMEM((len(PARTS[part]["slots"]), VOX + 2, VOX, lanes), jnp.bfloat16)]
    if not ready:
        scratch.append(pltpu.SemaphoreType.DMA((20,)))
    return pl.pallas_call(
        functools.partial(conv_kernel, part, kind, flipped, finish, counts),
        out_shape=[jax.ShapeDtypeStruct(shape, dtype) for shape, dtype in outs],
        in_specs=specs,
        out_specs=[pl.BlockSpec(memory_space=pltpu.VMEM)] * len(outs),
        scratch_shapes=scratch,
        compiler_params=pltpu.CompilerParams(vmem_limit_bytes=VMEM_LIMIT),
        cost_estimate=hint(0),
        name=name,
    )(*operands)


def filter_call(planes, mid_at, deltas, name):
    narrow = (1, VOX, VOX, HALF)
    specs = [
        pl.BlockSpec(narrow, functools.partial(lambda at, i: (at, 0, 0, 0), at)) for at in mid_at
    ]
    specs += [pl.BlockSpec((1, VOX, VOX, FULL), lambda i: (0, 0, 0, 0))] * 2
    return pl.pallas_call(
        filter_kernel,
        grid=(1,),
        out_shape=[
            jax.ShapeDtypeStruct((8, 27, 16, HALF), jnp.float32),
            jax.ShapeDtypeStruct((4, 27, 16, HALF), jnp.bfloat16),
            jax.ShapeDtypeStruct((4, 27, 16, HALF), jnp.bfloat16),
        ],
        in_specs=specs,
        out_specs=[
            pl.BlockSpec((size, 27, 16, HALF), lambda i: (0, 0, 0, 0)) for size in (8, 4, 4)
        ],
        scratch_shapes=[
            pltpu.VMEM((3 * HALF, 2 * VOX * VOX), jnp.bfloat16),
            pltpu.VMEM((3, 2, VOX + 2, VOX, FULL), jnp.bfloat16),
        ],
        compiler_params=pltpu.CompilerParams(vmem_limit_bytes=VMEM_LIMIT),
        cost_estimate=hint(0),
        name=name,
    )(*planes, *deltas)


def after(value, *earlier):
    return lax.optimization_barrier((value,) + earlier)[0]


def paired(volume, filter_one, filter_two, cotangent):
    count = lax.axis_size("dp")
    ahead = [(i, (i + 1) % count) for i in range(count)]
    behind = [(target, source) for source, target in ahead]
    scale = 1.0 / math.sqrt(count * 2 * VOX * VOX)
    one = filter_one.reshape(27, HALF, FULL)
    two = filter_two.reshape(27, HALF, FULL)
    level, side, core = place()

    def other(values):
        return lax.ppermute(values, "chan", [(0, 1), (1, 0)])

    def to_core(values):
        return lax.ppermute(values, "dp", [(i, i ^ 1) for i in range(count)])

    def to_side(values):
        return lax.ppermute(values, "dp", [(i, i ^ 2) for i in range(count)])

    def rims(first, last):
        return lax.ppermute(last, "dp", ahead), lax.ppermute(first, "dp", behind)

    wide = ((1, VOX, VOX, FULL), jnp.bfloat16)
    narrow = ((2, VOX, VOX, HALF), jnp.bfloat16)
    partial = ((2, VOX, VOX, FULL), jnp.float32)

    low_own, high_own = rims(volume[:1], volume[1:])
    one_0 = other(lax.dynamic_slice_in_dim(one, (2 * side + core) * 32, 32, axis=1))
    volume_other = other(after(volume, one_0, low_own, high_own))
    one_1 = to_side(one_0)
    one_2 = to_core(one_0)
    one_3 = to_core(one_1)
    quarters = [one_0, one_1, one_2, one_3]
    begun, own_ready = conv_call(
        "first_own", "all", "own", finish_partial, [partial],
        [after(low_own, volume_other), volume, high_own], [one],
    )
    two_0 = other(
        after(
            lax.dynamic_slice_in_dim(two, (2 * lax.rem(level, 2) + core) * 32, 32, axis=1),
            volume_other,
        )
    )
    low_other, high_other = rims(volume_other[:1], volume_other[1:])
    two_0 = after(two_0, begun)
    two_1 = lax.ppermute(two_0, "dp", [(i, i ^ 4) for i in range(count)])
    two_2 = to_core(two_0)
    cot_other = other(after(cotangent, two_0))
    begun, ready = conv_call(
        "first_other", "local", "quarters", finish_partial, [partial], [volume_other], quarters,
        [after(begun, two_0)],
    )
    act_0, act_1 = conv_call(
        "first_rim", "rim", "ready", finish_first, [wide, wide], [low_other, high_other],
        [ready], [begun],
    )
    low_act, high_act = rims(act_0, act_1)
    two_3 = to_core(two_1)
    pieces = [two, two_0, two_1, two_2, two_3]
    begun, ready = conv_call(
        "second_local", "local", "both", finish_partial, [partial], [act_0, act_1], pieces
    )
    output, delta_0, delta_1 = conv_call(
        "second_rim", "rim", "ready", finish_second, [narrow, wide, wide], [low_act, high_act],
        [ready], [begun], [cotangent, cot_other],
    )
    low_delta, high_delta = rims(delta_0, delta_1)
    keep, far, near = filter_call(
        [low_act, act_0, act_1, high_act], (0, 0, 0, 0), [delta_0, delta_1], "grad_two"
    )
    keep_two, *sends = sum_core_level(keep, to_core(far), to_core(near), "sum_two")
    levels_two = to_levels(sends)
    (begun,) = conv_call(
        "back_local", "local", "ready", finish_partial, [partial], [delta_0, after(delta_1, keep_two)],
        [ready], flipped=True,
    )
    prior_0, prior_1 = conv_call(
        "back_rim", "rim", "ready", finish_back, [wide, wide], [low_delta, high_delta],
        [ready], [begun], [act_0, act_1], flipped=True,
    )
    keep, far, near = filter_call(
        [low_own, volume, volume, high_own], (0, 0, 1, 0), [prior_0, prior_1], "grad_one"
    )
    far, near = to_core(far), to_core(near)
    keep_two, send_two = sum_level_far(after(keep_two, keep), levels_two, "sum_two")
    side_two = to_side(send_two)
    keep_one, send_one = sum_core(after(keep, keep_two), far, near, "sum_one")
    side_one = to_side(send_one)
    own_two = sum_level(after(keep_two, keep_one), [side_two], scale, "sum_two_side")
    levels_two = to_levels([own_two] * 3)
    keep_one, *sends = sum_side(after(keep_one, own_two), side_one, "sum_one")
    low_prior, high_prior = rims(after(prior_0, keep_one), after(prior_1, keep_one))
    levels_one = to_levels(sends)
    own_two = join_level(after(own_two, keep_one), levels_two, "sum_two")
    side_two = to_side(own_two)
    own_one = sum_level(after(keep_one, own_two), levels_one, scale, "sum_one")
    levels_one = to_levels([own_one] * 3)
    (input_grad,) = conv_call(
        "first_back", "all", "ready", finish_last, [narrow],
        [low_prior, after(prior_0, own_one), prior_1, high_prior], [own_ready], flipped=True,
    )
    own_two = join_side(after(own_two, input_grad), side_two, "sum_two")
    core_two = to_core(own_two)
    own_one = join_level(after(own_one, own_two), levels_one, "sum_one")
    side_one = to_side(own_one)
    summed_two = join_core(after(own_two, own_one), core_two, "sum_two")
    own_one = join_side(after(own_one, summed_two), side_one, "sum_one")
    summed_one = join_core(own_one, to_core(own_one), "sum_one")
    shape = filter_one.shape
    return output, input_grad, summed_one.reshape(shape), summed_two.reshape(shape)


def local(volume, filter_one, filter_two, cotangent):
    pair = lax.axis_size("chan") == 2 and lax.axis_size("dp") == 16
    if pair and volume.shape == (2, VOX, VOX, HALF):
        return paired(volume, filter_one, filter_two, cotangent)
    return plain(volume, filter_one, filter_two, cotangent)


def solution(mesh):
    in_specs = (
        P("dp", None, None, "chan"),
        P(None, None, None, "chan", None),
        P(None, None, None, "chan", None),
        P("dp", None, None, "chan"),
    )
    out_specs = (
        P("dp", None, None, "chan"),
        P("dp", None, None, "chan"),
        P(None, None, None, "chan", None),
        P(None, None, None, "chan", None),
    )
    return jax.shard_map(local, mesh=mesh, in_specs=in_specs, out_specs=out_specs, check_vma=False)
```

```python
import functools
import math

import jax
import jax.numpy as jnp
from jax import lax
from jax.experimental import pallas as pl
from jax.experimental.pallas import tpu as pltpu
from jax.sharding import PartitionSpec as P

VOX = 32
SLOPE = 0.3
HALF = 128
FULL = 256
TILE = 16
VMEM_LIMIT = 32 * 1024 * 1024


def extended(block, sides, width):
    for axis, dim in sides:
        count = lax.axis_size(axis)
        forward = [(i, i + 1) for i in range(count - 1)]
        forward.append((count - 1, 0))
        backward = [(target, source) for source, target in forward]
        low = lax.ppermute(
            lax.slice_in_dim(block, block.shape[dim] - width, None, axis=dim), axis, forward
        )
        high = lax.ppermute(lax.slice_in_dim(block, 0, width, axis=dim), axis, backward)
        block = jnp.concatenate([low, block, high], axis=dim)
    return block


def leaky(values):
    return jnp.where(values > 0, values, SLOPE * values)


def slope_of(values):
    return jnp.where(values > 0, jnp.float32(1.0), jnp.float32(SLOPE))


def tap_mask(rows, offset):
    base = lax.axis_index("dp") * rows
    total_rows = lax.axis_size("dp") * rows
    planes = jnp.mod(base + jnp.arange(rows, dtype=jnp.int32) - 1, total_rows)
    depth = jnp.mod(planes, VOX) + offset
    inside = jnp.logical_and(depth >= 0, depth < VOX)
    return inside[:, None, None, None]


def pad_plane(values):
    return jnp.pad(values, ((0, 0), (1, 1), (1, 1), (0, 0)))


def columns(plane, rows, height, breadth):
    taps = []
    for a in range(3):
        inside = tap_mask(rows, a - 1)
        depth_slab = plane[a : a + rows]
        depth_slab = jnp.where(inside, depth_slab, jnp.zeros_like(depth_slab))
        for b in range(3):
            for c in range(3):
                taps.append(depth_slab[:, b : b + height, c : c + breadth, :])
    stacked = jnp.concatenate(taps, axis=-1)
    return stacked.reshape(rows * height * breadth, stacked.shape[-1])


def plain(volume, filter_one, filter_two, cotangent):
    rows, height, breadth, narrow = volume.shape
    full = filter_one.shape[4]
    voxels = rows * height * breadth
    scale = 1.0 / math.sqrt(lax.axis_size("dp") * voxels)

    def forward(activity, weight):
        rim = extended(activity, (("dp", 0),), 1)
        plane = pad_plane(rim)
        stacked = columns(plane, rows, height, breadth)
        partial_value = jnp.dot(
            stacked, weight.reshape(27 * narrow, full), preferred_element_type=jnp.float32
        )
        summed = lax.psum_scatter(partial_value, "chan", scatter_dimension=1, tiled=True)
        return (plane, summed)

    def backward(plane, delta, weight):
        wide = lax.all_gather(delta, "chan", axis=3, tiled=True)
        rim = extended(wide, (("dp", 0),), 1)
        centre = rim[1 : rows + 1].reshape(voxels, full)
        stacked = columns(plane, rows, height, breadth)
        weight_grad = lax.dot_general(
            stacked, centre, (((0,), (0,)), ((), ())), preferred_element_type=jnp.float32
        )
        weight_grad = weight_grad.reshape(3, 3, 3, narrow, full)
        source = pad_plane(rim)
        total = jnp.zeros((rows, height, breadth, narrow), jnp.float32)
        for a in range(3):
            depth_slab = source[2 - a : 2 - a + rows]
            flat = depth_slab.reshape(-1, full)
            product = lax.dot_general(
                flat,
                weight[a].reshape(9 * narrow, full),
                (((1,), (1,)), ((), ())),
                preferred_element_type=jnp.float32,
            )
            product = product.reshape(rows, height + 2, breadth + 2, 9, narrow)
            part = jnp.zeros((rows, height, breadth, narrow), jnp.float32)
            for b in range(3):
                for c in range(3):
                    part = (
                        part
                        + product[:, 2 - b : 2 - b + height, 2 - c : 2 - c + breadth, b * 3 + c, :]
                    )
            inside = tap_mask(rows, 1 - a)
            total = total + jnp.where(inside, part, jnp.zeros_like(part))
        return (weight_grad, total.reshape(voxels, narrow))

    def layer_sum(weight_grad):
        return lax.psum(weight_grad, "dp")

    plane_one, pre_one = forward(volume, filter_one)
    act_one = leaky(pre_one).astype(jnp.bfloat16).reshape(rows, height, breadth, narrow)
    plane_two, pre_two = forward(act_one, filter_two)
    output = leaky(pre_two).astype(jnp.bfloat16).reshape(rows, height, breadth, narrow)
    delta_two = (cotangent.reshape(voxels, narrow).astype(jnp.float32) * slope_of(pre_two)).astype(
        jnp.bfloat16
    )
    local_two, back_two = backward(
        plane_two, delta_two.reshape(rows, height, breadth, narrow), filter_two
    )
    summed_two = layer_sum(local_two)
    delta_one = (back_two * slope_of(pre_one)).astype(jnp.bfloat16)
    local_one, back_one = backward(
        plane_one, delta_one.reshape(rows, height, breadth, narrow), filter_one
    )
    summed_one = layer_sum(local_one)
    input_grad = back_one.astype(jnp.bfloat16).reshape(rows, height, breadth, narrow)
    return (output, input_grad, summed_one * scale, summed_two * scale)


def is_seam():
    return lax.rem(lax.axis_index("dp") * 2, VOX) == 0


def place():
    at = lax.axis_index("dp")
    return at // 4, lax.rem(at // 2, 2), lax.rem(at, 2)


def place_bits():
    level, side, _ = place()
    return {"x": side, "z": lax.rem(level, 2), "zz": level // 2}


def shaped(values):
    return values.reshape(TILE, VOX, values.shape[1])


PARTS = {
    "all": dict(
        slots=((0, True), (1, True), (2, False), (1, False), (2, True), (3, True)),
        taps=(((0, 0), (1, 1), (2, 2)), ((0, 3), (1, 4), (2, 5))),
    ),
    "local": dict(
        slots=((0, True), (1, True), (0, False), (1, False)),
        taps=(((1, 0), (2, 3)), ((0, 2), (1, 1))),
    ),
    "rim": dict(
        slots=((0, True), (1, True)),
        taps=(((0, 0),), ((2, 1),)),
    ),
}


def filter_rows(kind):
    level, side, core = place()
    along, first = (side, 0) if kind == "quarters" else (lax.rem(level, 2), HALF)
    rows = [] if kind == "quarters" else [(HALF, 0)]
    if kind != "own":
        for unit in (core, 1 - core):
            rows += [(32, first + (2 * at + unit) * 32) for at in (along, 1 - along)]
    return rows


def copy_weights(kind, part, pieces, store, sems):
    me = lax.axis_index("chan")
    copies = []
    for (height, row), piece in zip(filter_rows(kind), pieces):
        if not isinstance(row, int):
            row = pl.multiple_of(row, 32)
        spans = ((0, 27),) if part != "rim" else ((0, 9), (18, 9))
        for side in range(2):
            column = pl.multiple_of((me if side == 0 else 1 - me) * HALF, HALF)
            for first, length in spans:
                taps = pl.ds(first, length)
                copies.append(
                    pltpu.make_async_copy(
                        piece.at[taps, :, pl.ds(column, HALF)],
                        store.at[taps, pl.ds(row, height), pl.ds(side * HALF, HALF)],
                        sems.at[len(copies)],
                    )
                )
    for copy in copies:
        copy.start()
    return copies


def fill_planes(part, planes, store):
    edge = jnp.zeros(store.shape[2:], store.dtype)
    seam = is_seam()
    for slot, (plane, always) in enumerate(PARTS[part]["slots"]):
        ref, at = planes[plane]
        store[slot, 0] = edge
        store[slot, VOX + 1] = edge
        if always:
            store[slot, 1 : VOX + 1] = ref[at]
            continue

        @pl.when(seam)
        def _():
            store[slot] = jnp.zeros(store.shape[1:], store.dtype)

        @pl.when(jnp.logical_not(seam))
        def _():
            store[slot, 1 : VOX + 1] = ref[at]


def conv_rows(store, weights, taps, row, flipped):
    pieces = []
    for _, slot in taps:
        for b in range(3):
            piece = store[slot, pl.ds(row + b, TILE)]
            pieces.append(piece.reshape(TILE * VOX, store.shape[3]))
    stacked = jnp.concatenate(pieces, axis=1)
    products = []
    for c in range(3):
        if flipped:
            tiles = [weights[(2 - a) * 9 + (2 - b) * 3 + 2 - c] for a, _ in taps for b in range(3)]
            dims = (((1,), (1,)), ((), ()))
            tiles = jnp.concatenate(tiles, axis=1)
        else:
            tiles = [weights[a * 9 + b * 3 + c] for a, _ in taps for b in range(3)]
            dims = (((1,), (0,)), ((), ()))
            tiles = jnp.concatenate(tiles, axis=0)
        products.append(
            lax.dot_general(stacked, tiles, dims, preferred_element_type=jnp.float32)
        )
    left, middle, right = products
    column = lax.rem(lax.broadcasted_iota(jnp.int32, left.shape, 0), VOX)
    left = jnp.where(column > 0, pltpu.roll(left, 1, 0), 0.0)
    right = jnp.where(column < VOX - 1, pltpu.roll(right, TILE * VOX - 1, 0), 0.0)
    return middle + left + right


def conv_kernel(part, kind, flipped, finish, counts, *refs):
    refs = list(refs)
    groups = []
    for count in counts:
        groups.append(refs[:count])
        refs = refs[count:]
    planes, pieces, begun, extra, outs = groups
    if kind == "ready":
        (weights,), copies = pieces, []
        (store,) = refs
    else:
        store, sems = refs
        weights = outs.pop()
        copies = copy_weights(kind, part, pieces, weights, sems)
    views = []
    for ref in planes:
        views += [(ref, at) for at in range(ref.shape[0])]
    fill_planes(part, views, store)
    for copy in copies:
        copy.wait()
    for plane in range(2):
        taps = PARTS[part]["taps"][plane]

        @pl.loop(0, VOX // TILE)
        def _(step):
            rows = pl.ds(pl.multiple_of(step * TILE, TILE), TILE)
            value = shaped(conv_rows(store, weights, taps, step * TILE, flipped))
            if begun:
                value = value + begun[0][plane, rows]
            finish(value, plane, rows, extra, outs)


def finish_partial(value, plane, rows, extra, outs):
    outs[0][plane, rows] = value


def finish_first(value, plane, rows, extra, outs):
    outs[plane][0, rows] = leaky(value).astype(jnp.bfloat16)


def finish_second(value, plane, rows, extra, outs):
    output, deltas = outs[0], outs[1:]
    output[plane, rows] = leaky(value[:, :, :HALF]).astype(jnp.bfloat16)
    slope = slope_of(value)
    for lane, cot in ((0, extra[0]), (HALF, extra[1])):
        delta = cot[plane, rows].astype(jnp.float32) * slope[:, :, lane : lane + HALF]
        deltas[plane][0, rows, :, lane : lane + HALF] = delta.astype(jnp.bfloat16)


def finish_back(value, plane, rows, extra, outs):
    act = extra[plane][0, rows].astype(jnp.float32)
    outs[plane][0, rows] = (value * slope_of(act)).astype(jnp.bfloat16)


def finish_last(value, plane, rows, extra, outs):
    outs[0][plane, rows] = value.astype(jnp.bfloat16)


def filter_kernel(axis, low, mid_0, mid_1, high, delta_0, delta_1, keep, far, near, turned, moved):
    _, _, core = place()
    bit = place_bits()[axis]
    pixels = VOX * VOX
    seam = is_seam()
    sources = ((0, low), (1, mid_0), (2, mid_1), (3, high))
    for plane, ref in sources:
        flipped = ref[0].reshape(pixels, HALF).T
        for output_plane in range(2):
            tap = plane - output_plane
            if not 0 <= tap < 3:
                continue
            rows = slice(tap * HALF, (tap + 1) * HALF)
            columns = slice(output_plane * pixels, (output_plane + 1) * pixels)
            if plane in (1, 2) and tap != 1:
                turned[rows, columns] = jnp.where(seam, jnp.zeros_like(flipped), flipped)
            else:
                turned[rows, columns] = flipped
    for plane, ref in ((0, delta_0), (1, delta_1)):
        for c in range(3):
            moved[c, plane, 0] = jnp.zeros(moved.shape[3:], moved.dtype)
            moved[c, plane, VOX + 1] = jnp.zeros(moved.shape[3:], moved.dtype)
        moved[1, plane, 1 : VOX + 1] = ref[0]

        @pl.loop(0, VOX // TILE)
        def _(step):
            row = step * TILE
            values = ref[0, pl.ds(row, TILE)].reshape(TILE * VOX, FULL).astype(jnp.float32)
            column = lax.rem(lax.broadcasted_iota(jnp.int32, values.shape, 0), VOX)
            ahead = jnp.where(column < VOX - 1, pltpu.roll(values, TILE * VOX - 1, 0), 0.0)
            behind = jnp.where(column > 0, pltpu.roll(values, 1, 0), 0.0)
            moved[0, plane, pl.ds(row + 1, TILE)] = shaped(ahead.astype(jnp.bfloat16))
            moved[2, plane, pl.ds(row + 1, TILE)] = shaped(behind.astype(jnp.bfloat16))

    mine = lax.axis_index("chan") == core
    for b in range(3):

        @pl.loop(0, 3)
        def _(c):
            right = moved[c, :, 2 - b : 2 - b + VOX].reshape(2 * pixels, FULL)
            product = jnp.dot(turned[...], right, preferred_element_type=jnp.float32)
            kept = jnp.where(mine, product[:, :HALF], product[:, HALF:])
            sent = jnp.where(mine, product[:, HALF:], product[:, :HALF])
            for a in range(3):
                rows = slice(a * HALF, (a + 1) * HALF)
                tap = a * 9 + b * 3 + c
                keep[:, tap] = kept[rows].reshape(8, 16, HALF)
                blocks = sent[rows].reshape(2, 4, 16, HALF).astype(far.dtype)
                far[:, tap] = jnp.where(bit == 0, blocks[1], blocks[0])
                near[:, tap] = jnp.where(bit == 0, blocks[0], blocks[1])


def halve_core_kernel(axis, keep, far, near, kept, sent):
    bit = place_bits()[axis]
    for target, came, first in ((kept, near, bit * 4), (sent, far, (1 - bit) * 4)):

        @pl.loop(0, 4)
        def _(block):
            total = keep[first + block] + came[block].astype(jnp.float32)
            target[block] = total.astype(target.dtype)


def halve_kernel(axis, keep, came, kept, sent):
    bit = place_bits()[axis]
    half = keep.shape[0] // 2
    for target, first in ((kept, bit * half), (sent, (1 - bit) * half)):
        for block in range(half):
            total = keep[first + block] + came[first + block].astype(jnp.float32)
            target[block] = total.astype(target.dtype)


def finish_kernel(scale, keep, came, total):
    total[...] = ((keep[...] + came[...].astype(jnp.float32)) * scale).astype(total.dtype)


def join_kernel(axis, own, came, target):
    bit = place_bits()[axis]
    half = own.shape[0]
    target[pl.ds(bit * half, half)] = own[...]
    target[pl.ds((1 - bit) * half, half)] = came[...]


def join_core_kernel(order, own, came, grad):
    _, _, core = place()
    for at, block in enumerate(order):
        rows = slice(block * 16, block * 16 + 16)
        first = jnp.where(core == 0, own[at], came[at])
        second = jnp.where(core == 0, came[at], own[at])
        grad[:, rows, :HALF] = first.astype(jnp.float32)
        grad[:, rows, HALF:] = second.astype(jnp.float32)


WEIGHT = {"sum_two_core": 0, "first_rim": 3 * 10**9}


def hint(flops):
    return pl.CostEstimate(flops=flops, bytes_accessed=0, transcendentals=0)


def small_call(kernel, outs, operands, name):
    return pl.pallas_call(
        kernel,
        out_shape=[jax.ShapeDtypeStruct(shape, dtype) for shape, dtype in outs],
        in_specs=[pl.BlockSpec(memory_space=pltpu.VMEM)] * len(operands),
        out_specs=[pl.BlockSpec(memory_space=pltpu.VMEM)] * len(outs),
        compiler_params=pltpu.CompilerParams(vmem_limit_bytes=VMEM_LIMIT),
        cost_estimate=hint(WEIGHT.get(name, 3 * 10**9)),
        name=name,
    )(*operands)


PART = (27, 16, HALF)


def halve_core(axis, keep, far, near, name):
    outs = [((4,) + PART, jnp.float32), ((4,) + PART, jnp.bfloat16)]
    return small_call(functools.partial(halve_core_kernel, axis), outs, [keep, far, near], name)


def halve(axis, keep, came, name):
    shape = (keep.shape[0] // 2,) + PART
    outs = [(shape, jnp.float32), (shape, jnp.bfloat16)]
    return small_call(functools.partial(halve_kernel, axis), outs, [keep, came], name)


def finish(scale, keep, came, name):
    outs = [((1,) + PART, jnp.bfloat16)]
    return small_call(functools.partial(finish_kernel, scale), outs, [keep, came], name)[0]


def join(axis, own, came, name):
    outs = [((2 * own.shape[0],) + PART, jnp.bfloat16)]
    return small_call(functools.partial(join_kernel, axis), outs, [own, came], name)[0]


def join_core(order, own, came, name):
    outs = [((27, HALF, FULL), jnp.float32)]
    return small_call(functools.partial(join_core_kernel, order), outs, [own, came], name)[0]


def conv_call(name, part, kind, finish, outs, planes, pieces, begun=(), extra=(), flipped=False):
    lanes = planes[0].shape[3]
    height = {"own": HALF, "quarters": HALF, "both": FULL, "ready": pieces[0].shape[1]}[kind]
    ready = kind == "ready"
    if not ready:
        outs = outs + [((27, height, FULL), jnp.bfloat16)]
    operands = [*planes, *pieces, *begun, *extra]
    counts = (len(planes), len(pieces), len(begun), len(extra), len(outs))
    specs = [pl.BlockSpec(memory_space=pltpu.VMEM) for _ in operands]
    if not ready:
        for at in range(len(planes), len(planes) + len(pieces)):
            own = kind != "quarters" and at == len(planes)
            specs[at] = pl.BlockSpec(memory_space=pltpu.HBM if own else pl.ANY)
    scratch = [pltpu.VMEM((len(PARTS[part]["slots"]), VOX + 2, VOX, lanes), jnp.bfloat16)]
    if not ready:
        scratch.append(pltpu.SemaphoreType.DMA((20,)))
    return pl.pallas_call(
        functools.partial(conv_kernel, part, kind, flipped, finish, counts),
        out_shape=[jax.ShapeDtypeStruct(shape, dtype) for shape, dtype in outs],
        in_specs=specs,
        out_specs=[pl.BlockSpec(memory_space=pltpu.VMEM)] * len(outs),
        scratch_shapes=scratch,
        compiler_params=pltpu.CompilerParams(vmem_limit_bytes=VMEM_LIMIT),
        cost_estimate=hint(WEIGHT.get(name, 0)),
        name=name,
    )(*operands)


def filter_call(axis, planes, mid_at, deltas, name):
    narrow = (1, VOX, VOX, HALF)
    specs = [
        pl.BlockSpec(narrow, functools.partial(lambda at, i: (at, 0, 0, 0), at)) for at in mid_at
    ]
    specs += [pl.BlockSpec((1, VOX, VOX, FULL), lambda i: (0, 0, 0, 0))] * 2
    return pl.pallas_call(
        functools.partial(filter_kernel, axis),
        grid=(1,),
        out_shape=[
            jax.ShapeDtypeStruct((8, 27, 16, HALF), jnp.float32),
            jax.ShapeDtypeStruct((4, 27, 16, HALF), jnp.bfloat16),
            jax.ShapeDtypeStruct((4, 27, 16, HALF), jnp.bfloat16),
        ],
        in_specs=specs,
        out_specs=[
            pl.BlockSpec((size, 27, 16, HALF), lambda i: (0, 0, 0, 0)) for size in (8, 4, 4)
        ],
        scratch_shapes=[
            pltpu.VMEM((3 * HALF, 2 * VOX * VOX), jnp.bfloat16),
            pltpu.VMEM((3, 2, VOX + 2, VOX, FULL), jnp.bfloat16),
        ],
        compiler_params=pltpu.CompilerParams(vmem_limit_bytes=VMEM_LIMIT),
        cost_estimate=hint(0),
        name=name,
    )(*planes, *deltas)


def after(value, *earlier):
    return lax.optimization_barrier((value,) + earlier)[0]


def paired(volume, filter_one, filter_two, cotangent):
    count = lax.axis_size("dp")
    ahead = [(i, (i + 1) % count) for i in range(count)]
    behind = [(target, source) for source, target in ahead]
    scale = 1.0 / math.sqrt(count * 2 * VOX * VOX)
    one = filter_one.reshape(27, HALF, FULL)
    two = filter_two.reshape(27, HALF, FULL)
    level, side, core = place()

    def other(values):
        return lax.ppermute(values, "chan", [(0, 1), (1, 0)])

    def to_core(values):
        return lax.ppermute(values, "dp", [(i, i ^ 1) for i in range(count)])

    def to_side(values):
        return lax.ppermute(values, "dp", [(i, i ^ 2) for i in range(count)])

    def to_level(values):
        return lax.ppermute(values, "dp", [(i, i ^ 4) for i in range(count)])

    def to_far_level(values):
        return lax.ppermute(values, "dp", [(i, i ^ 8) for i in range(count)])

    def rims(first, last):
        return lax.ppermute(last, "dp", ahead), lax.ppermute(first, "dp", behind)

    wide = ((1, VOX, VOX, FULL), jnp.bfloat16)
    narrow = ((2, VOX, VOX, HALF), jnp.bfloat16)
    partial = ((2, VOX, VOX, FULL), jnp.float32)

    low_own, high_own = rims(volume[:1], volume[1:])
    one_0 = other(lax.dynamic_slice_in_dim(one, (2 * side + core) * 32, 32, axis=1))
    volume_other = other(after(volume, one_0, low_own, high_own))
    one_1 = to_side(one_0)
    one_2 = to_core(one_0)
    one_3 = to_core(one_1)
    quarters = [one_0, one_1, one_2, one_3]
    begun, own_ready = conv_call(
        "first_own", "all", "own", finish_partial, [partial],
        [after(low_own, volume_other), volume, high_own], [one],
    )
    two_0 = other(
        after(
            lax.dynamic_slice_in_dim(two, (2 * lax.rem(level, 2) + core) * 32, 32, axis=1),
            volume_other,
        )
    )
    low_other, high_other = rims(volume_other[:1], volume_other[1:])
    two_0 = after(two_0, begun)
    two_1 = to_level(two_0)
    two_2 = to_core(two_0)
    cot_other = other(after(cotangent, two_0))
    begun, ready = conv_call(
        "first_other", "local", "quarters", finish_partial, [partial], [volume_other], quarters,
        [after(begun, two_0)],
    )
    act_0, act_1 = conv_call(
        "first_rim", "rim", "ready", finish_first, [wide, wide], [low_other, high_other],
        [ready], [begun],
    )
    low_act, high_act = rims(act_0, act_1)
    two_3 = to_core(two_1)
    pieces = [two, two_0, two_1, two_2, two_3]
    begun, ready = conv_call(
        "second_local", "local", "both", finish_partial, [partial], [act_0, act_1], pieces
    )
    output, delta_0, delta_1 = conv_call(
        "second_rim", "rim", "ready", finish_second, [narrow, wide, wide], [low_act, high_act],
        [ready], [begun], [cotangent, cot_other],
    )
    low_delta, high_delta = rims(delta_0, delta_1)
    keep, far, near = filter_call(
        "z", [low_act, act_0, act_1, high_act], (0, 0, 0, 0), [delta_0, delta_1], "grad_two"
    )
    far, near = to_core(far), to_core(near)
    (begun,) = conv_call(
        "back_local", "local", "ready", finish_partial, [partial], [delta_0, delta_1], [ready],
        flipped=True,
    )
    keep_two, sent = halve_core(
        "z", after(keep, begun, low_delta, high_delta), far, near, "sum_two_core"
    )
    came_two = to_level(sent)
    prior_0, prior_1 = conv_call(
        "back_rim", "rim", "ready", finish_back, [wide, wide], [after(low_delta, keep_two), high_delta],
        [ready], [begun], [act_0, act_1], flipped=True,
    )
    keep, far, near = filter_call(
        "x", [low_own, volume, volume, high_own], (0, 0, 1, 0), [prior_0, prior_1], "grad_one"
    )
    far, near = to_core(far), to_core(near)
    keep_two, sent = halve("x", after(keep_two, keep), came_two, "sum_two_z")
    came_two = to_side(sent)
    keep_one, sent = halve_core("x", after(keep, keep_two), far, near, "sum_one_core")
    came_one = to_side(sent)
    keep_two, sent = halve("zz", after(keep_two, keep_one), came_two, "sum_two_x")
    came_two = to_far_level(sent)
    keep_one, sent = halve("z", after(keep_one, keep_two), came_one, "sum_one_x")
    came_one = to_level(sent)
    low_prior, high_prior = rims(after(prior_0, keep_one), after(prior_1, keep_one))
    own_two = finish(scale, after(keep_two, keep_one), came_two, "sum_two_zz")
    came_two = to_far_level(own_two)
    keep_one, sent = halve("zz", after(keep_one, own_two), came_one, "sum_one_z")
    came_one = to_far_level(sent)
    own_two = join("zz", after(own_two, keep_one), came_two, "join_two_zz")
    came_two = to_level(own_two)
    own_one = finish(scale, after(keep_one, own_two), came_one, "sum_one_zz")
    came_one = to_far_level(own_one)
    own_two = join("z", after(own_two, own_one), came_two, "join_two_z")
    came_two = to_side(own_two)
    own_one = join("zz", after(own_one, own_two, low_prior, high_prior), came_one, "join_one_zz")
    came_one = to_level(own_one)
    own_two = join("x", after(own_two, own_one), came_two, "join_two_x")
    came_two = to_core(own_two)
    own_one = join("z", after(own_one, own_two), came_one, "join_one_z")
    came_one = to_side(own_one)
    summed_two = join_core((0, 1, 4, 5, 2, 3, 6, 7), after(own_two, own_one), came_two, "grads_two")
    (input_grad,) = conv_call(
        "first_back", "all", "ready", finish_last, [narrow],
        [low_prior, after(prior_0, summed_two), prior_1, high_prior], [own_ready], flipped=True,
    )
    own_one = join("x", after(own_one, input_grad), came_one, "join_one_x")
    summed_one = join_core(tuple(range(8)), own_one, to_core(own_one), "grads_one")
    shape = filter_one.shape
    return output, input_grad, summed_one.reshape(shape), summed_two.reshape(shape)


def local(volume, filter_one, filter_two, cotangent):
    pair = lax.axis_size("chan") == 2 and lax.axis_size("dp") == 16
    if pair and volume.shape == (2, VOX, VOX, HALF):
        return paired(volume, filter_one, filter_two, cotangent)
    return plain(volume, filter_one, filter_two, cotangent)


def solution(mesh):
    in_specs = (
        P("dp", None, None, "chan"),
        P(None, None, None, "chan", None),
        P(None, None, None, "chan", None),
        P("dp", None, None, "chan"),
    )
    out_specs = (
        P("dp", None, None, "chan"),
        P("dp", None, None, "chan"),
        P(None, None, None, "chan", None),
        P(None, None, None, "chan", None),
    )
    return jax.shard_map(local, mesh=mesh, in_specs=in_specs, out_specs=out_specs, check_vma=False)
```

```python
import functools
import math

import jax
import jax.numpy as jnp
from jax import lax
from jax.experimental import pallas as pl
from jax.experimental.pallas import tpu as pltpu
from jax.sharding import PartitionSpec as P

VOX = 32
SLOPE = 0.3
HALF = 128
FULL = 256
TILE = 16
SMALL = 10**9
VMEM_LIMIT = 32 * 1024 * 1024


def extended(block, sides, width):
    for axis, dim in sides:
        count = lax.axis_size(axis)
        forward = [(i, i + 1) for i in range(count - 1)]
        forward.append((count - 1, 0))
        backward = [(target, source) for source, target in forward]
        low = lax.ppermute(
            lax.slice_in_dim(block, block.shape[dim] - width, None, axis=dim), axis, forward
        )
        high = lax.ppermute(lax.slice_in_dim(block, 0, width, axis=dim), axis, backward)
        block = jnp.concatenate([low, block, high], axis=dim)
    return block


def leaky(values):
    return jnp.where(values > 0, values, SLOPE * values)


def slope_of(values):
    return jnp.where(values > 0, jnp.float32(1.0), jnp.float32(SLOPE))


def tap_mask(rows, offset):
    base = lax.axis_index("dp") * rows
    total_rows = lax.axis_size("dp") * rows
    planes = jnp.mod(base + jnp.arange(rows, dtype=jnp.int32) - 1, total_rows)
    depth = jnp.mod(planes, VOX) + offset
    inside = jnp.logical_and(depth >= 0, depth < VOX)
    return inside[:, None, None, None]


def pad_plane(values):
    return jnp.pad(values, ((0, 0), (1, 1), (1, 1), (0, 0)))


def columns(plane, rows, height, breadth):
    taps = []
    for a in range(3):
        inside = tap_mask(rows, a - 1)
        depth_slab = plane[a : a + rows]
        depth_slab = jnp.where(inside, depth_slab, jnp.zeros_like(depth_slab))
        for b in range(3):
            for c in range(3):
                taps.append(depth_slab[:, b : b + height, c : c + breadth, :])
    stacked = jnp.concatenate(taps, axis=-1)
    return stacked.reshape(rows * height * breadth, stacked.shape[-1])


def plain(volume, filter_one, filter_two, cotangent):
    rows, height, breadth, narrow = volume.shape
    full = filter_one.shape[4]
    voxels = rows * height * breadth
    scale = 1.0 / math.sqrt(lax.axis_size("dp") * voxels)

    def forward(activity, weight):
        rim = extended(activity, (("dp", 0),), 1)
        plane = pad_plane(rim)
        stacked = columns(plane, rows, height, breadth)
        partial_value = jnp.dot(
            stacked, weight.reshape(27 * narrow, full), preferred_element_type=jnp.float32
        )
        summed = lax.psum_scatter(partial_value, "chan", scatter_dimension=1, tiled=True)
        return (plane, summed)

    def backward(plane, delta, weight):
        wide = lax.all_gather(delta, "chan", axis=3, tiled=True)
        rim = extended(wide, (("dp", 0),), 1)
        centre = rim[1 : rows + 1].reshape(voxels, full)
        stacked = columns(plane, rows, height, breadth)
        weight_grad = lax.dot_general(
            stacked, centre, (((0,), (0,)), ((), ())), preferred_element_type=jnp.float32
        )
        weight_grad = weight_grad.reshape(3, 3, 3, narrow, full)
        source = pad_plane(rim)
        total = jnp.zeros((rows, height, breadth, narrow), jnp.float32)
        for a in range(3):
            depth_slab = source[2 - a : 2 - a + rows]
            flat = depth_slab.reshape(-1, full)
            product = lax.dot_general(
                flat,
                weight[a].reshape(9 * narrow, full),
                (((1,), (1,)), ((), ())),
                preferred_element_type=jnp.float32,
            )
            product = product.reshape(rows, height + 2, breadth + 2, 9, narrow)
            part = jnp.zeros((rows, height, breadth, narrow), jnp.float32)
            for b in range(3):
                for c in range(3):
                    part = (
                        part
                        + product[:, 2 - b : 2 - b + height, 2 - c : 2 - c + breadth, b * 3 + c, :]
                    )
            inside = tap_mask(rows, 1 - a)
            total = total + jnp.where(inside, part, jnp.zeros_like(part))
        return (weight_grad, total.reshape(voxels, narrow))

    def layer_sum(weight_grad):
        return lax.psum(weight_grad, "dp")

    plane_one, pre_one = forward(volume, filter_one)
    act_one = leaky(pre_one).astype(jnp.bfloat16).reshape(rows, height, breadth, narrow)
    plane_two, pre_two = forward(act_one, filter_two)
    output = leaky(pre_two).astype(jnp.bfloat16).reshape(rows, height, breadth, narrow)
    delta_two = (cotangent.reshape(voxels, narrow).astype(jnp.float32) * slope_of(pre_two)).astype(
        jnp.bfloat16
    )
    local_two, back_two = backward(
        plane_two, delta_two.reshape(rows, height, breadth, narrow), filter_two
    )
    summed_two = layer_sum(local_two)
    delta_one = (back_two * slope_of(pre_one)).astype(jnp.bfloat16)
    local_one, back_one = backward(
        plane_one, delta_one.reshape(rows, height, breadth, narrow), filter_one
    )
    summed_one = layer_sum(local_one)
    input_grad = back_one.astype(jnp.bfloat16).reshape(rows, height, breadth, narrow)
    return (output, input_grad, summed_one * scale, summed_two * scale)


def is_seam():
    return lax.rem(lax.axis_index("dp") * 2, VOX) == 0


def place():
    at = lax.axis_index("dp")
    return at // 4, lax.rem(at // 2, 2), lax.rem(at, 2)


def place_bits():
    level, side, _ = place()
    return {"x": side, "z": lax.rem(level, 2), "zz": level // 2}


def shaped(values):
    return values.reshape(TILE, VOX, values.shape[1])


PARTS = {
    "all": dict(
        slots=((0, True), (1, True), (2, False), (1, False), (2, True), (3, True)),
        taps=(((0, 0), (1, 1), (2, 2)), ((0, 3), (1, 4), (2, 5))),
    ),
    "local": dict(
        slots=((0, True), (1, True), (0, False), (1, False)),
        taps=(((1, 0), (2, 3)), ((0, 2), (1, 1))),
    ),
    "rim": dict(
        slots=((0, True), (1, True)),
        taps=(((0, 0),), ((2, 1),)),
    ),
}


def filter_rows(kind):
    level, side, core = place()
    along, first = (side, 0) if kind == "quarters" else (lax.rem(level, 2), HALF)
    rows = [] if kind == "quarters" else [(HALF, 0)]
    if kind != "own":
        for unit in (core, 1 - core):
            rows += [(32, first + (2 * at + unit) * 32) for at in (along, 1 - along)]
    return rows


def copy_weights(kind, part, pieces, store, sems):
    me = lax.axis_index("chan")
    copies = []
    for (height, row), piece in zip(filter_rows(kind), pieces):
        if not isinstance(row, int):
            row = pl.multiple_of(row, 32)
        spans = ((0, 27),) if part != "rim" else ((0, 9), (18, 9))
        for side in range(2):
            column = pl.multiple_of((me if side == 0 else 1 - me) * HALF, HALF)
            for first, length in spans:
                taps = pl.ds(first, length)
                copies.append(
                    pltpu.make_async_copy(
                        piece.at[taps, :, pl.ds(column, HALF)],
                        store.at[taps, pl.ds(row, height), pl.ds(side * HALF, HALF)],
                        sems.at[len(copies)],
                    )
                )
    for copy in copies:
        copy.start()
    return copies


def fill_planes(part, planes, store):
    edge = jnp.zeros(store.shape[2:], store.dtype)
    seam = is_seam()
    for slot, (plane, always) in enumerate(PARTS[part]["slots"]):
        ref, at = planes[plane]
        store[slot, 0] = edge
        store[slot, VOX + 1] = edge
        if always:
            store[slot, 1 : VOX + 1] = ref[at]
            continue

        @pl.when(seam)
        def _():
            store[slot] = jnp.zeros(store.shape[1:], store.dtype)

        @pl.when(jnp.logical_not(seam))
        def _():
            store[slot, 1 : VOX + 1] = ref[at]


def conv_rows(store, weights, taps, row, flipped):
    pieces = []
    for _, slot in taps:
        for b in range(3):
            piece = store[slot, pl.ds(row + b, TILE)]
            pieces.append(piece.reshape(TILE * VOX, store.shape[3]))
    stacked = jnp.concatenate(pieces, axis=1)
    products = []
    for c in range(3):
        if flipped:
            tiles = [weights[(2 - a) * 9 + (2 - b) * 3 + 2 - c] for a, _ in taps for b in range(3)]
            dims = (((1,), (1,)), ((), ()))
            tiles = jnp.concatenate(tiles, axis=1)
        else:
            tiles = [weights[a * 9 + b * 3 + c] for a, _ in taps for b in range(3)]
            dims = (((1,), (0,)), ((), ()))
            tiles = jnp.concatenate(tiles, axis=0)
        products.append(
            lax.dot_general(stacked, tiles, dims, preferred_element_type=jnp.float32)
        )
    left, middle, right = products
    column = lax.rem(lax.broadcasted_iota(jnp.int32, left.shape, 0), VOX)
    left = jnp.where(column > 0, pltpu.roll(left, 1, 0), 0.0)
    right = jnp.where(column < VOX - 1, pltpu.roll(right, TILE * VOX - 1, 0), 0.0)
    return middle + left + right


def conv_kernel(part, kind, flipped, finish, counts, *refs):
    refs = list(refs)
    groups = []
    for count in counts:
        groups.append(refs[:count])
        refs = refs[count:]
    planes, pieces, begun, extra, outs = groups
    if kind == "ready":
        (weights,), copies = pieces, []
        (store,) = refs
    else:
        store, sems = refs
        weights = outs.pop()
        copies = copy_weights(kind, part, pieces, weights, sems)
    views = []
    for ref in planes:
        views += [(ref, at) for at in range(ref.shape[0])]
    fill_planes(part, views, store)
    for copy in copies:
        copy.wait()
    for plane in range(2):
        taps = PARTS[part]["taps"][plane]

        @pl.loop(0, VOX // TILE)
        def _(step):
            rows = pl.ds(pl.multiple_of(step * TILE, TILE), TILE)
            value = shaped(conv_rows(store, weights, taps, step * TILE, flipped))
            if begun:
                value = value + begun[0][plane, rows]
            finish(value, plane, rows, extra, outs)


def finish_partial(value, plane, rows, extra, outs):
    outs[0][plane, rows] = value


def finish_first(value, plane, rows, extra, outs):
    outs[plane][0, rows] = leaky(value).astype(jnp.bfloat16)


def finish_second(value, plane, rows, extra, outs):
    output, deltas = outs[0], outs[1:]
    output[plane, rows] = leaky(value[:, :, :HALF]).astype(jnp.bfloat16)
    slope = slope_of(value)
    for lane, cot in ((0, extra[0]), (HALF, extra[1])):
        delta = cot[plane, rows].astype(jnp.float32) * slope[:, :, lane : lane + HALF]
        deltas[plane][0, rows, :, lane : lane + HALF] = delta.astype(jnp.bfloat16)


def finish_back(value, plane, rows, extra, outs):
    act = extra[plane][0, rows].astype(jnp.float32)
    outs[plane][0, rows] = (value * slope_of(act)).astype(jnp.bfloat16)


def finish_last(value, plane, rows, extra, outs):
    outs[0][plane, rows] = value.astype(jnp.bfloat16)


def filter_kernel(colours, *refs):
    low, mid_0, mid_1, high, delta_0, delta_1 = refs[:6]
    outs, (turned, moved) = refs[6:-2], refs[-2:]
    _, _, core = place()
    bits = place_bits()
    pixels = VOX * VOX
    seam = is_seam()
    sources = ((0, low), (1, mid_0), (2, mid_1), (3, high))
    for plane, ref in sources:
        flipped = ref[0].reshape(pixels, HALF).T
        for output_plane in range(2):
            tap = plane - output_plane
            if not 0 <= tap < 3:
                continue
            rows = slice(tap * HALF, (tap + 1) * HALF)
            columns = slice(output_plane * pixels, (output_plane + 1) * pixels)
            if plane in (1, 2) and tap != 1:
                turned[rows, columns] = jnp.where(seam, jnp.zeros_like(flipped), flipped)
            else:
                turned[rows, columns] = flipped
    for plane, ref in ((0, delta_0), (1, delta_1)):
        for c in range(3):
            moved[c, plane, 0] = jnp.zeros(moved.shape[3:], moved.dtype)
            moved[c, plane, VOX + 1] = jnp.zeros(moved.shape[3:], moved.dtype)
        moved[1, plane, 1 : VOX + 1] = ref[0]

        @pl.loop(0, VOX // TILE)
        def _(step):
            row = step * TILE
            values = ref[0, pl.ds(row, TILE)].reshape(TILE * VOX, FULL).astype(jnp.float32)
            column = lax.rem(lax.broadcasted_iota(jnp.int32, values.shape, 0), VOX)
            ahead = jnp.where(column < VOX - 1, pltpu.roll(values, TILE * VOX - 1, 0), 0.0)
            behind = jnp.where(column > 0, pltpu.roll(values, 1, 0), 0.0)
            moved[0, plane, pl.ds(row + 1, TILE)] = shaped(ahead.astype(jnp.bfloat16))
            moved[2, plane, pl.ds(row + 1, TILE)] = shaped(behind.astype(jnp.bfloat16))

    mine = lax.axis_index("chan") == core
    for tap in range(27):
        a, b, c = tap // 9, tap // 3 % 3, tap % 3
        if a:
            continue
        right = moved[c, :, 2 - b : 2 - b + VOX].reshape(2 * pixels, FULL)
        product = jnp.dot(turned[...], right, preferred_element_type=jnp.float32)
        kept = jnp.where(mine, product[:, :HALF], product[:, HALF:])
        sent = jnp.where(mine, product[:, HALF:], product[:, :HALF])
        for a in range(3):
            rows = slice(a * HALF, (a + 1) * HALF)
            for at, (first, taps, axis) in enumerate(colours):
                place_at = a * 9 + b * 3 + c - first
                if not 0 <= place_at < taps:
                    continue
                keep, far, near = outs[3 * at : 3 * at + 3]
                bit = bits[axis]
                keep[:, place_at] = kept[rows].reshape(8, 16, HALF)
                blocks = sent[rows].reshape(2, 4, 16, HALF).astype(far.dtype)
                far[:, place_at] = jnp.where(bit == 0, blocks[1], blocks[0])
                near[:, place_at] = jnp.where(bit == 0, blocks[0], blocks[1])


def halve_core_kernel(axis, keep, far, near, kept, sent):
    bit = place_bits()[axis]
    for target, came, first in ((kept, near, bit * 4), (sent, far, (1 - bit) * 4)):

        @pl.loop(0, 4)
        def _(block):
            total = keep[first + block] + came[block].astype(jnp.float32)
            target[block] = total.astype(target.dtype)


def halve_kernel(axis, keep, came, kept, sent):
    bit = place_bits()[axis]
    half = keep.shape[0] // 2
    for target, first in ((kept, bit * half), (sent, (1 - bit) * half)):
        for block in range(half):
            total = keep[first + block] + came[first + block].astype(jnp.float32)
            target[block] = total.astype(target.dtype)


def finish_kernel(scale, keep, came, total):
    total[...] = ((keep[...] + came[...].astype(jnp.float32)) * scale).astype(total.dtype)


def join_kernel(axis, own, came, target):
    bit = place_bits()[axis]
    half = own.shape[0]
    target[pl.ds(bit * half, half)] = own[...]
    target[pl.ds((1 - bit) * half, half)] = came[...]


def join_core_kernel(order, *refs):
    _, _, core = place()
    grad = refs[-1]
    first_tap = 0
    for own, came in zip(refs[0:-1:2], refs[1:-1:2]):
        taps = slice(first_tap, first_tap + own.shape[1])
        first_tap += own.shape[1]
        for at, block in enumerate(order):
            rows = slice(block * 16, block * 16 + 16)
            first = jnp.where(core == 0, own[at], came[at])
            second = jnp.where(core == 0, came[at], own[at])
            grad[taps, rows, :HALF] = first.astype(jnp.float32)
            grad[taps, rows, HALF:] = second.astype(jnp.float32)


WEIGHT = {
    "sum_two_core": 0,
    "first_rim": 3 * 10**9,
    "join_a_zz": 4 * 10**9,
    "join_b_zz": 4 * 10**9,
    "join_a_z": 6 * 10**9,
    "join_b_x": 6 * 10**9,
}


def hint(flops):
    return pl.CostEstimate(flops=flops, bytes_accessed=0, transcendentals=0)


def small_call(kernel, outs, operands, name):
    return pl.pallas_call(
        kernel,
        out_shape=[jax.ShapeDtypeStruct(shape, dtype) for shape, dtype in outs],
        in_specs=[pl.BlockSpec(memory_space=pltpu.VMEM)] * len(operands),
        out_specs=[pl.BlockSpec(memory_space=pltpu.VMEM)] * len(outs),
        compiler_params=pltpu.CompilerParams(vmem_limit_bytes=VMEM_LIMIT),
        cost_estimate=hint(WEIGHT.get(name, SMALL)),
        name=name,
    )(*operands)


def halve_core(axis, keep, far, near, name):
    outs = [(far.shape, jnp.float32), (far.shape, jnp.bfloat16)]
    return small_call(functools.partial(halve_core_kernel, axis), outs, [keep, far, near], name)


def halve(axis, keep, came, name):
    shape = (keep.shape[0] // 2,) + keep.shape[1:]
    outs = [(shape, jnp.float32), (shape, jnp.bfloat16)]
    return small_call(functools.partial(halve_kernel, axis), outs, [keep, came], name)


def finish(scale, keep, came, name):
    outs = [(keep.shape, jnp.bfloat16)]
    return small_call(functools.partial(finish_kernel, scale), outs, [keep, came], name)[0]


def join(axis, own, came, name):
    outs = [((2 * own.shape[0],) + own.shape[1:], jnp.bfloat16)]
    return small_call(functools.partial(join_kernel, axis), outs, [own, came], name)[0]


def join_core(order, colours, name):
    outs = [((27, HALF, FULL), jnp.float32)]
    operands = [half for pair in colours for half in pair]
    return small_call(functools.partial(join_core_kernel, order), outs, operands, name)[0]


def conv_call(name, part, kind, finish, outs, planes, pieces, begun=(), extra=(), flipped=False):
    lanes = planes[0].shape[3]
    height = {"own": HALF, "quarters": HALF, "both": FULL, "ready": pieces[0].shape[1]}[kind]
    ready = kind == "ready"
    if not ready:
        outs = outs + [((27, height, FULL), jnp.bfloat16)]
    operands = [*planes, *pieces, *begun, *extra]
    counts = (len(planes), len(pieces), len(begun), len(extra), len(outs))
    specs = [pl.BlockSpec(memory_space=pltpu.VMEM) for _ in operands]
    if not ready:
        for at in range(len(planes), len(planes) + len(pieces)):
            own = kind != "quarters" and at == len(planes)
            specs[at] = pl.BlockSpec(memory_space=pltpu.HBM if own else pl.ANY)
    scratch = [pltpu.VMEM((len(PARTS[part]["slots"]), VOX + 2, VOX, lanes), jnp.bfloat16)]
    if not ready:
        scratch.append(pltpu.SemaphoreType.DMA((20,)))
    return pl.pallas_call(
        functools.partial(conv_kernel, part, kind, flipped, finish, counts),
        out_shape=[jax.ShapeDtypeStruct(shape, dtype) for shape, dtype in outs],
        in_specs=specs,
        out_specs=[pl.BlockSpec(memory_space=pltpu.VMEM)] * len(outs),
        scratch_shapes=scratch,
        compiler_params=pltpu.CompilerParams(vmem_limit_bytes=VMEM_LIMIT),
        cost_estimate=hint(WEIGHT.get(name, 0)),
        name=name,
    )(*operands)


def filter_call(colours, planes, mid_at, deltas, name):
    narrow = (1, VOX, VOX, HALF)
    specs = [
        pl.BlockSpec(narrow, functools.partial(lambda at, i: (at, 0, 0, 0), at)) for at in mid_at
    ]
    specs += [pl.BlockSpec((1, VOX, VOX, FULL), lambda i: (0, 0, 0, 0))] * 2
    outs = []
    for _, taps, _ in colours:
        for blocks, dtype in ((8, jnp.float32), (4, jnp.bfloat16), (4, jnp.bfloat16)):
            outs.append(jax.ShapeDtypeStruct((blocks, taps, 16, HALF), dtype))
    values = pl.pallas_call(
        functools.partial(filter_kernel, colours),
        grid=(1,),
        out_shape=outs,
        in_specs=specs,
        out_specs=[pl.BlockSpec(out.shape, lambda i: (0, 0, 0, 0)) for out in outs],
        scratch_shapes=[
            pltpu.VMEM((3 * HALF, 2 * VOX * VOX), jnp.bfloat16),
            pltpu.VMEM((3, 2, VOX + 2, VOX, FULL), jnp.bfloat16),
        ],
        compiler_params=pltpu.CompilerParams(vmem_limit_bytes=VMEM_LIMIT),
        cost_estimate=hint(0),
        name=name,
    )(*planes, *deltas)
    return [values[at : at + 3] for at in range(0, len(values), 3)]


def after(value, *earlier):
    return lax.optimization_barrier((value,) + earlier)[0]


def paired(volume, filter_one, filter_two, cotangent):
    count = lax.axis_size("dp")
    ahead = [(i, (i + 1) % count) for i in range(count)]
    behind = [(target, source) for source, target in ahead]
    scale = 1.0 / math.sqrt(count * 2 * VOX * VOX)
    one = filter_one.reshape(27, HALF, FULL)
    two = filter_two.reshape(27, HALF, FULL)
    level, side, core = place()

    def other(values):
        return lax.ppermute(values, "chan", [(0, 1), (1, 0)])

    def to_core(values):
        return lax.ppermute(values, "dp", [(i, i ^ 1) for i in range(count)])

    def to_side(values):
        return lax.ppermute(values, "dp", [(i, i ^ 2) for i in range(count)])

    def to_level(values):
        return lax.ppermute(values, "dp", [(i, i ^ 4) for i in range(count)])

    def to_far_level(values):
        return lax.ppermute(values, "dp", [(i, i ^ 8) for i in range(count)])

    def rims(first, last):
        return lax.ppermute(last, "dp", ahead), lax.ppermute(first, "dp", behind)

    wide = ((1, VOX, VOX, FULL), jnp.bfloat16)
    narrow = ((2, VOX, VOX, HALF), jnp.bfloat16)
    partial = ((2, VOX, VOX, FULL), jnp.float32)
    half_partial = ((2, VOX, VOX, HALF), jnp.float32)

    low_own, high_own = rims(volume[:1], volume[1:])
    one_0 = other(lax.dynamic_slice_in_dim(one, (2 * side + core) * 32, 32, axis=1))
    volume_other = other(after(volume, one_0, low_own, high_own))
    one_1 = to_side(one_0)
    one_2 = to_core(one_0)
    one_3 = to_core(one_1)
    quarters = [one_0, one_1, one_2, one_3]
    begun, own_ready = conv_call(
        "first_own", "all", "own", finish_partial, [partial],
        [after(low_own, volume_other), volume, high_own], [one],
    )
    two_0 = other(
        after(
            lax.dynamic_slice_in_dim(two, (2 * lax.rem(level, 2) + core) * 32, 32, axis=1),
            volume_other,
        )
    )
    low_other, high_other = rims(volume_other[:1], volume_other[1:])
    two_0 = after(two_0, begun)
    two_1 = to_level(two_0)
    two_2 = to_core(two_0)
    cot_other = other(after(cotangent, two_0))
    begun, ready = conv_call(
        "first_other", "local", "quarters", finish_partial, [partial], [volume_other], quarters,
        [after(begun, two_0)],
    )
    act_0, act_1 = conv_call(
        "first_rim", "rim", "ready", finish_first, [wide, wide], [low_other, high_other],
        [ready], [begun],
    )
    low_act, high_act = rims(act_0, act_1)
    two_3 = to_core(two_1)
    pieces = [two, two_0, two_1, two_2, two_3]
    begun, ready = conv_call(
        "second_local", "local", "both", finish_partial, [partial], [act_0, after(act_1, cot_other)],
        pieces,
    )
    output, delta_0, delta_1 = conv_call(
        "second_rim", "rim", "ready", finish_second, [narrow, wide, wide], [low_act, high_act],
        [ready], [begun], [cotangent, cot_other],
    )
    low_delta, high_delta = rims(delta_0, delta_1)
    ((keep, far, near),) = filter_call(
        ((0, 27, "z"),), [low_act, act_0, act_1, high_act], (0, 0, 0, 0), [delta_0, delta_1],
        "grad_two",
    )
    far, near = to_core(far), to_core(near)
    (begun,) = conv_call(
        "back_local", "local", "ready", finish_partial, [partial], [delta_0, delta_1], [ready],
        flipped=True,
    )
    keep_two, sent = halve_core(
        "z", after(keep, begun, low_delta, high_delta), far, near, "sum_two_core"
    )
    came_two = to_level(sent)
    prior_0, prior_1 = conv_call(
        "back_rim", "rim", "ready", finish_back, [wide, wide], [after(low_delta, keep_two), high_delta],
        [ready], [begun], [act_0, act_1], flipped=True,
    )
    (keep_a, *sent_a), (keep_b, *sent_b) = filter_call(
        ((0, 14, "x"), (14, 13, "z")), [low_own, volume, volume, high_own], (0, 0, 1, 0),
        [prior_0, prior_1], "grad_one",
    )
    sent_a, sent_b = [to_core(half) for half in sent_a], [to_core(half) for half in sent_b]
    keep_two, sent = halve("x", after(keep_two, keep_a), came_two, "sum_two_z")
    came_two = to_side(sent)
    keep_a, sent = halve_core("x", after(keep_a, keep_two), *sent_a, "sum_a_core")
    came_a = to_side(sent)
    keep_b, sent = halve_core("z", after(keep_b, keep_a), *sent_b, "sum_b_core")
    came_b = to_level(sent)
    (begun,) = conv_call(
        "first_back_local", "local", "ready", finish_partial, [half_partial],
        [after(prior_0, keep_b), prior_1], [own_ready], flipped=True,
    )
    keep_two, sent = halve("zz", after(keep_two, begun), came_two, "sum_two_x")
    came_two = to_far_level(sent)
    keep_a, sent = halve("z", after(keep_a, keep_two), came_a, "sum_a_x")
    came_a = to_level(sent)
    keep_b, sent = halve("x", after(keep_b, keep_a), came_b, "sum_b_z")
    came_b = to_side(sent)
    low_prior, high_prior = rims(after(prior_0, keep_b), after(prior_1, keep_b))
    own_two = finish(scale, after(keep_two, keep_b), came_two, "sum_two_zz")
    came_two = to_far_level(own_two)
    keep_a, sent = halve("zz", after(keep_a, own_two), came_a, "sum_a_z")
    came_a = to_far_level(sent)
    keep_b, sent = halve("zz", after(keep_b, keep_a), came_b, "sum_b_x")
    came_b = to_far_level(sent)
    own_two = join("zz", after(own_two, keep_b), came_two, "join_two_zz")
    came_two = to_level(own_two)
    own_a = finish(scale, after(keep_a, own_two), came_a, "sum_a_zz")
    came_a = to_far_level(own_a)
    own_b = finish(scale, after(keep_b, own_a), came_b, "sum_b_zz")
    came_b = to_far_level(own_b)
    own_two = join("z", after(own_two, own_b), came_two, "join_two_z")
    came_two = to_side(own_two)
    own_a = join("zz", after(own_a, own_two, low_prior, high_prior), came_a, "join_a_zz")
    came_a = to_level(own_a)
    own_b = join("zz", after(own_b, own_a), came_b, "join_b_zz")
    came_b = to_side(own_b)
    own_two = join("x", after(own_two, own_b), came_two, "join_two_x")
    came_two = to_core(own_two)
    own_a = join("z", after(own_a, own_two), came_a, "join_a_z")
    came_a = to_side(own_a)
    own_b = join("x", after(own_b, own_a), came_b, "join_b_x")
    came_b = to_level(own_b)
    (input_grad,) = conv_call(
        "first_back_rim", "rim", "ready", finish_last, [narrow],
        [after(low_prior, own_b), high_prior], [own_ready], [begun], flipped=True,
    )
    summed_two = join_core(
        (0, 1, 4, 5, 2, 3, 6, 7), [(after(own_two, input_grad), came_two)], "grads_two"
    )
    own_a = join("x", after(own_a, summed_two), came_a, "join_a_x")
    came_a = to_core(own_a)
    own_b = join("z", after(own_b, own_a), came_b, "join_b_z")
    came_b = to_core(own_b)
    summed_one = join_core(tuple(range(8)), [(own_a, came_a), (own_b, came_b)], "grads_one")
    shape = filter_one.shape
    return output, input_grad, summed_one.reshape(shape), summed_two.reshape(shape)


def local(volume, filter_one, filter_two, cotangent):
    pair = lax.axis_size("chan") == 2 and lax.axis_size("dp") == 16
    if pair and volume.shape == (2, VOX, VOX, HALF):
        return paired(volume, filter_one, filter_two, cotangent)
    return plain(volume, filter_one, filter_two, cotangent)


def solution(mesh):
    in_specs = (
        P("dp", None, None, "chan"),
        P(None, None, None, "chan", None),
        P(None, None, None, "chan", None),
        P("dp", None, None, "chan"),
    )
    out_specs = (
        P("dp", None, None, "chan"),
        P("dp", None, None, "chan"),
        P(None, None, None, "chan", None),
        P(None, None, None, "chan", None),
    )
    return jax.shard_map(local, mesh=mesh, in_specs=in_specs, out_specs=out_specs, check_vma=False)
```

```python
import functools
import math

import jax
import jax.numpy as jnp
from jax import lax
from jax.experimental import pallas as pl
from jax.experimental.pallas import tpu as pltpu
from jax.sharding import PartitionSpec as P

VOX = 32
SLOPE = 0.3
HALF = 128
FULL = 256
TILE = 16
SMALL = 10**9
VMEM_LIMIT = 32 * 1024 * 1024


def extended(block, sides, width):
    for axis, dim in sides:
        count = lax.axis_size(axis)
        forward = [(i, i + 1) for i in range(count - 1)]
        forward.append((count - 1, 0))
        backward = [(target, source) for source, target in forward]
        low = lax.ppermute(
            lax.slice_in_dim(block, block.shape[dim] - width, None, axis=dim), axis, forward
        )
        high = lax.ppermute(lax.slice_in_dim(block, 0, width, axis=dim), axis, backward)
        block = jnp.concatenate([low, block, high], axis=dim)
    return block


def leaky(values):
    return jnp.where(values > 0, values, SLOPE * values)


def slope_of(values):
    return jnp.where(values > 0, jnp.float32(1.0), jnp.float32(SLOPE))


def tap_mask(rows, offset):
    base = lax.axis_index("dp") * rows
    total_rows = lax.axis_size("dp") * rows
    planes = jnp.mod(base + jnp.arange(rows, dtype=jnp.int32) - 1, total_rows)
    depth = jnp.mod(planes, VOX) + offset
    inside = jnp.logical_and(depth >= 0, depth < VOX)
    return inside[:, None, None, None]


def pad_plane(values):
    return jnp.pad(values, ((0, 0), (1, 1), (1, 1), (0, 0)))


def columns(plane, rows, height, breadth):
    taps = []
    for a in range(3):
        inside = tap_mask(rows, a - 1)
        depth_slab = plane[a : a + rows]
        depth_slab = jnp.where(inside, depth_slab, jnp.zeros_like(depth_slab))
        for b in range(3):
            for c in range(3):
                taps.append(depth_slab[:, b : b + height, c : c + breadth, :])
    stacked = jnp.concatenate(taps, axis=-1)
    return stacked.reshape(rows * height * breadth, stacked.shape[-1])


def plain(volume, filter_one, filter_two, cotangent):
    rows, height, breadth, narrow = volume.shape
    full = filter_one.shape[4]
    voxels = rows * height * breadth
    scale = 1.0 / math.sqrt(lax.axis_size("dp") * voxels)

    def forward(activity, weight):
        rim = extended(activity, (("dp", 0),), 1)
        plane = pad_plane(rim)
        stacked = columns(plane, rows, height, breadth)
        partial_value = jnp.dot(
            stacked, weight.reshape(27 * narrow, full), preferred_element_type=jnp.float32
        )
        summed = lax.psum_scatter(partial_value, "chan", scatter_dimension=1, tiled=True)
        return (plane, summed)

    def backward(plane, delta, weight):
        wide = lax.all_gather(delta, "chan", axis=3, tiled=True)
        rim = extended(wide, (("dp", 0),), 1)
        centre = rim[1 : rows + 1].reshape(voxels, full)
        stacked = columns(plane, rows, height, breadth)
        weight_grad = lax.dot_general(
            stacked, centre, (((0,), (0,)), ((), ())), preferred_element_type=jnp.float32
        )
        weight_grad = weight_grad.reshape(3, 3, 3, narrow, full)
        source = pad_plane(rim)
        total = jnp.zeros((rows, height, breadth, narrow), jnp.float32)
        for a in range(3):
            depth_slab = source[2 - a : 2 - a + rows]
            flat = depth_slab.reshape(-1, full)
            product = lax.dot_general(
                flat,
                weight[a].reshape(9 * narrow, full),
                (((1,), (1,)), ((), ())),
                preferred_element_type=jnp.float32,
            )
            product = product.reshape(rows, height + 2, breadth + 2, 9, narrow)
            part = jnp.zeros((rows, height, breadth, narrow), jnp.float32)
            for b in range(3):
                for c in range(3):
                    part = (
                        part
                        + product[:, 2 - b : 2 - b + height, 2 - c : 2 - c + breadth, b * 3 + c, :]
                    )
            inside = tap_mask(rows, 1 - a)
            total = total + jnp.where(inside, part, jnp.zeros_like(part))
        return (weight_grad, total.reshape(voxels, narrow))

    def layer_sum(weight_grad):
        return lax.psum(weight_grad, "dp")

    plane_one, pre_one = forward(volume, filter_one)
    act_one = leaky(pre_one).astype(jnp.bfloat16).reshape(rows, height, breadth, narrow)
    plane_two, pre_two = forward(act_one, filter_two)
    output = leaky(pre_two).astype(jnp.bfloat16).reshape(rows, height, breadth, narrow)
    delta_two = (cotangent.reshape(voxels, narrow).astype(jnp.float32) * slope_of(pre_two)).astype(
        jnp.bfloat16
    )
    local_two, back_two = backward(
        plane_two, delta_two.reshape(rows, height, breadth, narrow), filter_two
    )
    summed_two = layer_sum(local_two)
    delta_one = (back_two * slope_of(pre_one)).astype(jnp.bfloat16)
    local_one, back_one = backward(
        plane_one, delta_one.reshape(rows, height, breadth, narrow), filter_one
    )
    summed_one = layer_sum(local_one)
    input_grad = back_one.astype(jnp.bfloat16).reshape(rows, height, breadth, narrow)
    return (output, input_grad, summed_one * scale, summed_two * scale)


def is_seam():
    return lax.rem(lax.axis_index("dp") * 2, VOX) == 0


def place():
    at = lax.axis_index("dp")
    return at // 4, lax.rem(at // 2, 2), lax.rem(at, 2)


def place_bits():
    level, side, _ = place()
    return {"x": side, "z": lax.rem(level, 2), "zz": level // 2}


def shaped(values):
    return values.reshape(TILE, VOX, values.shape[1])


PARTS = {
    "all": dict(
        slots=((0, True), (1, True), (2, False), (1, False), (2, True), (3, True)),
        taps=(((0, 0), (1, 1), (2, 2)), ((0, 3), (1, 4), (2, 5))),
    ),
    "local": dict(
        slots=((0, True), (1, True), (0, False), (1, False)),
        taps=(((1, 0), (2, 3)), ((0, 2), (1, 1))),
    ),
    "rim": dict(
        slots=((0, True), (1, True)),
        taps=(((0, 0),), ((2, 1),)),
    ),
}


def filter_rows(kind):
    level, side, core = place()
    along, first = (side, 0) if kind == "quarters" else (lax.rem(level, 2), HALF)
    rows = [] if kind == "quarters" else [(HALF, 0)]
    if kind != "own":
        for unit in (core, 1 - core):
            rows += [(32, first + (2 * at + unit) * 32) for at in (along, 1 - along)]
    return rows


def copy_weights(kind, part, pieces, store, sems):
    me = lax.axis_index("chan")
    copies = []
    for (height, row), piece in zip(filter_rows(kind), pieces):
        if not isinstance(row, int):
            row = pl.multiple_of(row, 32)
        spans = ((0, 27),) if part != "rim" else ((0, 9), (18, 9))
        for side in range(2):
            column = pl.multiple_of((me if side == 0 else 1 - me) * HALF, HALF)
            for first, length in spans:
                taps = pl.ds(first, length)
                copies.append(
                    pltpu.make_async_copy(
                        piece.at[taps, :, pl.ds(column, HALF)],
                        store.at[taps, pl.ds(row, height), pl.ds(side * HALF, HALF)],
                        sems.at[len(copies)],
                    )
                )
    for copy in copies:
        copy.start()
    return copies


def fill_planes(part, planes, store):
    edge = jnp.zeros(store.shape[2:], store.dtype)
    seam = is_seam()
    for slot, (plane, always) in enumerate(PARTS[part]["slots"]):
        ref, at = planes[plane]
        store[slot, 0] = edge
        store[slot, VOX + 1] = edge
        if always:
            store[slot, 1 : VOX + 1] = ref[at]
            continue

        @pl.when(seam)
        def _():
            store[slot] = jnp.zeros(store.shape[1:], store.dtype)

        @pl.when(jnp.logical_not(seam))
        def _():
            store[slot, 1 : VOX + 1] = ref[at]


def conv_rows(store, weights, taps, row, flipped):
    pieces = []
    for _, slot in taps:
        for b in range(3):
            piece = store[slot, pl.ds(row + b, TILE)]
            pieces.append(piece.reshape(TILE * VOX, store.shape[3]))
    stacked = jnp.concatenate(pieces, axis=1)
    products = []
    for c in range(3):
        if flipped:
            tiles = [weights[(2 - a) * 9 + (2 - b) * 3 + 2 - c] for a, _ in taps for b in range(3)]
            dims = (((1,), (1,)), ((), ()))
            tiles = jnp.concatenate(tiles, axis=1)
        else:
            tiles = [weights[a * 9 + b * 3 + c] for a, _ in taps for b in range(3)]
            dims = (((1,), (0,)), ((), ()))
            tiles = jnp.concatenate(tiles, axis=0)
        products.append(
            lax.dot_general(stacked, tiles, dims, preferred_element_type=jnp.float32)
        )
    left, middle, right = products
    column = lax.rem(lax.broadcasted_iota(jnp.int32, left.shape, 0), VOX)
    left = jnp.where(column > 0, pltpu.roll(left, 1, 0), 0.0)
    right = jnp.where(column < VOX - 1, pltpu.roll(right, TILE * VOX - 1, 0), 0.0)
    return middle + left + right


def conv_kernel(part, kind, flipped, finish, counts, *refs):
    refs = list(refs)
    groups = []
    for count in counts:
        groups.append(refs[:count])
        refs = refs[count:]
    planes, pieces, begun, extra, outs = groups
    if kind == "ready":
        (weights,), copies = pieces, []
        (store,) = refs
    else:
        store, sems = refs
        weights = outs.pop()
        copies = copy_weights(kind, part, pieces, weights, sems)
    views = []
    for ref in planes:
        views += [(ref, at) for at in range(ref.shape[0])]
    fill_planes(part, views, store)
    for copy in copies:
        copy.wait()
    for plane in range(2):
        taps = PARTS[part]["taps"][plane]

        @pl.loop(0, VOX // TILE, unroll=True)
        def _(step):
            rows = pl.ds(pl.multiple_of(step * TILE, TILE), TILE)
            value = shaped(conv_rows(store, weights, taps, step * TILE, flipped))
            if begun:
                value = value + begun[0][plane, rows]
            finish(value, plane, rows, extra, outs)


def finish_partial(value, plane, rows, extra, outs):
    outs[0][plane, rows] = value


def finish_first(value, plane, rows, extra, outs):
    outs[plane][0, rows] = leaky(value).astype(jnp.bfloat16)


def finish_second(value, plane, rows, extra, outs):
    output, deltas = outs[0], outs[1:]
    output[plane, rows] = leaky(value[:, :, :HALF]).astype(jnp.bfloat16)
    slope = slope_of(value)
    for lane, cot in ((0, extra[0]), (HALF, extra[1])):
        delta = cot[plane, rows].astype(jnp.float32) * slope[:, :, lane : lane + HALF]
        deltas[plane][0, rows, :, lane : lane + HALF] = delta.astype(jnp.bfloat16)


def finish_back(value, plane, rows, extra, outs):
    act = extra[plane][0, rows].astype(jnp.float32)
    outs[plane][0, rows] = (value * slope_of(act)).astype(jnp.bfloat16)


def finish_last(value, plane, rows, extra, outs):
    outs[0][plane, rows] = value.astype(jnp.bfloat16)


def filter_kernel(colours, *refs):
    low, mid_0, mid_1, high, delta_0, delta_1 = refs[:6]
    outs, (turned, moved) = refs[6:-2], refs[-2:]
    _, _, core = place()
    bits = place_bits()
    pixels = VOX * VOX
    seam = is_seam()
    sources = ((0, low), (1, mid_0), (2, mid_1), (3, high))
    for plane, ref in sources:
        flipped = ref[0].reshape(pixels, HALF).T
        for output_plane in range(2):
            tap = plane - output_plane
            if not 0 <= tap < 3:
                continue
            rows = slice(tap * HALF, (tap + 1) * HALF)
            columns = slice(output_plane * pixels, (output_plane + 1) * pixels)
            if plane in (1, 2) and tap != 1:
                turned[rows, columns] = jnp.where(seam, jnp.zeros_like(flipped), flipped)
            else:
                turned[rows, columns] = flipped
    for plane, ref in ((0, delta_0), (1, delta_1)):
        for c in range(3):
            moved[c, plane, 0] = jnp.zeros(moved.shape[3:], moved.dtype)
            moved[c, plane, VOX + 1] = jnp.zeros(moved.shape[3:], moved.dtype)
        moved[1, plane, 1 : VOX + 1] = ref[0]

        @pl.loop(0, VOX // TILE, unroll=True)
        def _(step):
            row = step * TILE
            values = ref[0, pl.ds(row, TILE)].reshape(TILE * VOX, FULL).astype(jnp.float32)
            column = lax.rem(lax.broadcasted_iota(jnp.int32, values.shape, 0), VOX)
            ahead = jnp.where(column < VOX - 1, pltpu.roll(values, TILE * VOX - 1, 0), 0.0)
            behind = jnp.where(column > 0, pltpu.roll(values, 1, 0), 0.0)
            moved[0, plane, pl.ds(row + 1, TILE)] = shaped(ahead.astype(jnp.bfloat16))
            moved[2, plane, pl.ds(row + 1, TILE)] = shaped(behind.astype(jnp.bfloat16))

    mine = lax.axis_index("chan") == core
    for tap in range(27):
        a, b, c = tap // 9, tap // 3 % 3, tap % 3
        if a:
            continue
        right = moved[c, :, 2 - b : 2 - b + VOX].reshape(2 * pixels, FULL)
        product = jnp.dot(turned[...], right, preferred_element_type=jnp.float32)
        kept = jnp.where(mine, product[:, :HALF], product[:, HALF:])
        sent = jnp.where(mine, product[:, HALF:], product[:, :HALF])
        for a in range(3):
            rows = slice(a * HALF, (a + 1) * HALF)
            for at, (first, taps, axis) in enumerate(colours):
                place_at = a * 9 + b * 3 + c - first
                if not 0 <= place_at < taps:
                    continue
                keep, far, near = outs[3 * at : 3 * at + 3]
                bit = bits[axis]
                keep[:, place_at] = kept[rows].reshape(8, 16, HALF)
                blocks = sent[rows].reshape(2, 4, 16, HALF).astype(far.dtype)
                far[:, place_at] = jnp.where(bit == 0, blocks[1], blocks[0])
                near[:, place_at] = jnp.where(bit == 0, blocks[0], blocks[1])


def halve_core_kernel(axis, keep, far, near, kept, sent):
    bit = place_bits()[axis]
    for target, came, first in ((kept, near, bit * 4), (sent, far, (1 - bit) * 4)):

        @pl.loop(0, 4)
        def _(block):
            total = keep[first + block] + came[block].astype(jnp.float32)
            target[block] = total.astype(target.dtype)


def halve_kernel(axis, keep, came, kept, sent):
    bit = place_bits()[axis]
    half = keep.shape[0] // 2
    for target, first in ((kept, bit * half), (sent, (1 - bit) * half)):
        for block in range(half):
            total = keep[first + block] + came[first + block].astype(jnp.float32)
            target[block] = total.astype(target.dtype)


def finish_kernel(scale, keep, came, total):
    total[...] = ((keep[...] + came[...].astype(jnp.float32)) * scale).astype(total.dtype)


def join_kernel(axis, own, came, target):
    bit = place_bits()[axis]
    half = own.shape[0]
    target[pl.ds(bit * half, half)] = own[...]
    target[pl.ds((1 - bit) * half, half)] = came[...]


def join_core_kernel(order, *refs):
    _, _, core = place()
    grad = refs[-1]
    first_tap = 0
    for own, came in zip(refs[0:-1:2], refs[1:-1:2]):
        taps = slice(first_tap, first_tap + own.shape[1])
        first_tap += own.shape[1]
        for at, block in enumerate(order):
            rows = slice(block * 16, block * 16 + 16)
            first = jnp.where(core == 0, own[at], came[at])
            second = jnp.where(core == 0, came[at], own[at])
            grad[taps, rows, :HALF] = first.astype(jnp.float32)
            grad[taps, rows, HALF:] = second.astype(jnp.float32)


WEIGHT = {
    "sum_two_core": 0,
    "first_rim": 3 * 10**9,
    "back_rim": 4 * 10**9,
    "sum_a_zz": 4 * 10**9,
    "sum_b_zz": 4 * 10**9,
    "join_a_zz": 4 * 10**9,
    "join_b_zz": 4 * 10**9,
    "join_a_z": 6 * 10**9,
    "join_b_x": 6 * 10**9,
    "join_a_x": 6 * 10**9,
    "join_b_z": 6 * 10**9,
}


def hint(flops):
    return pl.CostEstimate(flops=flops, bytes_accessed=0, transcendentals=0)


def small_call(kernel, outs, operands, name):
    return pl.pallas_call(
        kernel,
        out_shape=[jax.ShapeDtypeStruct(shape, dtype) for shape, dtype in outs],
        in_specs=[pl.BlockSpec(memory_space=pltpu.VMEM)] * len(operands),
        out_specs=[pl.BlockSpec(memory_space=pltpu.VMEM)] * len(outs),
        compiler_params=pltpu.CompilerParams(vmem_limit_bytes=VMEM_LIMIT),
        cost_estimate=hint(WEIGHT.get(name, SMALL)),
        name=name,
    )(*operands)


def halve_core(axis, keep, far, near, name):
    outs = [(far.shape, jnp.float32), (far.shape, jnp.bfloat16)]
    return small_call(functools.partial(halve_core_kernel, axis), outs, [keep, far, near], name)


def halve(axis, keep, came, name):
    shape = (keep.shape[0] // 2,) + keep.shape[1:]
    outs = [(shape, jnp.float32), (shape, jnp.bfloat16)]
    return small_call(functools.partial(halve_kernel, axis), outs, [keep, came], name)


def finish(scale, keep, came, name):
    outs = [(keep.shape, jnp.bfloat16)]
    return small_call(functools.partial(finish_kernel, scale), outs, [keep, came], name)[0]


def join(axis, own, came, name):
    outs = [((2 * own.shape[0],) + own.shape[1:], jnp.bfloat16)]
    return small_call(functools.partial(join_kernel, axis), outs, [own, came], name)[0]


def join_core(order, colours, name):
    outs = [((27, HALF, FULL), jnp.float32)]
    operands = [half for pair in colours for half in pair]
    return small_call(functools.partial(join_core_kernel, order), outs, operands, name)[0]


def conv_call(name, part, kind, finish, outs, planes, pieces, begun=(), extra=(), flipped=False):
    lanes = planes[0].shape[3]
    height = {"own": HALF, "quarters": HALF, "both": FULL, "ready": pieces[0].shape[1]}[kind]
    ready = kind == "ready"
    if not ready:
        outs = outs + [((27, height, FULL), jnp.bfloat16)]
    operands = [*planes, *pieces, *begun, *extra]
    counts = (len(planes), len(pieces), len(begun), len(extra), len(outs))
    specs = [pl.BlockSpec(memory_space=pltpu.VMEM) for _ in operands]
    if not ready:
        for at in range(len(planes), len(planes) + len(pieces)):
            own = kind != "quarters" and at == len(planes)
            specs[at] = pl.BlockSpec(memory_space=pltpu.HBM if own else pl.ANY)
    scratch = [pltpu.VMEM((len(PARTS[part]["slots"]), VOX + 2, VOX, lanes), jnp.bfloat16)]
    if not ready:
        scratch.append(pltpu.SemaphoreType.DMA((20,)))
    return pl.pallas_call(
        functools.partial(conv_kernel, part, kind, flipped, finish, counts),
        out_shape=[jax.ShapeDtypeStruct(shape, dtype) for shape, dtype in outs],
        in_specs=specs,
        out_specs=[pl.BlockSpec(memory_space=pltpu.VMEM)] * len(outs),
        scratch_shapes=scratch,
        compiler_params=pltpu.CompilerParams(vmem_limit_bytes=VMEM_LIMIT),
        cost_estimate=hint(WEIGHT.get(name, 0)),
        name=name,
    )(*operands)


def filter_call(colours, planes, mid_at, deltas, name):
    narrow = (1, VOX, VOX, HALF)
    specs = [
        pl.BlockSpec(narrow, functools.partial(lambda at, i: (at, 0, 0, 0), at)) for at in mid_at
    ]
    specs += [pl.BlockSpec((1, VOX, VOX, FULL), lambda i: (0, 0, 0, 0))] * 2
    outs = []
    for _, taps, _ in colours:
        for blocks, dtype in ((8, jnp.float32), (4, jnp.bfloat16), (4, jnp.bfloat16)):
            outs.append(jax.ShapeDtypeStruct((blocks, taps, 16, HALF), dtype))
    values = pl.pallas_call(
        functools.partial(filter_kernel, colours),
        grid=(1,),
        out_shape=outs,
        in_specs=specs,
        out_specs=[pl.BlockSpec(out.shape, lambda i: (0, 0, 0, 0)) for out in outs],
        scratch_shapes=[
            pltpu.VMEM((3 * HALF, 2 * VOX * VOX), jnp.bfloat16),
            pltpu.VMEM((3, 2, VOX + 2, VOX, FULL), jnp.bfloat16),
        ],
        compiler_params=pltpu.CompilerParams(vmem_limit_bytes=VMEM_LIMIT),
        cost_estimate=hint(0),
        name=name,
    )(*planes, *deltas)
    return [values[at : at + 3] for at in range(0, len(values), 3)]


def after(value, *earlier):
    return lax.optimization_barrier((value,) + earlier)[0]


def paired(volume, filter_one, filter_two, cotangent):
    count = lax.axis_size("dp")
    ahead = [(i, (i + 1) % count) for i in range(count)]
    behind = [(target, source) for source, target in ahead]
    scale = 1.0 / math.sqrt(count * 2 * VOX * VOX)
    one = filter_one.reshape(27, HALF, FULL)
    two = filter_two.reshape(27, HALF, FULL)
    level, side, core = place()

    def other(values):
        return lax.ppermute(values, "chan", [(0, 1), (1, 0)])

    def to_core(values):
        return lax.ppermute(values, "dp", [(i, i ^ 1) for i in range(count)])

    def to_side(values):
        return lax.ppermute(values, "dp", [(i, i ^ 2) for i in range(count)])

    def to_level(values):
        return lax.ppermute(values, "dp", [(i, i ^ 4) for i in range(count)])

    def to_far_level(values):
        return lax.ppermute(values, "dp", [(i, i ^ 8) for i in range(count)])

    def rims(first, last):
        return lax.ppermute(last, "dp", ahead), lax.ppermute(first, "dp", behind)

    wide = ((1, VOX, VOX, FULL), jnp.bfloat16)
    narrow = ((2, VOX, VOX, HALF), jnp.bfloat16)
    partial = ((2, VOX, VOX, FULL), jnp.float32)
    half_partial = ((2, VOX, VOX, HALF), jnp.float32)

    low_own, high_own = rims(volume[:1], volume[1:])
    one_0 = other(lax.dynamic_slice_in_dim(one, (2 * side + core) * 32, 32, axis=1))
    volume_other = other(after(volume, one_0, low_own, high_own))
    one_1 = to_side(one_0)
    one_2 = to_core(one_0)
    begun, own_ready = conv_call(
        "first_own", "all", "own", finish_partial, [partial], [low_own, volume, high_own], [one]
    )
    one_3 = to_core(after(one_1, begun))
    quarters = [one_0, one_1, one_2, one_3]
    volume_other = after(volume_other, begun)
    two_0 = other(
        after(
            lax.dynamic_slice_in_dim(two, (2 * lax.rem(level, 2) + core) * 32, 32, axis=1),
            volume_other,
        )
    )
    low_other, high_other = rims(volume_other[:1], volume_other[1:])
    begun, ready = conv_call(
        "first_other", "local", "quarters", finish_partial, [partial], [volume_other], quarters,
        [begun],
    )
    two_0 = after(two_0, begun)
    two_1 = to_level(two_0)
    two_2 = to_core(two_0)
    cot_other = other(after(cotangent, two_0))
    act_0, act_1 = conv_call(
        "first_rim", "rim", "ready", finish_first, [wide, wide], [low_other, high_other],
        [ready], [begun],
    )
    low_act, high_act = rims(act_0, act_1)
    two_3 = to_core(two_1)
    pieces = [two, two_0, two_1, two_2, two_3]
    begun, ready = conv_call(
        "second_local", "local", "both", finish_partial, [partial], [act_0, act_1], pieces,
    )
    output, delta_0, delta_1 = conv_call(
        "second_rim", "rim", "ready", finish_second, [narrow, wide, wide], [low_act, high_act],
        [ready], [begun], [cotangent, cot_other],
    )
    low_delta, high_delta = rims(delta_0, delta_1)
    ((keep, far, near),) = filter_call(
        ((0, 27, "z"),), [low_act, act_0, act_1, high_act], (0, 0, 0, 0), [delta_0, delta_1],
        "grad_two",
    )
    keep_two, sent = halve_core("z", keep, to_core(far), to_core(near), "sum_two_core")
    came_two = to_level(sent)
    (begun,) = conv_call(
        "back_local", "local", "ready", finish_partial, [partial], [delta_0, after(delta_1, keep_two)],
        [ready], flipped=True,
    )
    prior_0, prior_1 = conv_call(
        "back_rim", "rim", "ready", finish_back, [wide, wide], [low_delta, high_delta],
        [ready], [begun], [act_0, act_1], flipped=True,
    )
    keep_two, sent = halve("x", after(keep_two, prior_0), came_two, "sum_two_z")
    came_two = to_side(sent)
    (keep_a, *sent_a), (keep_b, *sent_b) = filter_call(
        ((0, 14, "x"), (14, 13, "z")), [low_own, volume, volume, high_own], (0, 0, 1, 0),
        [prior_0, after(prior_1, keep_two)], "grad_one",
    )
    sent_a, sent_b = [to_core(half) for half in sent_a], [to_core(half) for half in sent_b]
    keep_two, sent = halve("zz", after(keep_two, keep_a), came_two, "sum_two_x")
    came_two = to_far_level(sent)
    keep_a, sent = halve_core("x", after(keep_a, keep_two), *sent_a, "sum_a_core")
    came_a = to_side(sent)
    keep_b, sent = halve_core("z", after(keep_b, keep_a), *sent_b, "sum_b_core")
    came_b = to_level(sent)
    (begun,) = conv_call(
        "first_back_local", "local", "ready", finish_partial, [half_partial],
        [after(prior_0, keep_b), prior_1], [own_ready], flipped=True,
    )
    keep_a, sent = halve("z", after(keep_a, begun), came_a, "sum_a_x")
    came_a = to_level(sent)
    keep_b, sent = halve("x", after(keep_b, keep_a), came_b, "sum_b_z")
    came_b = to_side(sent)
    low_prior, high_prior = rims(after(prior_0, keep_b), after(prior_1, keep_b))
    own_two = finish(scale, after(keep_two, keep_b), came_two, "sum_two_zz")
    came_two = to_far_level(own_two)
    keep_a, sent = halve("zz", after(keep_a, own_two), came_a, "sum_a_z")
    came_a = to_far_level(sent)
    keep_b, sent = halve("zz", after(keep_b, keep_a), came_b, "sum_b_x")
    came_b = to_far_level(sent)
    own_a = finish(scale, after(keep_a, keep_b), came_a, "sum_a_zz")
    came_a = to_far_level(own_a)
    own_b = finish(scale, after(keep_b, own_a), came_b, "sum_b_zz")
    came_b = to_far_level(own_b)
    own_two = join("zz", after(own_two, own_b), came_two, "join_two_zz")
    came_two = to_level(own_two)
    own_a = join("zz", after(own_a, own_two, low_prior, high_prior), came_a, "join_a_zz")
    came_a = to_level(own_a)
    own_b = join("zz", after(own_b, own_a), came_b, "join_b_zz")
    came_b = to_side(own_b)
    own_two = join("z", after(own_two, own_b), came_two, "join_two_z")
    came_two = to_side(own_two)
    own_a = join("z", after(own_a, own_two), came_a, "join_a_z")
    came_a = to_side(own_a)
    own_b = join("x", after(own_b, own_a), came_b, "join_b_x")
    came_b = to_level(own_b)
    (input_grad,) = conv_call(
        "first_back_rim", "rim", "ready", finish_last, [narrow],
        [after(low_prior, own_b), high_prior], [own_ready], [begun], flipped=True,
    )
    own_two = join("x", after(own_two, input_grad), came_two, "join_two_x")
    came_two = to_core(own_two)
    own_a = join("x", after(own_a, own_two), came_a, "join_a_x")
    came_a = to_core(own_a)
    own_b = join("z", after(own_b, own_a), came_b, "join_b_z")
    came_b = to_core(own_b)
    summed_two = join_core(
        (0, 1, 4, 5, 2, 3, 6, 7), [(after(own_two, own_b), came_two)], "grads_two"
    )
    summed_one = join_core(
        tuple(range(8)), [(after(own_a, summed_two), came_a), (own_b, came_b)], "grads_one"
    )
    shape = filter_one.shape
    return output, input_grad, summed_one.reshape(shape), summed_two.reshape(shape)


def local(volume, filter_one, filter_two, cotangent):
    pair = lax.axis_size("chan") == 2 and lax.axis_size("dp") == 16
    if pair and volume.shape == (2, VOX, VOX, HALF):
        return paired(volume, filter_one, filter_two, cotangent)
    return plain(volume, filter_one, filter_two, cotangent)


def solution(mesh):
    in_specs = (
        P("dp", None, None, "chan"),
        P(None, None, None, "chan", None),
        P(None, None, None, "chan", None),
        P("dp", None, None, "chan"),
    )
    out_specs = (
        P("dp", None, None, "chan"),
        P("dp", None, None, "chan"),
        P(None, None, None, "chan", None),
        P(None, None, None, "chan", None),
    )
    return jax.shard_map(local, mesh=mesh, in_specs=in_specs, out_specs=out_specs, check_vma=False)
```

```python
import functools
import math

import jax
import jax.numpy as jnp
from jax import lax
from jax.experimental import pallas as pl
from jax.experimental.pallas import tpu as pltpu
from jax.sharding import PartitionSpec as P

VOX = 32
SLOPE = 0.3
HALF = 128
FULL = 256
TILE = 16
SMALL = 10**9
VMEM_LIMIT = 32 * 1024 * 1024


def extended(block, sides, width):
    for axis, dim in sides:
        count = lax.axis_size(axis)
        forward = [(i, i + 1) for i in range(count - 1)]
        forward.append((count - 1, 0))
        backward = [(target, source) for source, target in forward]
        low = lax.ppermute(
            lax.slice_in_dim(block, block.shape[dim] - width, None, axis=dim), axis, forward
        )
        high = lax.ppermute(lax.slice_in_dim(block, 0, width, axis=dim), axis, backward)
        block = jnp.concatenate([low, block, high], axis=dim)
    return block


def leaky(values):
    return jnp.where(values > 0, values, SLOPE * values)


def slope_of(values):
    return jnp.where(values > 0, jnp.float32(1.0), jnp.float32(SLOPE))


def tap_mask(rows, offset):
    base = lax.axis_index("dp") * rows
    total_rows = lax.axis_size("dp") * rows
    planes = jnp.mod(base + jnp.arange(rows, dtype=jnp.int32) - 1, total_rows)
    depth = jnp.mod(planes, VOX) + offset
    inside = jnp.logical_and(depth >= 0, depth < VOX)
    return inside[:, None, None, None]


def pad_plane(values):
    return jnp.pad(values, ((0, 0), (1, 1), (1, 1), (0, 0)))


def columns(plane, rows, height, breadth):
    taps = []
    for a in range(3):
        inside = tap_mask(rows, a - 1)
        depth_slab = plane[a : a + rows]
        depth_slab = jnp.where(inside, depth_slab, jnp.zeros_like(depth_slab))
        for b in range(3):
            for c in range(3):
                taps.append(depth_slab[:, b : b + height, c : c + breadth, :])
    stacked = jnp.concatenate(taps, axis=-1)
    return stacked.reshape(rows * height * breadth, stacked.shape[-1])


def plain(volume, filter_one, filter_two, cotangent):
    rows, height, breadth, narrow = volume.shape
    full = filter_one.shape[4]
    voxels = rows * height * breadth
    scale = 1.0 / math.sqrt(lax.axis_size("dp") * voxels)

    def forward(activity, weight):
        rim = extended(activity, (("dp", 0),), 1)
        plane = pad_plane(rim)
        stacked = columns(plane, rows, height, breadth)
        partial_value = jnp.dot(
            stacked, weight.reshape(27 * narrow, full), preferred_element_type=jnp.float32
        )
        summed = lax.psum_scatter(partial_value, "chan", scatter_dimension=1, tiled=True)
        return (plane, summed)

    def backward(plane, delta, weight):
        wide = lax.all_gather(delta, "chan", axis=3, tiled=True)
        rim = extended(wide, (("dp", 0),), 1)
        centre = rim[1 : rows + 1].reshape(voxels, full)
        stacked = columns(plane, rows, height, breadth)
        weight_grad = lax.dot_general(
            stacked, centre, (((0,), (0,)), ((), ())), preferred_element_type=jnp.float32
        )
        weight_grad = weight_grad.reshape(3, 3, 3, narrow, full)
        source = pad_plane(rim)
        total = jnp.zeros((rows, height, breadth, narrow), jnp.float32)
        for a in range(3):
            depth_slab = source[2 - a : 2 - a + rows]
            flat = depth_slab.reshape(-1, full)
            product = lax.dot_general(
                flat,
                weight[a].reshape(9 * narrow, full),
                (((1,), (1,)), ((), ())),
                preferred_element_type=jnp.float32,
            )
            product = product.reshape(rows, height + 2, breadth + 2, 9, narrow)
            part = jnp.zeros((rows, height, breadth, narrow), jnp.float32)
            for b in range(3):
                for c in range(3):
                    part = (
                        part
                        + product[:, 2 - b : 2 - b + height, 2 - c : 2 - c + breadth, b * 3 + c, :]
                    )
            inside = tap_mask(rows, 1 - a)
            total = total + jnp.where(inside, part, jnp.zeros_like(part))
        return (weight_grad, total.reshape(voxels, narrow))

    def layer_sum(weight_grad):
        return lax.psum(weight_grad, "dp")

    plane_one, pre_one = forward(volume, filter_one)
    act_one = leaky(pre_one).astype(jnp.bfloat16).reshape(rows, height, breadth, narrow)
    plane_two, pre_two = forward(act_one, filter_two)
    output = leaky(pre_two).astype(jnp.bfloat16).reshape(rows, height, breadth, narrow)
    delta_two = (cotangent.reshape(voxels, narrow).astype(jnp.float32) * slope_of(pre_two)).astype(
        jnp.bfloat16
    )
    local_two, back_two = backward(
        plane_two, delta_two.reshape(rows, height, breadth, narrow), filter_two
    )
    summed_two = layer_sum(local_two)
    delta_one = (back_two * slope_of(pre_one)).astype(jnp.bfloat16)
    local_one, back_one = backward(
        plane_one, delta_one.reshape(rows, height, breadth, narrow), filter_one
    )
    summed_one = layer_sum(local_one)
    input_grad = back_one.astype(jnp.bfloat16).reshape(rows, height, breadth, narrow)
    return (output, input_grad, summed_one * scale, summed_two * scale)


def is_seam():
    return lax.rem(lax.axis_index("dp") * 2, VOX) == 0


def place():
    at = lax.axis_index("dp")
    return at // 4, lax.rem(at // 2, 2), lax.rem(at, 2)


def place_bits():
    level, side, _ = place()
    return {"x": side, "z": lax.rem(level, 2), "zz": level // 2}


def shaped(values):
    return values.reshape(TILE, VOX, values.shape[1])


PARTS = {
    "all": dict(
        slots=((0, True), (1, True), (2, False), (1, False), (2, True), (3, True)),
        taps=(((0, 0), (1, 1), (2, 2)), ((0, 3), (1, 4), (2, 5))),
    ),
    "local": dict(
        slots=((0, True), (1, True), (0, False), (1, False)),
        taps=(((1, 0), (2, 3)), ((0, 2), (1, 1))),
    ),
    "rim": dict(
        slots=((0, True), (1, True)),
        taps=(((0, 0),), ((2, 1),)),
    ),
}


def filter_rows(kind):
    level, side, core = place()
    along, first = (side, 0) if kind == "quarters" else (lax.rem(level, 2), HALF)
    rows = [] if kind == "quarters" else [(HALF, 0)]
    if kind != "own":
        for unit in (core, 1 - core):
            rows += [(32, first + (2 * at + unit) * 32) for at in (along, 1 - along)]
    return rows


def copy_weights(kind, part, pieces, store, sems):
    me = lax.axis_index("chan")
    copies = []
    for (height, row), piece in zip(filter_rows(kind), pieces):
        if not isinstance(row, int):
            row = pl.multiple_of(row, 32)
        spans = ((0, 27),) if part != "rim" else ((0, 9), (18, 9))
        for side in range(2):
            column = pl.multiple_of((me if side == 0 else 1 - me) * HALF, HALF)
            for first, length in spans:
                taps = pl.ds(first, length)
                copies.append(
                    pltpu.make_async_copy(
                        piece.at[taps, :, pl.ds(column, HALF)],
                        store.at[taps, pl.ds(row, height), pl.ds(side * HALF, HALF)],
                        sems.at[len(copies)],
                    )
                )
    for copy in copies:
        copy.start()
    return copies


def fill_planes(part, planes, store, lane):
    lanes = pl.ds(lane, store.shape[3])
    edge = jnp.zeros(store.shape[2:], store.dtype)
    seam = is_seam()
    for slot, (plane, always) in enumerate(PARTS[part]["slots"]):
        ref, at = planes[plane]
        store[slot, 0] = edge
        store[slot, VOX + 1] = edge
        if always:
            store[slot, 1 : VOX + 1] = ref[at, :, :, lanes]
            continue

        @pl.when(seam)
        def _():
            store[slot] = jnp.zeros(store.shape[1:], store.dtype)

        @pl.when(jnp.logical_not(seam))
        def _():
            store[slot, 1 : VOX + 1] = ref[at, :, :, lanes]


def conv_rows(store, weights, taps, row, flipped, first):
    pieces = []
    for _, slot in taps:
        for b in range(3):
            piece = store[slot, pl.ds(row + b, TILE)]
            pieces.append(piece.reshape(TILE * VOX, store.shape[3]))
    stacked = jnp.concatenate(pieces, axis=1)
    products = []
    for c in range(3):
        if flipped:
            tiles = [weights[(2 - a) * 9 + (2 - b) * 3 + 2 - c] for a, _ in taps for b in range(3)]
            dims = (((1,), (1,)), ((), ()))
            tiles = jnp.concatenate(tiles, axis=1)
        else:
            rows = slice(first, first + store.shape[3])
            tiles = [weights[a * 9 + b * 3 + c, rows] for a, _ in taps for b in range(3)]
            dims = (((1,), (0,)), ((), ()))
            tiles = jnp.concatenate(tiles, axis=0)
        products.append(
            lax.dot_general(stacked, tiles, dims, preferred_element_type=jnp.float32)
        )
    left, middle, right = products
    column = lax.rem(lax.broadcasted_iota(jnp.int32, left.shape, 0), VOX)
    left = jnp.where(column > 0, pltpu.roll(left, 1, 0), 0.0)
    right = jnp.where(column < VOX - 1, pltpu.roll(right, TILE * VOX - 1, 0), 0.0)
    return middle + left + right


def conv_kernel(part, kind, flipped, finish, counts, lane, row, *refs):
    refs = list(refs)
    groups = []
    for count in counts:
        groups.append(refs[:count])
        refs = refs[count:]
    planes, pieces, begun, extra, outs = groups
    if kind == "ready":
        (weights,), copies = pieces, []
        (store,) = refs
    else:
        store, sems = refs
        weights = outs.pop()
        copies = copy_weights(kind, part, pieces, weights, sems)
    views = []
    for ref in planes:
        views += [(ref, at) for at in range(ref.shape[0])]
    fill_planes(part, views, store, lane)
    for copy in copies:
        copy.wait()
    for plane in range(2):
        taps = PARTS[part]["taps"][plane]

        @pl.loop(0, VOX // TILE, unroll=True)
        def _(step):
            rows = pl.ds(pl.multiple_of(step * TILE, TILE), TILE)
            value = shaped(conv_rows(store, weights, taps, step * TILE, flipped, row))
            if begun:
                value = value + begun[0][plane, rows]
            finish(value, plane, rows, extra, outs)


def finish_partial(value, plane, rows, extra, outs):
    outs[0][plane, rows] = value


def finish_first(value, plane, rows, extra, outs):
    outs[plane][0, rows] = leaky(value).astype(jnp.bfloat16)


def finish_second(value, plane, rows, extra, outs):
    output, deltas = outs[0], outs[1:]
    output[plane, rows] = leaky(value[:, :, :HALF]).astype(jnp.bfloat16)
    slope = slope_of(value)
    for lane, cot in ((0, extra[0]), (HALF, extra[1])):
        delta = cot[plane, rows].astype(jnp.float32) * slope[:, :, lane : lane + HALF]
        deltas[plane][0, rows, :, lane : lane + HALF] = delta.astype(jnp.bfloat16)


def finish_back(value, plane, rows, extra, outs):
    act = extra[plane][0, rows].astype(jnp.float32)
    outs[plane][0, rows] = (value * slope_of(act)).astype(jnp.bfloat16)


def finish_last(value, plane, rows, extra, outs):
    outs[0][plane, rows] = value.astype(jnp.bfloat16)


def filter_kernel(colours, *refs):
    low, mid_0, mid_1, high, delta_0, delta_1 = refs[:6]
    outs, (turned, moved) = refs[6:-2], refs[-2:]
    _, _, core = place()
    bits = place_bits()
    pixels = VOX * VOX
    seam = is_seam()
    sources = ((0, low), (1, mid_0), (2, mid_1), (3, high))
    for plane, ref in sources:
        flipped = ref[0].reshape(pixels, HALF).T
        for output_plane in range(2):
            tap = plane - output_plane
            if not 0 <= tap < 3:
                continue
            rows = slice(tap * HALF, (tap + 1) * HALF)
            columns = slice(output_plane * pixels, (output_plane + 1) * pixels)
            if plane in (1, 2) and tap != 1:
                turned[rows, columns] = jnp.where(seam, jnp.zeros_like(flipped), flipped)
            else:
                turned[rows, columns] = flipped
    for plane, ref in ((0, delta_0), (1, delta_1)):
        for c in range(3):
            moved[c, plane, 0] = jnp.zeros(moved.shape[3:], moved.dtype)
            moved[c, plane, VOX + 1] = jnp.zeros(moved.shape[3:], moved.dtype)
        moved[1, plane, 1 : VOX + 1] = ref[0]

        @pl.loop(0, VOX // TILE, unroll=True)
        def _(step):
            row = step * TILE
            values = ref[0, pl.ds(row, TILE)].reshape(TILE * VOX, FULL).astype(jnp.float32)
            column = lax.rem(lax.broadcasted_iota(jnp.int32, values.shape, 0), VOX)
            ahead = jnp.where(column < VOX - 1, pltpu.roll(values, TILE * VOX - 1, 0), 0.0)
            behind = jnp.where(column > 0, pltpu.roll(values, 1, 0), 0.0)
            moved[0, plane, pl.ds(row + 1, TILE)] = shaped(ahead.astype(jnp.bfloat16))
            moved[2, plane, pl.ds(row + 1, TILE)] = shaped(behind.astype(jnp.bfloat16))

    mine = lax.axis_index("chan") == core
    for tap in range(27):
        a, b, c = tap // 9, tap // 3 % 3, tap % 3
        if a:
            continue
        right = moved[c, :, 2 - b : 2 - b + VOX].reshape(2 * pixels, FULL)
        product = jnp.dot(turned[...], right, preferred_element_type=jnp.float32)
        kept = jnp.where(mine, product[:, :HALF], product[:, HALF:])
        sent = jnp.where(mine, product[:, HALF:], product[:, :HALF])
        for a in range(3):
            rows = slice(a * HALF, (a + 1) * HALF)
            for at, (first, taps, axis) in enumerate(colours):
                place_at = a * 9 + b * 3 + c - first
                if not 0 <= place_at < taps:
                    continue
                keep, far, near = outs[3 * at : 3 * at + 3]
                bit = bits[axis]
                keep[:, place_at] = kept[rows].reshape(8, 16, HALF)
                blocks = sent[rows].reshape(2, 4, 16, HALF).astype(far.dtype)
                far[:, place_at] = jnp.where(bit == 0, blocks[1], blocks[0])
                near[:, place_at] = jnp.where(bit == 0, blocks[0], blocks[1])


def halve_core_kernel(axis, keep, far, near, kept, sent):
    bit = place_bits()[axis]
    for target, came, first in ((kept, near, bit * 4), (sent, far, (1 - bit) * 4)):

        @pl.loop(0, 4)
        def _(block):
            total = keep[first + block] + came[block].astype(jnp.float32)
            target[block] = total.astype(target.dtype)


def halve_kernel(axis, keep, came, kept, sent):
    bit = place_bits()[axis]
    half = keep.shape[0] // 2
    for target, first in ((kept, bit * half), (sent, (1 - bit) * half)):
        for block in range(half):
            total = keep[first + block] + came[first + block].astype(jnp.float32)
            target[block] = total.astype(target.dtype)


def finish_kernel(scale, keep, came, total):
    total[...] = ((keep[...] + came[...].astype(jnp.float32)) * scale).astype(total.dtype)


def join_kernel(axis, own, came, target):
    bit = place_bits()[axis]
    half = own.shape[0]
    target[pl.ds(bit * half, half)] = own[...]
    target[pl.ds((1 - bit) * half, half)] = came[...]


def join_core_kernel(order, *refs):
    _, _, core = place()
    grad = refs[-1]
    first_tap = 0
    for own, came in zip(refs[0:-1:2], refs[1:-1:2]):
        taps = slice(first_tap, first_tap + own.shape[1])
        first_tap += own.shape[1]
        for at, block in enumerate(order):
            rows = slice(block * 16, block * 16 + 16)
            first = jnp.where(core == 0, own[at], came[at])
            second = jnp.where(core == 0, came[at], own[at])
            grad[taps, rows, :HALF] = first.astype(jnp.float32)
            grad[taps, rows, HALF:] = second.astype(jnp.float32)


WEIGHT = {
    "sum_two_core": 0,
    "sum_two_z": 0,
    "sum_two_x": 2 * 10**9,
    "sum_a_core": 0,
    "sum_b_core": 0,
    "first_rim": 3 * 10**9,
    "back_rim": 10**9,
    "sum_a_zz": 2 * 10**9,
    "sum_b_zz": 2 * 10**9,
    "join_a_zz": 2 * 10**9,
    "join_b_zz": 2 * 10**9,
    "join_a_z": 6 * 10**9,
    "join_b_x": 6 * 10**9,
    "join_a_x": 6 * 10**9,
    "join_b_z": 6 * 10**9,
}


def hint(flops):
    return pl.CostEstimate(flops=flops, bytes_accessed=0, transcendentals=0)


def small_call(kernel, outs, operands, name):
    return pl.pallas_call(
        kernel,
        out_shape=[jax.ShapeDtypeStruct(shape, dtype) for shape, dtype in outs],
        in_specs=[pl.BlockSpec(memory_space=pltpu.VMEM)] * len(operands),
        out_specs=[pl.BlockSpec(memory_space=pltpu.VMEM)] * len(outs),
        compiler_params=pltpu.CompilerParams(vmem_limit_bytes=VMEM_LIMIT),
        cost_estimate=hint(WEIGHT.get(name, SMALL)),
        name=name,
    )(*operands)


def halve_core(axis, keep, far, near, name):
    outs = [(far.shape, jnp.float32), (far.shape, jnp.bfloat16)]
    return small_call(functools.partial(halve_core_kernel, axis), outs, [keep, far, near], name)


def halve(axis, keep, came, name):
    shape = (keep.shape[0] // 2,) + keep.shape[1:]
    outs = [(shape, jnp.float32), (shape, jnp.bfloat16)]
    return small_call(functools.partial(halve_kernel, axis), outs, [keep, came], name)


def finish(scale, keep, came, name):
    outs = [(keep.shape, jnp.bfloat16)]
    return small_call(functools.partial(finish_kernel, scale), outs, [keep, came], name)[0]


def join(axis, own, came, name):
    outs = [((2 * own.shape[0],) + own.shape[1:], jnp.bfloat16)]
    return small_call(functools.partial(join_kernel, axis), outs, [own, came], name)[0]


def join_core(order, colours, name):
    outs = [((27, HALF, FULL), jnp.float32)]
    operands = [half for pair in colours for half in pair]
    return small_call(functools.partial(join_core_kernel, order), outs, operands, name)[0]


def conv_call(
    name, part, kind, finish, outs, planes, pieces, begun=(), extra=(), flipped=False,
    lane=0, lanes=None, row=0,
):
    lanes = lanes or planes[0].shape[3]
    height = {"own": HALF, "quarters": HALF, "both": FULL, "ready": pieces[0].shape[1]}[kind]
    ready = kind == "ready"
    if not ready:
        outs = outs + [((27, height, FULL), jnp.bfloat16)]
    operands = [*planes, *pieces, *begun, *extra]
    counts = (len(planes), len(pieces), len(begun), len(extra), len(outs))
    specs = [pl.BlockSpec(memory_space=pltpu.VMEM) for _ in operands]
    if not ready:
        for at in range(len(planes), len(planes) + len(pieces)):
            own = kind != "quarters" and at == len(planes)
            specs[at] = pl.BlockSpec(memory_space=pltpu.HBM if own else pl.ANY)
    scratch = [pltpu.VMEM((len(PARTS[part]["slots"]), VOX + 2, VOX, lanes), jnp.bfloat16)]
    if not ready:
        scratch.append(pltpu.SemaphoreType.DMA((20,)))
    return pl.pallas_call(
        functools.partial(conv_kernel, part, kind, flipped, finish, counts, lane, row),
        out_shape=[jax.ShapeDtypeStruct(shape, dtype) for shape, dtype in outs],
        in_specs=specs,
        out_specs=[pl.BlockSpec(memory_space=pltpu.VMEM)] * len(outs),
        scratch_shapes=scratch,
        compiler_params=pltpu.CompilerParams(vmem_limit_bytes=VMEM_LIMIT),
        cost_estimate=hint(WEIGHT.get(name, 0)),
        name=name,
    )(*operands)


def filter_call(colours, planes, mid_at, deltas, name):
    narrow = (1, VOX, VOX, HALF)
    specs = [
        pl.BlockSpec(narrow, functools.partial(lambda at, i: (at, 0, 0, 0), at)) for at in mid_at
    ]
    specs += [pl.BlockSpec((1, VOX, VOX, FULL), lambda i: (0, 0, 0, 0))] * 2
    outs = []
    for _, taps, _ in colours:
        for blocks, dtype in ((8, jnp.float32), (4, jnp.bfloat16), (4, jnp.bfloat16)):
            outs.append(jax.ShapeDtypeStruct((blocks, taps, 16, HALF), dtype))
    values = pl.pallas_call(
        functools.partial(filter_kernel, colours),
        grid=(1,),
        out_shape=outs,
        in_specs=specs,
        out_specs=[pl.BlockSpec(out.shape, lambda i: (0, 0, 0, 0)) for out in outs],
        scratch_shapes=[
            pltpu.VMEM((3 * HALF, 2 * VOX * VOX), jnp.bfloat16),
            pltpu.VMEM((3, 2, VOX + 2, VOX, FULL), jnp.bfloat16),
        ],
        compiler_params=pltpu.CompilerParams(vmem_limit_bytes=VMEM_LIMIT),
        cost_estimate=hint(0),
        name=name,
    )(*planes, *deltas)
    return [values[at : at + 3] for at in range(0, len(values), 3)]


def after(value, *earlier):
    return lax.optimization_barrier((value,) + earlier)[0]


def paired(volume, filter_one, filter_two, cotangent):
    count = lax.axis_size("dp")
    ahead = [(i, (i + 1) % count) for i in range(count)]
    behind = [(target, source) for source, target in ahead]
    scale = 1.0 / math.sqrt(count * 2 * VOX * VOX)
    one = filter_one.reshape(27, HALF, FULL)
    two = filter_two.reshape(27, HALF, FULL)
    level, side, core = place()

    def other(values):
        return lax.ppermute(values, "chan", [(0, 1), (1, 0)])

    def to_core(values):
        return lax.ppermute(values, "dp", [(i, i ^ 1) for i in range(count)])

    def to_side(values):
        return lax.ppermute(values, "dp", [(i, i ^ 2) for i in range(count)])

    def to_level(values):
        return lax.ppermute(values, "dp", [(i, i ^ 4) for i in range(count)])

    def to_far_level(values):
        return lax.ppermute(values, "dp", [(i, i ^ 8) for i in range(count)])

    def rims(first, last):
        return lax.ppermute(last, "dp", ahead), lax.ppermute(first, "dp", behind)

    wide = ((1, VOX, VOX, FULL), jnp.bfloat16)
    narrow = ((2, VOX, VOX, HALF), jnp.bfloat16)
    partial = ((2, VOX, VOX, FULL), jnp.float32)
    half_partial = ((2, VOX, VOX, HALF), jnp.float32)

    low_own, high_own = rims(volume[:1], volume[1:])
    one_0 = other(lax.dynamic_slice_in_dim(one, (2 * side + core) * 32, 32, axis=1))
    volume_other = other(after(volume, one_0, low_own, high_own))
    one_1 = to_side(one_0)
    one_2 = to_core(one_0)
    begun, own_ready = conv_call(
        "first_own", "all", "own", finish_partial, [partial], [low_own, volume, high_own], [one]
    )
    one_3 = to_core(after(one_1, begun))
    quarters = [one_0, one_1, one_2, one_3]
    volume_other = after(volume_other, begun)
    two_0 = other(
        after(
            lax.dynamic_slice_in_dim(two, (2 * lax.rem(level, 2) + core) * 32, 32, axis=1),
            volume_other,
        )
    )
    low_other, high_other = rims(volume_other[:1], volume_other[1:])
    begun, ready = conv_call(
        "first_other", "local", "quarters", finish_partial, [partial], [volume_other], quarters,
        [begun],
    )
    two_0 = after(two_0, begun)
    two_1 = to_level(two_0)
    two_2 = to_core(two_0)
    cot_other = other(after(cotangent, two_0))
    act_0, act_1 = conv_call(
        "first_rim", "rim", "ready", finish_first, [wide, wide], [low_other, high_other],
        [ready], [begun],
    )
    low_act, high_act = rims(act_0, act_1)
    begun, _ = conv_call(
        "second_own", "local", "own", finish_partial, [partial], [act_0, act_1], [two], lanes=HALF
    )
    two_3 = to_core(after(two_1, begun))
    pieces = [two, two_0, two_1, two_2, two_3]
    begun, ready = conv_call(
        "second_other", "local", "both", finish_partial, [partial], [act_0, act_1], pieces, [begun],
        lane=HALF, lanes=HALF, row=HALF,
    )
    output, delta_0, delta_1 = conv_call(
        "second_rim", "rim", "ready", finish_second, [narrow, wide, wide], [low_act, high_act],
        [ready], [begun], [cotangent, cot_other],
    )
    low_delta, high_delta = rims(delta_0, delta_1)
    ((keep, far, near),) = filter_call(
        ((0, 27, "z"),), [low_act, act_0, act_1, high_act], (0, 0, 0, 0), [delta_0, delta_1],
        "grad_two",
    )
    keep_two, sent = halve_core("z", keep, to_core(far), to_core(near), "sum_two_core")
    came_two = to_level(sent)
    (begun,) = conv_call(
        "back_local", "local", "ready", finish_partial, [partial], [delta_0, after(delta_1, keep_two)],
        [ready], flipped=True,
    )
    prior_0, prior_1 = conv_call(
        "back_rim", "rim", "ready", finish_back, [wide, wide], [low_delta, high_delta],
        [ready], [begun], [act_0, act_1], flipped=True,
    )
    low_prior, high_prior = rims(prior_0, prior_1)
    (keep_a, *sent_a), (keep_b, *sent_b) = filter_call(
        ((0, 14, "x"), (14, 13, "z")), [low_own, volume, volume, high_own], (0, 0, 1, 0),
        [prior_0, prior_1], "grad_one",
    )
    sent_a, sent_b = [to_core(half) for half in sent_a], [to_core(half) for half in sent_b]
    keep_two, sent = halve("x", after(keep_two, keep_a), came_two, "sum_two_z")
    came_two = to_side(sent)
    keep_a, sent = halve_core("x", after(keep_a, keep_two), *sent_a, "sum_a_core")
    came_a = to_side(sent)
    keep_b, sent = halve_core("z", after(keep_b, keep_a), *sent_b, "sum_b_core")
    came_b = to_level(sent)
    (begun,) = conv_call(
        "first_back_local", "local", "ready", finish_partial, [half_partial],
        [after(prior_0, keep_b), prior_1], [own_ready], flipped=True,
    )
    keep_two, sent = halve("zz", after(keep_two, begun, low_prior, high_prior), came_two, "sum_two_x")
    came_two = to_far_level(sent)
    keep_a, sent = halve("z", after(keep_a, keep_two), came_a, "sum_a_x")
    came_a = to_level(sent)
    keep_b, sent = halve("x", after(keep_b, keep_a), came_b, "sum_b_z")
    came_b = to_side(sent)
    own_two = finish(scale, after(keep_two, keep_b), came_two, "sum_two_zz")
    came_two = to_far_level(own_two)
    keep_a, sent = halve("zz", after(keep_a, own_two), came_a, "sum_a_z")
    came_a = to_far_level(sent)
    keep_b, sent = halve("zz", after(keep_b, keep_a), came_b, "sum_b_x")
    came_b = to_far_level(sent)
    own_two = join("zz", after(own_two, keep_b), came_two, "join_two_zz")
    came_two = to_level(own_two)
    own_a = finish(scale, after(keep_a, own_two), came_a, "sum_a_zz")
    came_a = to_far_level(own_a)
    own_b = finish(scale, after(keep_b, own_a), came_b, "sum_b_zz")
    came_b = to_far_level(own_b)
    own_two = join("z", after(own_two, own_b), came_two, "join_two_z")
    came_two = to_side(own_two)
    own_a = join("zz", after(own_a, own_two), came_a, "join_a_zz")
    came_a = to_level(own_a)
    own_b = join("zz", after(own_b, own_a), came_b, "join_b_zz")
    came_b = to_side(own_b)
    own_a = join("z", after(own_a, own_b), came_a, "join_a_z")
    came_a = to_side(own_a)
    own_b = join("x", after(own_b, own_a), came_b, "join_b_x")
    came_b = to_level(own_b)
    (input_grad,) = conv_call(
        "first_back_rim", "rim", "ready", finish_last, [narrow],
        [after(low_prior, own_b), high_prior], [own_ready], [begun], flipped=True,
    )
    own_two = join("x", after(own_two, input_grad), came_two, "join_two_x")
    came_two = to_core(own_two)
    own_a = join("x", after(own_a, own_two), came_a, "join_a_x")
    came_a = to_core(own_a)
    own_b = join("z", after(own_b, own_a), came_b, "join_b_z")
    came_b = to_core(own_b)
    summed_two = join_core(
        (0, 1, 4, 5, 2, 3, 6, 7), [(after(own_two, own_b), came_two)], "grads_two"
    )
    summed_one = join_core(
        tuple(range(8)), [(after(own_a, summed_two), came_a), (own_b, came_b)], "grads_one"
    )
    shape = filter_one.shape
    return output, input_grad, summed_one.reshape(shape), summed_two.reshape(shape)


def local(volume, filter_one, filter_two, cotangent):
    pair = lax.axis_size("chan") == 2 and lax.axis_size("dp") == 16
    if pair and volume.shape == (2, VOX, VOX, HALF):
        return paired(volume, filter_one, filter_two, cotangent)
    return plain(volume, filter_one, filter_two, cotangent)


def solution(mesh):
    in_specs = (
        P("dp", None, None, "chan"),
        P(None, None, None, "chan", None),
        P(None, None, None, "chan", None),
        P("dp", None, None, "chan"),
    )
    out_specs = (
        P("dp", None, None, "chan"),
        P("dp", None, None, "chan"),
        P(None, None, None, "chan", None),
        P(None, None, None, "chan", None),
    )
    return jax.shard_map(local, mesh=mesh, in_specs=in_specs, out_specs=out_specs, check_vma=False)
```

```python
import functools
import math

import jax
import jax.numpy as jnp
from jax import lax
from jax.experimental import pallas as pl
from jax.experimental.pallas import tpu as pltpu
from jax.sharding import PartitionSpec as P

VOX = 32
SLOPE = 0.3
HALF = 128
FULL = 256
TILE = 16
SMALL = 10**9
VMEM_LIMIT = 32 * 1024 * 1024


def extended(block, sides, width):
    for axis, dim in sides:
        count = lax.axis_size(axis)
        forward = [(i, i + 1) for i in range(count - 1)]
        forward.append((count - 1, 0))
        backward = [(target, source) for source, target in forward]
        low = lax.ppermute(
            lax.slice_in_dim(block, block.shape[dim] - width, None, axis=dim), axis, forward
        )
        high = lax.ppermute(lax.slice_in_dim(block, 0, width, axis=dim), axis, backward)
        block = jnp.concatenate([low, block, high], axis=dim)
    return block


def leaky(values):
    return jnp.where(values > 0, values, SLOPE * values)


def slope_of(values):
    return jnp.where(values > 0, jnp.float32(1.0), jnp.float32(SLOPE))


def tap_mask(rows, offset):
    base = lax.axis_index("dp") * rows
    total_rows = lax.axis_size("dp") * rows
    planes = jnp.mod(base + jnp.arange(rows, dtype=jnp.int32) - 1, total_rows)
    depth = jnp.mod(planes, VOX) + offset
    inside = jnp.logical_and(depth >= 0, depth < VOX)
    return inside[:, None, None, None]


def pad_plane(values):
    return jnp.pad(values, ((0, 0), (1, 1), (1, 1), (0, 0)))


def columns(plane, rows, height, breadth):
    taps = []
    for a in range(3):
        inside = tap_mask(rows, a - 1)
        depth_slab = plane[a : a + rows]
        depth_slab = jnp.where(inside, depth_slab, jnp.zeros_like(depth_slab))
        for b in range(3):
            for c in range(3):
                taps.append(depth_slab[:, b : b + height, c : c + breadth, :])
    stacked = jnp.concatenate(taps, axis=-1)
    return stacked.reshape(rows * height * breadth, stacked.shape[-1])


def plain(volume, filter_one, filter_two, cotangent):
    rows, height, breadth, narrow = volume.shape
    full = filter_one.shape[4]
    voxels = rows * height * breadth
    scale = 1.0 / math.sqrt(lax.axis_size("dp") * voxels)

    def forward(activity, weight):
        rim = extended(activity, (("dp", 0),), 1)
        plane = pad_plane(rim)
        stacked = columns(plane, rows, height, breadth)
        partial_value = jnp.dot(
            stacked, weight.reshape(27 * narrow, full), preferred_element_type=jnp.float32
        )
        summed = lax.psum_scatter(partial_value, "chan", scatter_dimension=1, tiled=True)
        return (plane, summed)

    def backward(plane, delta, weight):
        wide = lax.all_gather(delta, "chan", axis=3, tiled=True)
        rim = extended(wide, (("dp", 0),), 1)
        centre = rim[1 : rows + 1].reshape(voxels, full)
        stacked = columns(plane, rows, height, breadth)
        weight_grad = lax.dot_general(
            stacked, centre, (((0,), (0,)), ((), ())), preferred_element_type=jnp.float32
        )
        weight_grad = weight_grad.reshape(3, 3, 3, narrow, full)
        source = pad_plane(rim)
        total = jnp.zeros((rows, height, breadth, narrow), jnp.float32)
        for a in range(3):
            depth_slab = source[2 - a : 2 - a + rows]
            flat = depth_slab.reshape(-1, full)
            product = lax.dot_general(
                flat,
                weight[a].reshape(9 * narrow, full),
                (((1,), (1,)), ((), ())),
                preferred_element_type=jnp.float32,
            )
            product = product.reshape(rows, height + 2, breadth + 2, 9, narrow)
            part = jnp.zeros((rows, height, breadth, narrow), jnp.float32)
            for b in range(3):
                for c in range(3):
                    part = (
                        part
                        + product[:, 2 - b : 2 - b + height, 2 - c : 2 - c + breadth, b * 3 + c, :]
                    )
            inside = tap_mask(rows, 1 - a)
            total = total + jnp.where(inside, part, jnp.zeros_like(part))
        return (weight_grad, total.reshape(voxels, narrow))

    def layer_sum(weight_grad):
        return lax.psum(weight_grad, "dp")

    plane_one, pre_one = forward(volume, filter_one)
    act_one = leaky(pre_one).astype(jnp.bfloat16).reshape(rows, height, breadth, narrow)
    plane_two, pre_two = forward(act_one, filter_two)
    output = leaky(pre_two).astype(jnp.bfloat16).reshape(rows, height, breadth, narrow)
    delta_two = (cotangent.reshape(voxels, narrow).astype(jnp.float32) * slope_of(pre_two)).astype(
        jnp.bfloat16
    )
    local_two, back_two = backward(
        plane_two, delta_two.reshape(rows, height, breadth, narrow), filter_two
    )
    summed_two = layer_sum(local_two)
    delta_one = (back_two * slope_of(pre_one)).astype(jnp.bfloat16)
    local_one, back_one = backward(
        plane_one, delta_one.reshape(rows, height, breadth, narrow), filter_one
    )
    summed_one = layer_sum(local_one)
    input_grad = back_one.astype(jnp.bfloat16).reshape(rows, height, breadth, narrow)
    return (output, input_grad, summed_one * scale, summed_two * scale)


def is_seam():
    return lax.rem(lax.axis_index("dp") * 2, VOX) == 0


def place():
    at = lax.axis_index("dp")
    return at // 4, lax.rem(at // 2, 2), lax.rem(at, 2)


def place_bits():
    level, side, _ = place()
    return {"x": side, "z": lax.rem(level, 2), "zz": level // 2}


def shaped(values):
    return values.reshape(TILE, VOX, values.shape[1])


PARTS = {
    "all": dict(
        slots=((0, True), (1, True), (2, False), (1, False), (2, True), (3, True)),
        taps=(((0, 0), (1, 1), (2, 2)), ((0, 3), (1, 4), (2, 5))),
    ),
    "local": dict(
        slots=((0, True), (1, True), (0, False), (1, False)),
        taps=(((1, 0), (2, 3)), ((0, 2), (1, 1))),
    ),
    "rim": dict(
        slots=((0, True), (1, True)),
        taps=(((0, 0),), ((2, 1),)),
    ),
}


def filter_rows(kind):
    level, side, core = place()
    along, first = (side, 0) if kind == "quarters" else (lax.rem(level, 2), HALF)
    rows = [] if kind == "quarters" else [(HALF, 0)]
    if kind != "own":
        for unit in (core, 1 - core):
            rows += [(32, first + (2 * at + unit) * 32) for at in (along, 1 - along)]
    return rows


def copy_weights(kind, part, pieces, store, sems):
    me = lax.axis_index("chan")
    copies = []
    for (height, row), piece in zip(filter_rows(kind), pieces):
        if not isinstance(row, int):
            row = pl.multiple_of(row, 32)
        spans = ((0, 27),) if part != "rim" else ((0, 9), (18, 9))
        for side in range(2):
            column = pl.multiple_of((me if side == 0 else 1 - me) * HALF, HALF)
            for first, length in spans:
                taps = pl.ds(first, length)
                copies.append(
                    pltpu.make_async_copy(
                        piece.at[taps, :, pl.ds(column, HALF)],
                        store.at[taps, pl.ds(row, height), pl.ds(side * HALF, HALF)],
                        sems.at[len(copies)],
                    )
                )
    for copy in copies:
        copy.start()
    return copies


def fill_planes(part, planes, store, lane):
    lanes = pl.ds(lane, store.shape[3])
    edge = jnp.zeros(store.shape[2:], store.dtype)
    seam = is_seam()
    for slot, (plane, always) in enumerate(PARTS[part]["slots"]):
        ref, at = planes[plane]
        store[slot, 0] = edge
        store[slot, VOX + 1] = edge
        if always:
            store[slot, 1 : VOX + 1] = ref[at, :, :, lanes]
            continue

        @pl.when(seam)
        def _():
            store[slot] = jnp.zeros(store.shape[1:], store.dtype)

        @pl.when(jnp.logical_not(seam))
        def _():
            store[slot, 1 : VOX + 1] = ref[at, :, :, lanes]


def conv_rows(store, weights, taps, row, flipped, first):
    pieces = []
    for _, slot in taps:
        for b in range(3):
            piece = store[slot, pl.ds(row + b, TILE)]
            pieces.append(piece.reshape(TILE * VOX, store.shape[3]))
    stacked = jnp.concatenate(pieces, axis=1)
    products = []
    for c in range(3):
        if flipped:
            tiles = [weights[(2 - a) * 9 + (2 - b) * 3 + 2 - c] for a, _ in taps for b in range(3)]
            dims = (((1,), (1,)), ((), ()))
            tiles = jnp.concatenate(tiles, axis=1)
        else:
            rows = slice(first, first + store.shape[3])
            tiles = [weights[a * 9 + b * 3 + c, rows] for a, _ in taps for b in range(3)]
            dims = (((1,), (0,)), ((), ()))
            tiles = jnp.concatenate(tiles, axis=0)
        products.append(
            lax.dot_general(stacked, tiles, dims, preferred_element_type=jnp.float32)
        )
    left, middle, right = products
    column = lax.rem(lax.broadcasted_iota(jnp.int32, left.shape, 0), VOX)
    left = jnp.where(column > 0, pltpu.roll(left, 1, 0), 0.0)
    right = jnp.where(column < VOX - 1, pltpu.roll(right, TILE * VOX - 1, 0), 0.0)
    return middle + left + right


def conv_kernel(part, kind, flipped, finish, counts, lane, row, unroll, *refs):
    refs = list(refs)
    groups = []
    for count in counts:
        groups.append(refs[:count])
        refs = refs[count:]
    planes, pieces, begun, extra, outs = groups
    if kind == "ready":
        (weights,), copies = pieces, []
        (store,) = refs
    else:
        store, sems = refs
        weights = outs.pop()
        copies = copy_weights(kind, part, pieces, weights, sems)
    views = []
    for ref in planes:
        views += [(ref, at) for at in range(ref.shape[0])]
    fill_planes(part, views, store, lane)
    for copy in copies:
        copy.wait()
    for plane in range(2):
        taps = PARTS[part]["taps"][plane]

        @pl.loop(0, VOX // TILE, unroll=unroll)
        def _(step):
            rows = pl.ds(pl.multiple_of(step * TILE, TILE), TILE)
            value = shaped(conv_rows(store, weights, taps, step * TILE, flipped, row))
            if begun:
                value = value + begun[0][plane, rows]
            finish(value, plane, rows, extra, outs)


def finish_partial(value, plane, rows, extra, outs):
    outs[0][plane, rows] = value


def finish_first(value, plane, rows, extra, outs):
    outs[plane][0, rows] = leaky(value).astype(jnp.bfloat16)


def finish_second(value, plane, rows, extra, outs):
    output, deltas = outs[0], outs[1:]
    output[plane, rows] = leaky(value[:, :, :HALF]).astype(jnp.bfloat16)
    slope = slope_of(value)
    for lane, cot in ((0, extra[0]), (HALF, extra[1])):
        delta = cot[plane, rows].astype(jnp.float32) * slope[:, :, lane : lane + HALF]
        deltas[plane][0, rows, :, lane : lane + HALF] = delta.astype(jnp.bfloat16)


def finish_back(value, plane, rows, extra, outs):
    act = extra[plane][0, rows].astype(jnp.float32)
    outs[plane][0, rows] = (value * slope_of(act)).astype(jnp.bfloat16)


def finish_last(value, plane, rows, extra, outs):
    outs[0][plane, rows] = value.astype(jnp.bfloat16)


def filter_kernel(colours, *refs):
    low, mid_0, mid_1, high, delta_0, delta_1 = refs[:6]
    outs, (turned, moved) = refs[6:-2], refs[-2:]
    _, _, core = place()
    bits = place_bits()
    pixels = VOX * VOX
    seam = is_seam()
    sources = ((0, low), (1, mid_0), (2, mid_1), (3, high))
    for plane, ref in sources:
        flipped = ref[0].reshape(pixels, HALF).T
        for output_plane in range(2):
            tap = plane - output_plane
            if not 0 <= tap < 3:
                continue
            rows = slice(tap * HALF, (tap + 1) * HALF)
            columns = slice(output_plane * pixels, (output_plane + 1) * pixels)
            if plane in (1, 2) and tap != 1:
                turned[rows, columns] = jnp.where(seam, jnp.zeros_like(flipped), flipped)
            else:
                turned[rows, columns] = flipped
    for plane, ref in ((0, delta_0), (1, delta_1)):
        for c in range(3):
            moved[c, plane, 0] = jnp.zeros(moved.shape[3:], moved.dtype)
            moved[c, plane, VOX + 1] = jnp.zeros(moved.shape[3:], moved.dtype)
        moved[1, plane, 1 : VOX + 1] = ref[0]

        @pl.loop(0, VOX // TILE, unroll=True)
        def _(step):
            row = step * TILE
            values = ref[0, pl.ds(row, TILE)].reshape(TILE * VOX, FULL).astype(jnp.float32)
            column = lax.rem(lax.broadcasted_iota(jnp.int32, values.shape, 0), VOX)
            ahead = jnp.where(column < VOX - 1, pltpu.roll(values, TILE * VOX - 1, 0), 0.0)
            behind = jnp.where(column > 0, pltpu.roll(values, 1, 0), 0.0)
            moved[0, plane, pl.ds(row + 1, TILE)] = shaped(ahead.astype(jnp.bfloat16))
            moved[2, plane, pl.ds(row + 1, TILE)] = shaped(behind.astype(jnp.bfloat16))

    mine = lax.axis_index("chan") == core
    for tap in range(27):
        a, b, c = tap // 9, tap // 3 % 3, tap % 3
        if a:
            continue
        right = moved[c, :, 2 - b : 2 - b + VOX].reshape(2 * pixels, FULL)
        product = jnp.dot(turned[...], right, preferred_element_type=jnp.float32)
        kept = jnp.where(mine, product[:, :HALF], product[:, HALF:])
        sent = jnp.where(mine, product[:, HALF:], product[:, :HALF])
        for a in range(3):
            rows = slice(a * HALF, (a + 1) * HALF)
            for at, (first, taps, axis) in enumerate(colours):
                place_at = a * 9 + b * 3 + c - first
                if not 0 <= place_at < taps:
                    continue
                keep, far, near = outs[3 * at : 3 * at + 3]
                bit = bits[axis]
                keep[:, place_at] = kept[rows].reshape(8, 16, HALF)
                blocks = sent[rows].reshape(2, 4, 16, HALF).astype(far.dtype)
                far[:, place_at] = jnp.where(bit == 0, blocks[1], blocks[0])
                near[:, place_at] = jnp.where(bit == 0, blocks[0], blocks[1])


def halve_core_kernel(axis, keep, far, near, kept, sent):
    bit = place_bits()[axis]
    for target, came, first in ((kept, near, bit * 4), (sent, far, (1 - bit) * 4)):

        @pl.loop(0, 4)
        def _(block):
            total = keep[first + block] + came[block].astype(jnp.float32)
            target[block] = total.astype(target.dtype)


def halve_kernel(axis, keep, came, kept, sent):
    bit = place_bits()[axis]
    half = keep.shape[0] // 2
    for target, first in ((kept, bit * half), (sent, (1 - bit) * half)):
        for block in range(half):
            total = keep[first + block] + came[first + block].astype(jnp.float32)
            target[block] = total.astype(target.dtype)


def finish_kernel(scale, keep, came, total):
    total[...] = ((keep[...] + came[...].astype(jnp.float32)) * scale).astype(total.dtype)


def join_kernel(axis, own, came, target):
    bit = place_bits()[axis]
    half = own.shape[0]
    target[pl.ds(bit * half, half)] = own[...]
    target[pl.ds((1 - bit) * half, half)] = came[...]


def join_core_kernel(order, *refs):
    _, _, core = place()
    grad = refs[-1]
    first_tap = 0
    for own, came in zip(refs[0:-1:2], refs[1:-1:2]):
        base = first_tap
        first_tap += own.shape[1]

        @pl.loop(0, own.shape[1])
        def _(tap):
            for at, block in enumerate(order):
                rows = slice(block * 16, block * 16 + 16)
                first = jnp.where(core == 0, own[at, tap], came[at, tap])
                second = jnp.where(core == 0, came[at, tap], own[at, tap])
                grad[base + tap, rows, :HALF] = first.astype(jnp.float32)
                grad[base + tap, rows, HALF:] = second.astype(jnp.float32)


WEIGHT = {
    "sum_two_core": 0,
    "sum_two_z": 0,
    "sum_two_x": 2 * 10**9,
    "sum_a_core": 0,
    "sum_b_core": 0,
    "first_rim": 3 * 10**9,
    "back_rim": 10**9,
    "sum_a_zz": 2 * 10**9,
    "sum_b_zz": 2 * 10**9,
    "join_a_zz": 2 * 10**9,
    "join_b_zz": 2 * 10**9,
    "join_a_z": 6 * 10**9,
    "join_b_x": 6 * 10**9,
    "join_a_x": 6 * 10**9,
    "join_b_z": 6 * 10**9,
}


def hint(flops):
    return pl.CostEstimate(flops=flops, bytes_accessed=0, transcendentals=0)


def small_call(kernel, outs, operands, name):
    return pl.pallas_call(
        kernel,
        out_shape=[jax.ShapeDtypeStruct(shape, dtype) for shape, dtype in outs],
        in_specs=[pl.BlockSpec(memory_space=pltpu.VMEM)] * len(operands),
        out_specs=[pl.BlockSpec(memory_space=pltpu.VMEM)] * len(outs),
        compiler_params=pltpu.CompilerParams(vmem_limit_bytes=VMEM_LIMIT),
        cost_estimate=hint(WEIGHT.get(name, SMALL)),
        name=name,
    )(*operands)


def halve_core(axis, keep, far, near, name):
    outs = [(far.shape, jnp.float32), (far.shape, jnp.bfloat16)]
    return small_call(functools.partial(halve_core_kernel, axis), outs, [keep, far, near], name)


def halve(axis, keep, came, name):
    shape = (keep.shape[0] // 2,) + keep.shape[1:]
    outs = [(shape, jnp.float32), (shape, jnp.bfloat16)]
    return small_call(functools.partial(halve_kernel, axis), outs, [keep, came], name)


def finish(scale, keep, came, name):
    outs = [(keep.shape, jnp.bfloat16)]
    return small_call(functools.partial(finish_kernel, scale), outs, [keep, came], name)[0]


def join(axis, own, came, name):
    outs = [((2 * own.shape[0],) + own.shape[1:], jnp.bfloat16)]
    return small_call(functools.partial(join_kernel, axis), outs, [own, came], name)[0]


def join_core(order, colours, name):
    outs = [((27, HALF, FULL), jnp.float32)]
    operands = [half for pair in colours for half in pair]
    return small_call(functools.partial(join_core_kernel, order), outs, operands, name)[0]


def conv_call(
    name, part, kind, finish, outs, planes, pieces, begun=(), extra=(), flipped=False,
    lane=0, lanes=None, row=0, unroll=True,
):
    lanes = lanes or planes[0].shape[3]
    height = {"own": HALF, "quarters": HALF, "both": FULL, "ready": pieces[0].shape[1]}[kind]
    ready = kind == "ready"
    if not ready:
        outs = outs + [((27, height, FULL), jnp.bfloat16)]
    operands = [*planes, *pieces, *begun, *extra]
    counts = (len(planes), len(pieces), len(begun), len(extra), len(outs))
    specs = [pl.BlockSpec(memory_space=pltpu.VMEM) for _ in operands]
    if not ready:
        for at in range(len(planes), len(planes) + len(pieces)):
            own = kind != "quarters" and at == len(planes)
            specs[at] = pl.BlockSpec(memory_space=pltpu.HBM if own else pl.ANY)
    scratch = [pltpu.VMEM((len(PARTS[part]["slots"]), VOX + 2, VOX, lanes), jnp.bfloat16)]
    if not ready:
        scratch.append(pltpu.SemaphoreType.DMA((20,)))
    return pl.pallas_call(
        functools.partial(conv_kernel, part, kind, flipped, finish, counts, lane, row, unroll),
        out_shape=[jax.ShapeDtypeStruct(shape, dtype) for shape, dtype in outs],
        in_specs=specs,
        out_specs=[pl.BlockSpec(memory_space=pltpu.VMEM)] * len(outs),
        scratch_shapes=scratch,
        compiler_params=pltpu.CompilerParams(vmem_limit_bytes=VMEM_LIMIT),
        cost_estimate=hint(WEIGHT.get(name, 0)),
        name=name,
    )(*operands)


def filter_call(colours, planes, mid_at, deltas, name):
    narrow = (1, VOX, VOX, HALF)
    specs = [
        pl.BlockSpec(narrow, functools.partial(lambda at, i: (at, 0, 0, 0), at)) for at in mid_at
    ]
    specs += [pl.BlockSpec((1, VOX, VOX, FULL), lambda i: (0, 0, 0, 0))] * 2
    outs = []
    for _, taps, _ in colours:
        for blocks, dtype in ((8, jnp.float32), (4, jnp.bfloat16), (4, jnp.bfloat16)):
            outs.append(jax.ShapeDtypeStruct((blocks, taps, 16, HALF), dtype))
    values = pl.pallas_call(
        functools.partial(filter_kernel, colours),
        grid=(1,),
        out_shape=outs,
        in_specs=specs,
        out_specs=[pl.BlockSpec(out.shape, lambda i: (0, 0, 0, 0)) for out in outs],
        scratch_shapes=[
            pltpu.VMEM((3 * HALF, 2 * VOX * VOX), jnp.bfloat16),
            pltpu.VMEM((3, 2, VOX + 2, VOX, FULL), jnp.bfloat16),
        ],
        compiler_params=pltpu.CompilerParams(vmem_limit_bytes=VMEM_LIMIT),
        cost_estimate=hint(0),
        name=name,
    )(*planes, *deltas)
    return [values[at : at + 3] for at in range(0, len(values), 3)]


def after(value, *earlier):
    return lax.optimization_barrier((value,) + earlier)[0]


def paired(volume, filter_one, filter_two, cotangent):
    count = lax.axis_size("dp")
    ahead = [(i, (i + 1) % count) for i in range(count)]
    behind = [(target, source) for source, target in ahead]
    scale = 1.0 / math.sqrt(count * 2 * VOX * VOX)
    one = filter_one.reshape(27, HALF, FULL)
    two = filter_two.reshape(27, HALF, FULL)
    level, side, core = place()

    def other(values):
        return lax.ppermute(values, "chan", [(0, 1), (1, 0)])

    def to_core(values):
        return lax.ppermute(values, "dp", [(i, i ^ 1) for i in range(count)])

    def to_side(values):
        return lax.ppermute(values, "dp", [(i, i ^ 2) for i in range(count)])

    def to_level(values):
        return lax.ppermute(values, "dp", [(i, i ^ 4) for i in range(count)])

    def to_far_level(values):
        return lax.ppermute(values, "dp", [(i, i ^ 8) for i in range(count)])

    def rims(first, last):
        return lax.ppermute(last, "dp", ahead), lax.ppermute(first, "dp", behind)

    wide = ((1, VOX, VOX, FULL), jnp.bfloat16)
    narrow = ((2, VOX, VOX, HALF), jnp.bfloat16)
    partial = ((2, VOX, VOX, FULL), jnp.float32)
    half_partial = ((2, VOX, VOX, HALF), jnp.float32)

    low_own, high_own = rims(volume[:1], volume[1:])
    one_0 = other(lax.dynamic_slice_in_dim(one, (2 * side + core) * 32, 32, axis=1))
    volume_other = other(after(volume, one_0, low_own, high_own))
    one_1 = to_side(one_0)
    one_2 = to_core(one_0)
    begun, own_ready = conv_call(
        "first_own", "all", "own", finish_partial, [partial], [low_own, volume, high_own], [one],
        unroll=False,
    )
    one_3 = to_core(after(one_1, begun))
    quarters = [one_0, one_1, one_2, one_3]
    volume_other = after(volume_other, begun)
    two_0 = other(
        after(
            lax.dynamic_slice_in_dim(two, (2 * lax.rem(level, 2) + core) * 32, 32, axis=1),
            volume_other,
        )
    )
    low_other, high_other = rims(volume_other[:1], volume_other[1:])
    begun, ready = conv_call(
        "first_other", "local", "quarters", finish_partial, [partial], [volume_other], quarters,
        [begun],
    )
    two_0 = after(two_0, begun)
    two_1 = to_level(two_0)
    two_2 = to_core(two_0)
    cot_other = other(after(cotangent, two_0))
    act_0, act_1 = conv_call(
        "first_rim", "rim", "ready", finish_first, [wide, wide], [low_other, high_other],
        [ready], [begun],
    )
    low_act, high_act = rims(act_0, act_1)
    begun, _ = conv_call(
        "second_own", "local", "own", finish_partial, [partial], [act_0, act_1], [two], lanes=HALF,
        unroll=False,
    )
    two_3 = to_core(after(two_1, begun))
    pieces = [two, two_0, two_1, two_2, two_3]
    begun, ready = conv_call(
        "second_other", "local", "both", finish_partial, [partial], [act_0, act_1], pieces, [begun],
        lane=HALF, lanes=HALF, row=HALF,
    )
    output, delta_0, delta_1 = conv_call(
        "second_rim", "rim", "ready", finish_second, [narrow, wide, wide], [low_act, high_act],
        [ready], [begun], [cotangent, cot_other],
    )
    low_delta, high_delta = rims(delta_0, delta_1)
    ((keep, far, near),) = filter_call(
        ((0, 27, "z"),), [low_act, act_0, act_1, high_act], (0, 0, 0, 0), [delta_0, delta_1],
        "grad_two",
    )
    keep_two, sent = halve_core("z", keep, to_core(far), to_core(near), "sum_two_core")
    came_two = to_level(sent)
    (begun,) = conv_call(
        "back_local", "local", "ready", finish_partial, [partial], [delta_0, after(delta_1, keep_two)],
        [ready], flipped=True,
    )
    prior_0, prior_1 = conv_call(
        "back_rim", "rim", "ready", finish_back, [wide, wide], [low_delta, high_delta],
        [ready], [begun], [act_0, act_1], flipped=True,
    )
    low_prior, high_prior = rims(prior_0, prior_1)
    (keep_a, *sent_a), (keep_b, *sent_b) = filter_call(
        ((0, 14, "x"), (14, 13, "z")), [low_own, volume, volume, high_own], (0, 0, 1, 0),
        [prior_0, prior_1], "grad_one",
    )
    sent_a, sent_b = [to_core(half) for half in sent_a], [to_core(half) for half in sent_b]
    keep_two, sent = halve("x", after(keep_two, keep_a), came_two, "sum_two_z")
    came_two = to_side(sent)
    keep_a, sent = halve_core("x", after(keep_a, keep_two), *sent_a, "sum_a_core")
    came_a = to_side(sent)
    keep_b, sent = halve_core("z", after(keep_b, keep_a), *sent_b, "sum_b_core")
    came_b = to_level(sent)
    (begun,) = conv_call(
        "first_back_local", "local", "ready", finish_partial, [half_partial],
        [after(prior_0, keep_b), prior_1], [own_ready], flipped=True, unroll=False,
    )
    keep_two, sent = halve("zz", after(keep_two, begun, low_prior, high_prior), came_two, "sum_two_x")
    came_two = to_far_level(sent)
    keep_a, sent = halve("z", after(keep_a, keep_two), came_a, "sum_a_x")
    came_a = to_level(sent)
    keep_b, sent = halve("x", after(keep_b, keep_a), came_b, "sum_b_z")
    came_b = to_side(sent)
    own_two = finish(scale, after(keep_two, keep_b), came_two, "sum_two_zz")
    came_two = to_far_level(own_two)
    keep_a, sent = halve("zz", after(keep_a, own_two), came_a, "sum_a_z")
    came_a = to_far_level(sent)
    keep_b, sent = halve("zz", after(keep_b, keep_a), came_b, "sum_b_x")
    came_b = to_far_level(sent)
    own_two = join("zz", after(own_two, keep_b), came_two, "join_two_zz")
    came_two = to_level(own_two)
    own_a = finish(scale, after(keep_a, own_two), came_a, "sum_a_zz")
    came_a = to_far_level(own_a)
    own_b = finish(scale, after(keep_b, own_a), came_b, "sum_b_zz")
    came_b = to_far_level(own_b)
    own_two = join("z", after(own_two, own_b), came_two, "join_two_z")
    came_two = to_side(own_two)
    own_a = join("zz", after(own_a, own_two), came_a, "join_a_zz")
    came_a = to_level(own_a)
    own_b = join("zz", after(own_b, own_a), came_b, "join_b_zz")
    came_b = to_side(own_b)
    own_a = join("z", after(own_a, own_b), came_a, "join_a_z")
    came_a = to_side(own_a)
    own_b = join("x", after(own_b, own_a), came_b, "join_b_x")
    came_b = to_level(own_b)
    (input_grad,) = conv_call(
        "first_back_rim", "rim", "ready", finish_last, [narrow],
        [after(low_prior, own_b), high_prior], [own_ready], [begun], flipped=True,
    )
    own_two = join("x", after(own_two, input_grad), came_two, "join_two_x")
    came_two = to_core(own_two)
    own_a = join("x", after(own_a, own_two), came_a, "join_a_x")
    came_a = to_core(own_a)
    own_b = join("z", after(own_b, own_a), came_b, "join_b_z")
    came_b = to_core(own_b)
    summed_two = join_core(
        (0, 1, 4, 5, 2, 3, 6, 7), [(after(own_two, own_b), came_two)], "grads_two"
    )
    summed_one = join_core(
        tuple(range(8)), [(after(own_a, summed_two), came_a), (own_b, came_b)], "grads_one"
    )
    shape = filter_one.shape
    return output, input_grad, summed_one.reshape(shape), summed_two.reshape(shape)


def local(volume, filter_one, filter_two, cotangent):
    pair = lax.axis_size("chan") == 2 and lax.axis_size("dp") == 16
    if pair and volume.shape == (2, VOX, VOX, HALF):
        return paired(volume, filter_one, filter_two, cotangent)
    return plain(volume, filter_one, filter_two, cotangent)


def solution(mesh):
    in_specs = (
        P("dp", None, None, "chan"),
        P(None, None, None, "chan", None),
        P(None, None, None, "chan", None),
        P("dp", None, None, "chan"),
    )
    out_specs = (
        P("dp", None, None, "chan"),
        P("dp", None, None, "chan"),
        P(None, None, None, "chan", None),
        P(None, None, None, "chan", None),
    )
    return jax.shard_map(local, mesh=mesh, in_specs=in_specs, out_specs=out_specs, check_vma=False)
```

```python
import functools
import math

import jax
import jax.numpy as jnp
from jax import lax
from jax.experimental import pallas as pl
from jax.experimental.pallas import tpu as pltpu
from jax.sharding import PartitionSpec as P

VOX = 32
SLOPE = 0.3
HALF = 128
FULL = 256
TILE = 16
SMALL = 10**9
VMEM_LIMIT = 32 * 1024 * 1024


def extended(block, sides, width):
    for axis, dim in sides:
        count = lax.axis_size(axis)
        forward = [(i, i + 1) for i in range(count - 1)]
        forward.append((count - 1, 0))
        backward = [(target, source) for source, target in forward]
        low = lax.ppermute(
            lax.slice_in_dim(block, block.shape[dim] - width, None, axis=dim), axis, forward
        )
        high = lax.ppermute(lax.slice_in_dim(block, 0, width, axis=dim), axis, backward)
        block = jnp.concatenate([low, block, high], axis=dim)
    return block


def leaky(values):
    return jnp.where(values > 0, values, SLOPE * values)


def slope_of(values):
    return jnp.where(values > 0, jnp.float32(1.0), jnp.float32(SLOPE))


def tap_mask(rows, offset):
    base = lax.axis_index("dp") * rows
    total_rows = lax.axis_size("dp") * rows
    planes = jnp.mod(base + jnp.arange(rows, dtype=jnp.int32) - 1, total_rows)
    depth = jnp.mod(planes, VOX) + offset
    inside = jnp.logical_and(depth >= 0, depth < VOX)
    return inside[:, None, None, None]


def pad_plane(values):
    return jnp.pad(values, ((0, 0), (1, 1), (1, 1), (0, 0)))


def columns(plane, rows, height, breadth):
    taps = []
    for a in range(3):
        inside = tap_mask(rows, a - 1)
        depth_slab = plane[a : a + rows]
        depth_slab = jnp.where(inside, depth_slab, jnp.zeros_like(depth_slab))
        for b in range(3):
            for c in range(3):
                taps.append(depth_slab[:, b : b + height, c : c + breadth, :])
    stacked = jnp.concatenate(taps, axis=-1)
    return stacked.reshape(rows * height * breadth, stacked.shape[-1])


def plain(volume, filter_one, filter_two, cotangent):
    rows, height, breadth, narrow = volume.shape
    full = filter_one.shape[4]
    voxels = rows * height * breadth
    scale = 1.0 / math.sqrt(lax.axis_size("dp") * voxels)

    def forward(activity, weight):
        rim = extended(activity, (("dp", 0),), 1)
        plane = pad_plane(rim)
        stacked = columns(plane, rows, height, breadth)
        partial_value = jnp.dot(
            stacked, weight.reshape(27 * narrow, full), preferred_element_type=jnp.float32
        )
        summed = lax.psum_scatter(partial_value, "chan", scatter_dimension=1, tiled=True)
        return (plane, summed)

    def backward(plane, delta, weight):
        wide = lax.all_gather(delta, "chan", axis=3, tiled=True)
        rim = extended(wide, (("dp", 0),), 1)
        centre = rim[1 : rows + 1].reshape(voxels, full)
        stacked = columns(plane, rows, height, breadth)
        weight_grad = lax.dot_general(
            stacked, centre, (((0,), (0,)), ((), ())), preferred_element_type=jnp.float32
        )
        weight_grad = weight_grad.reshape(3, 3, 3, narrow, full)
        source = pad_plane(rim)
        total = jnp.zeros((rows, height, breadth, narrow), jnp.float32)
        for a in range(3):
            depth_slab = source[2 - a : 2 - a + rows]
            flat = depth_slab.reshape(-1, full)
            product = lax.dot_general(
                flat,
                weight[a].reshape(9 * narrow, full),
                (((1,), (1,)), ((), ())),
                preferred_element_type=jnp.float32,
            )
            product = product.reshape(rows, height + 2, breadth + 2, 9, narrow)
            part = jnp.zeros((rows, height, breadth, narrow), jnp.float32)
            for b in range(3):
                for c in range(3):
                    part = (
                        part
                        + product[:, 2 - b : 2 - b + height, 2 - c : 2 - c + breadth, b * 3 + c, :]
                    )
            inside = tap_mask(rows, 1 - a)
            total = total + jnp.where(inside, part, jnp.zeros_like(part))
        return (weight_grad, total.reshape(voxels, narrow))

    def layer_sum(weight_grad):
        return lax.psum(weight_grad, "dp")

    plane_one, pre_one = forward(volume, filter_one)
    act_one = leaky(pre_one).astype(jnp.bfloat16).reshape(rows, height, breadth, narrow)
    plane_two, pre_two = forward(act_one, filter_two)
    output = leaky(pre_two).astype(jnp.bfloat16).reshape(rows, height, breadth, narrow)
    delta_two = (cotangent.reshape(voxels, narrow).astype(jnp.float32) * slope_of(pre_two)).astype(
        jnp.bfloat16
    )
    local_two, back_two = backward(
        plane_two, delta_two.reshape(rows, height, breadth, narrow), filter_two
    )
    summed_two = layer_sum(local_two)
    delta_one = (back_two * slope_of(pre_one)).astype(jnp.bfloat16)
    local_one, back_one = backward(
        plane_one, delta_one.reshape(rows, height, breadth, narrow), filter_one
    )
    summed_one = layer_sum(local_one)
    input_grad = back_one.astype(jnp.bfloat16).reshape(rows, height, breadth, narrow)
    return (output, input_grad, summed_one * scale, summed_two * scale)


def is_seam():
    return lax.rem(lax.axis_index("dp") * 2, VOX) == 0


def place():
    at = lax.axis_index("dp")
    return at // 4, lax.rem(at // 2, 2), lax.rem(at, 2)


def place_bits():
    level, side, _ = place()
    return {"x": side, "z": lax.rem(level, 2), "zz": level // 2}


def shaped(values):
    return values.reshape(TILE, VOX, values.shape[1])


PARTS = {
    "all": dict(
        slots=((0, True), (1, True), (2, False), (1, False), (2, True), (3, True)),
        taps=(((0, 0), (1, 1), (2, 2)), ((0, 3), (1, 4), (2, 5))),
    ),
    "local": dict(
        slots=((0, True), (1, True), (0, False), (1, False)),
        taps=(((1, 0), (2, 3)), ((0, 2), (1, 1))),
    ),
    "rim": dict(
        slots=((0, True), (1, True)),
        taps=(((0, 0),), ((2, 1),)),
    ),
}


def filter_rows(kind):
    _, side, core = place()
    if kind == "own":
        return [(HALF, 0)]
    if kind == "both":
        return [(HALF, 0)] + [
            (32, HALF + unit * 64 + at) for unit in (core, 1 - core) for at in (0, 32)
        ]
    return [
        (32, (2 * along + unit) * 32) for unit in (core, 1 - core) for along in (side, 1 - side)
    ]


def copy_weights(kind, part, pieces, store, sems):
    me = lax.axis_index("chan")
    copies = []
    for (height, row), piece in zip(filter_rows(kind), pieces):
        if not isinstance(row, int):
            row = pl.multiple_of(row, 32)
        spans = ((0, 27),) if part != "rim" else ((0, 9), (18, 9))
        for side in range(2):
            column = pl.multiple_of((me if side == 0 else 1 - me) * HALF, HALF)
            for first, length in spans:
                taps = pl.ds(first, length)
                copies.append(
                    pltpu.make_async_copy(
                        piece.at[taps, :, pl.ds(column, HALF)],
                        store.at[taps, pl.ds(row, height), pl.ds(side * HALF, HALF)],
                        sems.at[len(copies)],
                    )
                )
    for copy in copies:
        copy.start()
    return copies


def fill_planes(part, planes, store, lane):
    lanes = pl.ds(lane, store.shape[3])
    edge = jnp.zeros(store.shape[2:], store.dtype)
    seam = is_seam()
    for slot, (plane, always) in enumerate(PARTS[part]["slots"]):
        ref, at = planes[plane]
        store[slot, 0] = edge
        store[slot, VOX + 1] = edge
        if always:
            store[slot, 1 : VOX + 1] = ref[at, :, :, lanes]
            continue

        @pl.when(seam)
        def _():
            store[slot] = jnp.zeros(store.shape[1:], store.dtype)

        @pl.when(jnp.logical_not(seam))
        def _():
            store[slot, 1 : VOX + 1] = ref[at, :, :, lanes]


def conv_rows(store, weights, taps, row, flipped, first):
    pieces = []
    for _, slot in taps:
        for b in range(3):
            piece = store[slot, pl.ds(row + b, TILE)]
            pieces.append(piece.reshape(TILE * VOX, store.shape[3]))
    stacked = jnp.concatenate(pieces, axis=1)
    products = []
    for c in range(3):
        if flipped:
            tiles = [weights[(2 - a) * 9 + (2 - b) * 3 + 2 - c] for a, _ in taps for b in range(3)]
            dims = (((1,), (1,)), ((), ()))
            tiles = jnp.concatenate(tiles, axis=1)
        else:
            rows = slice(first, first + store.shape[3])
            tiles = [weights[a * 9 + b * 3 + c, rows] for a, _ in taps for b in range(3)]
            dims = (((1,), (0,)), ((), ()))
            tiles = jnp.concatenate(tiles, axis=0)
        products.append(
            lax.dot_general(stacked, tiles, dims, preferred_element_type=jnp.float32)
        )
    left, middle, right = products
    column = lax.rem(lax.broadcasted_iota(jnp.int32, left.shape, 0), VOX)
    left = jnp.where(column > 0, pltpu.roll(left, 1, 0), 0.0)
    right = jnp.where(column < VOX - 1, pltpu.roll(right, TILE * VOX - 1, 0), 0.0)
    return middle + left + right


def conv_kernel(part, kind, flipped, finish, counts, lane, row, unroll, *refs):
    refs = list(refs)
    groups = []
    for count in counts:
        groups.append(refs[:count])
        refs = refs[count:]
    planes, pieces, begun, extra, outs = groups
    if kind == "ready":
        (weights,), copies = pieces, []
        (store,) = refs
    else:
        store, sems = refs
        weights = outs.pop()
        copies = copy_weights(kind, part, pieces, weights, sems)
    views = []
    for ref in planes:
        views += [(ref, at) for at in range(ref.shape[0])]
    fill_planes(part, views, store, lane)
    for copy in copies:
        copy.wait()
    for plane in range(2):
        taps = PARTS[part]["taps"][plane]

        @pl.loop(0, VOX // TILE, unroll=unroll)
        def _(step):
            rows = pl.ds(pl.multiple_of(step * TILE, TILE), TILE)
            value = shaped(conv_rows(store, weights, taps, step * TILE, flipped, row))
            if begun:
                value = value + begun[0][plane, rows]
            finish(value, plane, rows, extra, outs)


def finish_partial(value, plane, rows, extra, outs):
    outs[0][plane, rows] = value


def finish_first(value, plane, rows, extra, outs):
    outs[plane][0, rows] = leaky(value).astype(jnp.bfloat16)


def finish_second(value, plane, rows, extra, outs):
    output, deltas = outs[0], outs[1:]
    output[plane, rows] = leaky(value[:, :, :HALF]).astype(jnp.bfloat16)
    slope = slope_of(value)
    for lane, cot in ((0, extra[0]), (HALF, extra[1])):
        delta = cot[plane, rows].astype(jnp.float32) * slope[:, :, lane : lane + HALF]
        deltas[plane][0, rows, :, lane : lane + HALF] = delta.astype(jnp.bfloat16)


def finish_back(value, plane, rows, extra, outs):
    act = extra[plane][0, rows].astype(jnp.float32)
    outs[plane][0, rows] = (value * slope_of(act)).astype(jnp.bfloat16)


def finish_last(value, plane, rows, extra, outs):
    outs[0][plane, rows] = value.astype(jnp.bfloat16)


def filter_kernel(colours, *refs):
    low, mid_0, mid_1, high, delta_0, delta_1 = refs[:6]
    outs, (turned, moved) = refs[6:-2], refs[-2:]
    _, _, core = place()
    bits = place_bits()
    pixels = VOX * VOX
    seam = is_seam()
    sources = ((0, low), (1, mid_0), (2, mid_1), (3, high))
    for plane, ref in sources:
        flipped = ref[0].reshape(pixels, HALF).T
        for output_plane in range(2):
            tap = plane - output_plane
            if not 0 <= tap < 3:
                continue
            rows = slice(tap * HALF, (tap + 1) * HALF)
            columns = slice(output_plane * pixels, (output_plane + 1) * pixels)
            if plane in (1, 2) and tap != 1:
                turned[rows, columns] = jnp.where(seam, jnp.zeros_like(flipped), flipped)
            else:
                turned[rows, columns] = flipped
    for plane, ref in ((0, delta_0), (1, delta_1)):
        for c in range(3):
            moved[c, plane, 0] = jnp.zeros(moved.shape[3:], moved.dtype)
            moved[c, plane, VOX + 1] = jnp.zeros(moved.shape[3:], moved.dtype)
        moved[1, plane, 1 : VOX + 1] = ref[0]

        @pl.loop(0, VOX // TILE, unroll=True)
        def _(step):
            row = step * TILE
            values = ref[0, pl.ds(row, TILE)].reshape(TILE * VOX, FULL).astype(jnp.float32)
            column = lax.rem(lax.broadcasted_iota(jnp.int32, values.shape, 0), VOX)
            ahead = jnp.where(column < VOX - 1, pltpu.roll(values, TILE * VOX - 1, 0), 0.0)
            behind = jnp.where(column > 0, pltpu.roll(values, 1, 0), 0.0)
            moved[0, plane, pl.ds(row + 1, TILE)] = shaped(ahead.astype(jnp.bfloat16))
            moved[2, plane, pl.ds(row + 1, TILE)] = shaped(behind.astype(jnp.bfloat16))

    mine = lax.axis_index("chan") == core
    for tap in range(27):
        a, b, c = tap // 9, tap // 3 % 3, tap % 3
        if a:
            continue
        right = moved[c, :, 2 - b : 2 - b + VOX].reshape(2 * pixels, FULL)
        product = jnp.dot(turned[...], right, preferred_element_type=jnp.float32)
        kept = jnp.where(mine, product[:, :HALF], product[:, HALF:])
        sent = jnp.where(mine, product[:, HALF:], product[:, :HALF])
        for a in range(3):
            rows = slice(a * HALF, (a + 1) * HALF)
            for at, (first, taps, axis) in enumerate(colours):
                place_at = a * 9 + b * 3 + c - first
                if not 0 <= place_at < taps:
                    continue
                keep, far, near = outs[3 * at : 3 * at + 3]
                bit = bits[axis]
                keep[:, place_at] = kept[rows].reshape(8, 16, HALF)
                blocks = sent[rows].reshape(2, 4, 16, HALF).astype(far.dtype)
                far[:, place_at] = jnp.where(bit == 0, blocks[1], blocks[0])
                near[:, place_at] = jnp.where(bit == 0, blocks[0], blocks[1])


def halve_core_kernel(axis, keep, far, near, kept, sent):
    bit = place_bits()[axis]
    for target, came, first in ((kept, near, bit * 4), (sent, far, (1 - bit) * 4)):

        @pl.loop(0, 4)
        def _(block):
            total = keep[first + block] + came[block].astype(jnp.float32)
            target[block] = total.astype(target.dtype)


def halve_kernel(axis, keep, came, kept, sent):
    bit = place_bits()[axis]
    half = keep.shape[0] // 2
    for target, first in ((kept, bit * half), (sent, (1 - bit) * half)):
        for block in range(half):
            total = keep[first + block] + came[first + block].astype(jnp.float32)
            target[block] = total.astype(target.dtype)


def finish_kernel(scale, keep, came, total):
    total[...] = ((keep[...] + came[...].astype(jnp.float32)) * scale).astype(total.dtype)


def join_kernel(axis, own, came, target):
    bit = place_bits()[axis]
    half = own.shape[0]
    target[pl.ds(bit * half, half)] = own[...]
    target[pl.ds((1 - bit) * half, half)] = came[...]


def join_core_kernel(order, *refs):
    _, _, core = place()
    grad = refs[-1]
    first_tap = 0
    for own, came in zip(refs[0:-1:2], refs[1:-1:2]):
        base = first_tap
        first_tap += own.shape[1]

        @pl.loop(0, own.shape[1])
        def _(tap):
            for at, block in enumerate(order):
                rows = slice(block * 16, block * 16 + 16)
                first = jnp.where(core == 0, own[at, tap], came[at, tap])
                second = jnp.where(core == 0, came[at, tap], own[at, tap])
                grad[base + tap, rows, :HALF] = first.astype(jnp.float32)
                grad[base + tap, rows, HALF:] = second.astype(jnp.float32)


WEIGHT = {
    "sum_two_core": 0,
    "sum_two_z": 0,
    "sum_two_x": 2 * 10**9,
    "sum_a_core": 0,
    "sum_b_core": 0,
    "first_rim": 3 * 10**9,
    "back_rim": 10**9,
    "sum_a_zz": 2 * 10**9,
    "sum_b_zz": 2 * 10**9,
    "join_a_zz": 2 * 10**9,
    "join_b_zz": 2 * 10**9,
    "join_a_z": 6 * 10**9,
    "join_b_x": 6 * 10**9,
    "join_a_x": 6 * 10**9,
    "join_b_z": 6 * 10**9,
}


def hint(flops):
    return pl.CostEstimate(flops=flops, bytes_accessed=0, transcendentals=0)


def small_call(kernel, outs, operands, name):
    return pl.pallas_call(
        kernel,
        out_shape=[jax.ShapeDtypeStruct(shape, dtype) for shape, dtype in outs],
        in_specs=[pl.BlockSpec(memory_space=pltpu.VMEM)] * len(operands),
        out_specs=[pl.BlockSpec(memory_space=pltpu.VMEM)] * len(outs),
        compiler_params=pltpu.CompilerParams(vmem_limit_bytes=VMEM_LIMIT),
        cost_estimate=hint(WEIGHT.get(name, SMALL)),
        name=name,
    )(*operands)


def halve_core(axis, keep, far, near, name):
    outs = [(far.shape, jnp.float32), (far.shape, jnp.bfloat16)]
    return small_call(functools.partial(halve_core_kernel, axis), outs, [keep, far, near], name)


def halve(axis, keep, came, name):
    shape = (keep.shape[0] // 2,) + keep.shape[1:]
    outs = [(shape, jnp.float32), (shape, jnp.bfloat16)]
    return small_call(functools.partial(halve_kernel, axis), outs, [keep, came], name)


def finish(scale, keep, came, name):
    outs = [(keep.shape, jnp.bfloat16)]
    return small_call(functools.partial(finish_kernel, scale), outs, [keep, came], name)[0]


def join(axis, own, came, name):
    outs = [((2 * own.shape[0],) + own.shape[1:], jnp.bfloat16)]
    return small_call(functools.partial(join_kernel, axis), outs, [own, came], name)[0]


def join_core(order, colours, name):
    outs = [((27, HALF, FULL), jnp.float32)]
    operands = [half for pair in colours for half in pair]
    return small_call(functools.partial(join_core_kernel, order), outs, operands, name)[0]


def conv_call(
    name, part, kind, finish, outs, planes, pieces, begun=(), extra=(), flipped=False,
    lane=0, lanes=None, row=0, unroll=True,
):
    lanes = lanes or planes[0].shape[3]
    height = {"own": HALF, "quarters": HALF, "both": FULL, "ready": pieces[0].shape[1]}[kind]
    ready = kind == "ready"
    if not ready:
        outs = outs + [((27, height, FULL), jnp.bfloat16)]
    operands = [*planes, *pieces, *begun, *extra]
    counts = (len(planes), len(pieces), len(begun), len(extra), len(outs))
    specs = [pl.BlockSpec(memory_space=pltpu.VMEM) for _ in operands]
    if not ready:
        for at in range(len(planes), len(planes) + len(pieces)):
            own = kind != "quarters" and at == len(planes)
            specs[at] = pl.BlockSpec(memory_space=pltpu.HBM if own else pl.ANY)
    scratch = [pltpu.VMEM((len(PARTS[part]["slots"]), VOX + 2, VOX, lanes), jnp.bfloat16)]
    if not ready:
        scratch.append(pltpu.SemaphoreType.DMA((20,)))
    return pl.pallas_call(
        functools.partial(conv_kernel, part, kind, flipped, finish, counts, lane, row, unroll),
        out_shape=[jax.ShapeDtypeStruct(shape, dtype) for shape, dtype in outs],
        in_specs=specs,
        out_specs=[pl.BlockSpec(memory_space=pltpu.VMEM)] * len(outs),
        scratch_shapes=scratch,
        compiler_params=pltpu.CompilerParams(vmem_limit_bytes=VMEM_LIMIT),
        cost_estimate=hint(WEIGHT.get(name, 0)),
        name=name,
    )(*operands)


def filter_call(colours, planes, mid_at, deltas, name):
    narrow = (1, VOX, VOX, HALF)
    specs = [
        pl.BlockSpec(narrow, functools.partial(lambda at, i: (at, 0, 0, 0), at)) for at in mid_at
    ]
    specs += [pl.BlockSpec((1, VOX, VOX, FULL), lambda i: (0, 0, 0, 0))] * 2
    outs = []
    for _, taps, _ in colours:
        for blocks, dtype in ((8, jnp.float32), (4, jnp.bfloat16), (4, jnp.bfloat16)):
            outs.append(jax.ShapeDtypeStruct((blocks, taps, 16, HALF), dtype))
    values = pl.pallas_call(
        functools.partial(filter_kernel, colours),
        grid=(1,),
        out_shape=outs,
        in_specs=specs,
        out_specs=[pl.BlockSpec(out.shape, lambda i: (0, 0, 0, 0)) for out in outs],
        scratch_shapes=[
            pltpu.VMEM((3 * HALF, 2 * VOX * VOX), jnp.bfloat16),
            pltpu.VMEM((3, 2, VOX + 2, VOX, FULL), jnp.bfloat16),
        ],
        compiler_params=pltpu.CompilerParams(vmem_limit_bytes=VMEM_LIMIT),
        cost_estimate=hint(0),
        name=name,
    )(*planes, *deltas)
    return [values[at : at + 3] for at in range(0, len(values), 3)]


def after(value, *earlier):
    return lax.optimization_barrier((value,) + earlier)[0]


def paired(volume, filter_one, filter_two, cotangent):
    count = lax.axis_size("dp")
    ahead = [(i, (i + 1) % count) for i in range(count)]
    behind = [(target, source) for source, target in ahead]
    scale = 1.0 / math.sqrt(count * 2 * VOX * VOX)
    one = filter_one.reshape(27, HALF, FULL)
    two = filter_two.reshape(27, HALF, FULL)
    _, side, core = place()

    def other(values):
        return lax.ppermute(values, "chan", [(0, 1), (1, 0)])

    def to_core(values):
        return lax.ppermute(values, "dp", [(i, i ^ 1) for i in range(count)])

    def to_side(values):
        return lax.ppermute(values, "dp", [(i, i ^ 2) for i in range(count)])

    def to_level(values):
        return lax.ppermute(values, "dp", [(i, i ^ 4) for i in range(count)])

    def to_far_level(values):
        return lax.ppermute(values, "dp", [(i, i ^ 8) for i in range(count)])

    def rims(first, last):
        return lax.ppermute(last, "dp", ahead), lax.ppermute(first, "dp", behind)

    wide = ((1, VOX, VOX, FULL), jnp.bfloat16)
    narrow = ((2, VOX, VOX, HALF), jnp.bfloat16)
    partial = ((2, VOX, VOX, FULL), jnp.float32)
    half_partial = ((2, VOX, VOX, HALF), jnp.float32)

    low_own, high_own = rims(volume[:1], volume[1:])
    one_0 = other(lax.dynamic_slice_in_dim(one, (2 * side + core) * 32, 32, axis=1))
    volume_other = other(after(volume, one_0, low_own, high_own))
    one_1 = to_side(one_0)
    one_2 = to_core(one_0)
    begun, own_ready = conv_call(
        "first_own", "all", "own", finish_partial, [partial], [low_own, volume, high_own], [one],
        unroll=False,
    )
    one_3 = to_core(after(one_1, begun))
    quarters = [one_0, one_1, one_2, one_3]
    volume_other = after(volume_other, begun)
    two_came = [
        other(after(lax.dynamic_slice_in_dim(two, core * 64 + at, 32, axis=1), volume_other))
        for at in (0, 32)
    ]
    low_other, high_other = rims(volume_other[:1], volume_other[1:])
    begun, ready = conv_call(
        "first_other", "local", "quarters", finish_partial, [partial], [volume_other], quarters,
        [begun],
    )
    act_0, act_1 = conv_call(
        "first_rim", "rim", "ready", finish_first, [wide, wide], [low_other, high_other],
        [ready], [begun],
    )
    low_act, high_act = rims(act_0, act_1)
    cot_other = other(after(cotangent, act_0))
    begun, _ = conv_call(
        "second_own", "local", "own", finish_partial, [partial], [act_0, act_1], [two], lanes=HALF,
        unroll=False,
    )
    two_came = [after(part, begun) for part in two_came]
    pieces = [two] + two_came + [to_core(part) for part in two_came]
    begun, ready = conv_call(
        "second_other", "local", "both", finish_partial, [partial], [act_0, act_1], pieces, [begun],
        lane=HALF, lanes=HALF, row=HALF,
    )
    output, delta_0, delta_1 = conv_call(
        "second_rim", "rim", "ready", finish_second, [narrow, wide, wide], [low_act, high_act],
        [ready], [begun], [cotangent, cot_other],
    )
    low_delta, high_delta = rims(delta_0, delta_1)
    ((keep, far, near),) = filter_call(
        ((0, 27, "z"),), [low_act, act_0, act_1, high_act], (0, 0, 0, 0), [delta_0, delta_1],
        "grad_two",
    )
    keep_two, sent = halve_core("z", keep, to_core(far), to_core(near), "sum_two_core")
    came_two = to_level(sent)
    (begun,) = conv_call(
        "back_local", "local", "ready", finish_partial, [partial], [delta_0, after(delta_1, keep_two)],
        [ready], flipped=True,
    )
    prior_0, prior_1 = conv_call(
        "back_rim", "rim", "ready", finish_back, [wide, wide], [low_delta, high_delta],
        [ready], [begun], [act_0, act_1], flipped=True,
    )
    low_prior, high_prior = rims(prior_0, prior_1)
    (keep_a, *sent_a), (keep_b, *sent_b) = filter_call(
        ((0, 14, "x"), (14, 13, "z")), [low_own, volume, volume, high_own], (0, 0, 1, 0),
        [prior_0, prior_1], "grad_one",
    )
    sent_a, sent_b = [to_core(half) for half in sent_a], [to_core(half) for half in sent_b]
    keep_two, sent = halve("x", after(keep_two, keep_a), came_two, "sum_two_z")
    came_two = to_side(sent)
    keep_a, sent = halve_core("x", after(keep_a, keep_two), *sent_a, "sum_a_core")
    came_a = to_side(sent)
    keep_b, sent = halve_core("z", after(keep_b, keep_a), *sent_b, "sum_b_core")
    came_b = to_level(sent)
    (begun,) = conv_call(
        "first_back_local", "local", "ready", finish_partial, [half_partial],
        [after(prior_0, keep_b), prior_1], [own_ready], flipped=True, unroll=False,
    )
    keep_two, sent = halve("zz", after(keep_two, begun, low_prior, high_prior), came_two, "sum_two_x")
    came_two = to_far_level(sent)
    keep_a, sent = halve("z", after(keep_a, keep_two), came_a, "sum_a_x")
    came_a = to_level(sent)
    keep_b, sent = halve("x", after(keep_b, keep_a), came_b, "sum_b_z")
    came_b = to_side(sent)
    own_two = finish(scale, after(keep_two, keep_b), came_two, "sum_two_zz")
    came_two = to_far_level(own_two)
    keep_a, sent = halve("zz", after(keep_a, own_two), came_a, "sum_a_z")
    came_a = to_far_level(sent)
    keep_b, sent = halve("zz", after(keep_b, keep_a), came_b, "sum_b_x")
    came_b = to_far_level(sent)
    own_two = join("zz", after(own_two, keep_b), came_two, "join_two_zz")
    came_two = to_level(own_two)
    own_a = finish(scale, after(keep_a, own_two), came_a, "sum_a_zz")
    came_a = to_far_level(own_a)
    own_b = finish(scale, after(keep_b, own_a), came_b, "sum_b_zz")
    came_b = to_far_level(own_b)
    own_two = join("z", after(own_two, own_b), came_two, "join_two_z")
    came_two = to_side(own_two)
    own_a = join("zz", after(own_a, own_two), came_a, "join_a_zz")
    came_a = to_level(own_a)
    own_b = join("zz", after(own_b, own_a), came_b, "join_b_zz")
    came_b = to_side(own_b)
    own_a = join("z", after(own_a, own_b), came_a, "join_a_z")
    came_a = to_side(own_a)
    own_b = join("x", after(own_b, own_a), came_b, "join_b_x")
    came_b = to_level(own_b)
    (input_grad,) = conv_call(
        "first_back_rim", "rim", "ready", finish_last, [narrow],
        [after(low_prior, own_b), high_prior], [own_ready], [begun], flipped=True,
    )
    own_two = join("x", after(own_two, input_grad), came_two, "join_two_x")
    came_two = to_core(own_two)
    own_a = join("x", after(own_a, own_two), came_a, "join_a_x")
    came_a = to_core(own_a)
    own_b = join("z", after(own_b, own_a), came_b, "join_b_z")
    came_b = to_core(own_b)
    summed_two = join_core(
        (0, 1, 4, 5, 2, 3, 6, 7), [(after(own_two, own_b), came_two)], "grads_two"
    )
    summed_one = join_core(
        tuple(range(8)), [(after(own_a, summed_two), came_a), (own_b, came_b)], "grads_one"
    )
    shape = filter_one.shape
    return output, input_grad, summed_one.reshape(shape), summed_two.reshape(shape)


def local(volume, filter_one, filter_two, cotangent):
    pair = lax.axis_size("chan") == 2 and lax.axis_size("dp") == 16
    if pair and volume.shape == (2, VOX, VOX, HALF):
        return paired(volume, filter_one, filter_two, cotangent)
    return plain(volume, filter_one, filter_two, cotangent)


def solution(mesh):
    in_specs = (
        P("dp", None, None, "chan"),
        P(None, None, None, "chan", None),
        P(None, None, None, "chan", None),
        P("dp", None, None, "chan"),
    )
    out_specs = (
        P("dp", None, None, "chan"),
        P("dp", None, None, "chan"),
        P(None, None, None, "chan", None),
        P(None, None, None, "chan", None),
    )
    return jax.shard_map(local, mesh=mesh, in_specs=in_specs, out_specs=out_specs, check_vma=False)
```

```python
import functools
import math

import jax
import jax.numpy as jnp
from jax import lax
from jax.experimental import pallas as pl
from jax.experimental.pallas import tpu as pltpu
from jax.sharding import PartitionSpec as P

VOX = 32
SLOPE = 0.3
HALF = 128
FULL = 256
TILE = 16
SMALL = 10**9
VMEM_LIMIT = 32 * 1024 * 1024


def extended(block, sides, width):
    for axis, dim in sides:
        count = lax.axis_size(axis)
        forward = [(i, i + 1) for i in range(count - 1)]
        forward.append((count - 1, 0))
        backward = [(target, source) for source, target in forward]
        low = lax.ppermute(
            lax.slice_in_dim(block, block.shape[dim] - width, None, axis=dim), axis, forward
        )
        high = lax.ppermute(lax.slice_in_dim(block, 0, width, axis=dim), axis, backward)
        block = jnp.concatenate([low, block, high], axis=dim)
    return block


def leaky(values):
    return jnp.where(values > 0, values, SLOPE * values)


def slope_of(values):
    return jnp.where(values > 0, jnp.float32(1.0), jnp.float32(SLOPE))


def tap_mask(rows, offset):
    base = lax.axis_index("dp") * rows
    total_rows = lax.axis_size("dp") * rows
    planes = jnp.mod(base + jnp.arange(rows, dtype=jnp.int32) - 1, total_rows)
    depth = jnp.mod(planes, VOX) + offset
    inside = jnp.logical_and(depth >= 0, depth < VOX)
    return inside[:, None, None, None]


def pad_plane(values):
    return jnp.pad(values, ((0, 0), (1, 1), (1, 1), (0, 0)))


def columns(plane, rows, height, breadth):
    taps = []
    for a in range(3):
        inside = tap_mask(rows, a - 1)
        depth_slab = plane[a : a + rows]
        depth_slab = jnp.where(inside, depth_slab, jnp.zeros_like(depth_slab))
        for b in range(3):
            for c in range(3):
                taps.append(depth_slab[:, b : b + height, c : c + breadth, :])
    stacked = jnp.concatenate(taps, axis=-1)
    return stacked.reshape(rows * height * breadth, stacked.shape[-1])


def plain(volume, filter_one, filter_two, cotangent):
    rows, height, breadth, narrow = volume.shape
    full = filter_one.shape[4]
    voxels = rows * height * breadth
    scale = 1.0 / math.sqrt(lax.axis_size("dp") * voxels)

    def forward(activity, weight):
        rim = extended(activity, (("dp", 0),), 1)
        plane = pad_plane(rim)
        stacked = columns(plane, rows, height, breadth)
        partial_value = jnp.dot(
            stacked, weight.reshape(27 * narrow, full), preferred_element_type=jnp.float32
        )
        summed = lax.psum_scatter(partial_value, "chan", scatter_dimension=1, tiled=True)
        return (plane, summed)

    def backward(plane, delta, weight):
        wide = lax.all_gather(delta, "chan", axis=3, tiled=True)
        rim = extended(wide, (("dp", 0),), 1)
        centre = rim[1 : rows + 1].reshape(voxels, full)
        stacked = columns(plane, rows, height, breadth)
        weight_grad = lax.dot_general(
            stacked, centre, (((0,), (0,)), ((), ())), preferred_element_type=jnp.float32
        )
        weight_grad = weight_grad.reshape(3, 3, 3, narrow, full)
        source = pad_plane(rim)
        total = jnp.zeros((rows, height, breadth, narrow), jnp.float32)
        for a in range(3):
            depth_slab = source[2 - a : 2 - a + rows]
            flat = depth_slab.reshape(-1, full)
            product = lax.dot_general(
                flat,
                weight[a].reshape(9 * narrow, full),
                (((1,), (1,)), ((), ())),
                preferred_element_type=jnp.float32,
            )
            product = product.reshape(rows, height + 2, breadth + 2, 9, narrow)
            part = jnp.zeros((rows, height, breadth, narrow), jnp.float32)
            for b in range(3):
                for c in range(3):
                    part = (
                        part
                        + product[:, 2 - b : 2 - b + height, 2 - c : 2 - c + breadth, b * 3 + c, :]
                    )
            inside = tap_mask(rows, 1 - a)
            total = total + jnp.where(inside, part, jnp.zeros_like(part))
        return (weight_grad, total.reshape(voxels, narrow))

    def layer_sum(weight_grad):
        return lax.psum(weight_grad, "dp")

    plane_one, pre_one = forward(volume, filter_one)
    act_one = leaky(pre_one).astype(jnp.bfloat16).reshape(rows, height, breadth, narrow)
    plane_two, pre_two = forward(act_one, filter_two)
    output = leaky(pre_two).astype(jnp.bfloat16).reshape(rows, height, breadth, narrow)
    delta_two = (cotangent.reshape(voxels, narrow).astype(jnp.float32) * slope_of(pre_two)).astype(
        jnp.bfloat16
    )
    local_two, back_two = backward(
        plane_two, delta_two.reshape(rows, height, breadth, narrow), filter_two
    )
    summed_two = layer_sum(local_two)
    delta_one = (back_two * slope_of(pre_one)).astype(jnp.bfloat16)
    local_one, back_one = backward(
        plane_one, delta_one.reshape(rows, height, breadth, narrow), filter_one
    )
    summed_one = layer_sum(local_one)
    input_grad = back_one.astype(jnp.bfloat16).reshape(rows, height, breadth, narrow)
    return (output, input_grad, summed_one * scale, summed_two * scale)


def is_seam():
    return lax.rem(lax.axis_index("dp") * 2, VOX) == 0


def place():
    at = lax.axis_index("dp")
    return at // 4, lax.rem(at // 2, 2), lax.rem(at, 2)


def place_bits():
    level, side, _ = place()
    return {"x": side, "z": lax.rem(level, 2), "zz": level // 2}


def shaped(values):
    return values.reshape(TILE, VOX, values.shape[1])


PARTS = {
    "all": dict(
        slots=((0, True), (1, True), (2, False), (1, False), (2, True), (3, True)),
        taps=(((0, 0), (1, 1), (2, 2)), ((0, 3), (1, 4), (2, 5))),
    ),
    "local": dict(
        slots=((0, True), (1, True), (0, False), (1, False)),
        taps=(((1, 0), (2, 3)), ((0, 2), (1, 1))),
    ),
    "rim": dict(
        slots=((0, True), (1, True)),
        taps=(((0, 0),), ((2, 1),)),
    ),
}


def filter_rows(kind):
    _, side, core = place()
    if kind == "own":
        return [(HALF, 0)]
    if kind == "both":
        return [(HALF, 0)] + [
            (32, HALF + unit * 64 + at) for unit in (core, 1 - core) for at in (0, 32)
        ]
    return [
        (32, (2 * along + unit) * 32) for unit in (core, 1 - core) for along in (side, 1 - side)
    ]


def copy_weights(kind, part, pieces, store, sems):
    me = lax.axis_index("chan")
    copies = []
    for (height, row), piece in zip(filter_rows(kind), pieces):
        if not isinstance(row, int):
            row = pl.multiple_of(row, 32)
        spans = ((0, 27),) if part != "rim" else ((0, 9), (18, 9))
        for side in range(2):
            column = pl.multiple_of((me if side == 0 else 1 - me) * HALF, HALF)
            for first, length in spans:
                taps = pl.ds(first, length)
                copies.append(
                    pltpu.make_async_copy(
                        piece.at[taps, :, pl.ds(column, HALF)],
                        store.at[taps, pl.ds(row, height), pl.ds(side * HALF, HALF)],
                        sems.at[len(copies)],
                    )
                )
    for copy in copies:
        copy.start()
    return copies


def fill_planes(part, planes, store, lane):
    lanes = pl.ds(lane, store.shape[3])
    edge = jnp.zeros(store.shape[2:], store.dtype)
    seam = is_seam()
    for slot, (plane, always) in enumerate(PARTS[part]["slots"]):
        ref, at = planes[plane]
        store[slot, 0] = edge
        store[slot, VOX + 1] = edge
        if always:
            store[slot, 1 : VOX + 1] = ref[at, :, :, lanes]
            continue

        @pl.when(seam)
        def _():
            store[slot] = jnp.zeros(store.shape[1:], store.dtype)

        @pl.when(jnp.logical_not(seam))
        def _():
            store[slot, 1 : VOX + 1] = ref[at, :, :, lanes]


def conv_rows(store, weights, taps, row, flipped, first):
    pieces = []
    for _, slot in taps:
        for b in range(3):
            piece = store[slot, pl.ds(row + b, TILE)]
            pieces.append(piece.reshape(TILE * VOX, store.shape[3]))
    stacked = jnp.concatenate(pieces, axis=1)
    products = []
    for c in range(3):
        if flipped:
            tiles = [weights[(2 - a) * 9 + (2 - b) * 3 + 2 - c] for a, _ in taps for b in range(3)]
            dims = (((1,), (1,)), ((), ()))
            tiles = jnp.concatenate(tiles, axis=1)
        else:
            rows = slice(first, first + store.shape[3])
            tiles = [weights[a * 9 + b * 3 + c, rows] for a, _ in taps for b in range(3)]
            dims = (((1,), (0,)), ((), ()))
            tiles = jnp.concatenate(tiles, axis=0)
        products.append(
            lax.dot_general(stacked, tiles, dims, preferred_element_type=jnp.float32)
        )
    left, middle, right = products
    column = lax.rem(lax.broadcasted_iota(jnp.int32, left.shape, 0), VOX)
    left = jnp.where(column > 0, pltpu.roll(left, 1, 0), 0.0)
    right = jnp.where(column < VOX - 1, pltpu.roll(right, TILE * VOX - 1, 0), 0.0)
    return middle + left + right


def conv_kernel(part, kind, flipped, finish, counts, lane, row, unroll, *refs):
    refs = list(refs)
    groups = []
    for count in counts:
        groups.append(refs[:count])
        refs = refs[count:]
    planes, pieces, begun, extra, outs = groups
    if kind == "ready":
        (weights,), copies = pieces, []
        (store,) = refs
    else:
        store, sems = refs
        weights = outs.pop()
        copies = copy_weights(kind, part, pieces, weights, sems)
    views = []
    for ref in planes:
        views += [(ref, at) for at in range(ref.shape[0])]
    fill_planes(part, views, store, lane)
    for copy in copies:
        copy.wait()
    for plane in range(2):
        taps = PARTS[part]["taps"][plane]

        @pl.loop(0, VOX // TILE, unroll=unroll)
        def _(step):
            rows = pl.ds(pl.multiple_of(step * TILE, TILE), TILE)
            value = shaped(conv_rows(store, weights, taps, step * TILE, flipped, row))
            if begun:
                value = value + begun[0][plane, rows]
            finish(value, plane, rows, extra, outs)


def finish_partial(value, plane, rows, extra, outs):
    outs[0][plane, rows] = value


def finish_first(value, plane, rows, extra, outs):
    outs[plane][0, rows] = leaky(value).astype(jnp.bfloat16)


def finish_second(value, plane, rows, extra, outs):
    output, deltas = outs[0], outs[1:]
    output[plane, rows] = leaky(value[:, :, :HALF]).astype(jnp.bfloat16)
    slope = slope_of(value)
    for lane, cot in ((0, extra[0]), (HALF, extra[1])):
        delta = cot[plane, rows].astype(jnp.float32) * slope[:, :, lane : lane + HALF]
        deltas[plane][0, rows, :, lane : lane + HALF] = delta.astype(jnp.bfloat16)


def finish_back(value, plane, rows, extra, outs):
    act = extra[plane][0, rows].astype(jnp.float32)
    outs[plane][0, rows] = (value * slope_of(act)).astype(jnp.bfloat16)


def finish_last(value, plane, rows, extra, outs):
    outs[0][plane, rows] = value.astype(jnp.bfloat16)


def filter_kernel(colours, *refs):
    low, mid_0, mid_1, high, delta_0, delta_1 = refs[:6]
    outs, (turned, moved) = refs[6:-2], refs[-2:]
    _, _, core = place()
    bits = place_bits()
    pixels = VOX * VOX
    seam = is_seam()
    sources = ((0, low), (1, mid_0), (2, mid_1), (3, high))
    for plane, ref in sources:
        flipped = ref[0].reshape(pixels, HALF).T
        for output_plane in range(2):
            tap = plane - output_plane
            if not 0 <= tap < 3:
                continue
            rows = slice(tap * HALF, (tap + 1) * HALF)
            columns = slice(output_plane * pixels, (output_plane + 1) * pixels)
            if plane in (1, 2) and tap != 1:
                turned[rows, columns] = jnp.where(seam, jnp.zeros_like(flipped), flipped)
            else:
                turned[rows, columns] = flipped
    for plane, ref in ((0, delta_0), (1, delta_1)):
        for c in range(3):
            moved[c, plane, 0] = jnp.zeros(moved.shape[3:], moved.dtype)
            moved[c, plane, VOX + 1] = jnp.zeros(moved.shape[3:], moved.dtype)
        moved[1, plane, 1 : VOX + 1] = ref[0]

        @pl.loop(0, VOX // TILE, unroll=True)
        def _(step):
            row = step * TILE
            values = ref[0, pl.ds(row, TILE)].reshape(TILE * VOX, FULL).astype(jnp.float32)
            column = lax.rem(lax.broadcasted_iota(jnp.int32, values.shape, 0), VOX)
            ahead = jnp.where(column < VOX - 1, pltpu.roll(values, TILE * VOX - 1, 0), 0.0)
            behind = jnp.where(column > 0, pltpu.roll(values, 1, 0), 0.0)
            moved[0, plane, pl.ds(row + 1, TILE)] = shaped(ahead.astype(jnp.bfloat16))
            moved[2, plane, pl.ds(row + 1, TILE)] = shaped(behind.astype(jnp.bfloat16))

    mine = lax.axis_index("chan") == core
    for tap in range(27):
        a, b, c = tap // 9, tap // 3 % 3, tap % 3
        if a:
            continue
        right = moved[c, :, 2 - b : 2 - b + VOX].reshape(2 * pixels, FULL)
        product = jnp.dot(turned[...], right, preferred_element_type=jnp.float32)
        kept = jnp.where(mine, product[:, :HALF], product[:, HALF:])
        sent = jnp.where(mine, product[:, HALF:], product[:, :HALF])
        for a in range(3):
            rows = slice(a * HALF, (a + 1) * HALF)
            for at, (first, taps, axis) in enumerate(colours):
                place_at = a * 9 + b * 3 + c - first
                if not 0 <= place_at < taps:
                    continue
                keep, far, near = outs[3 * at : 3 * at + 3]
                bit = bits[axis]
                keep[:, place_at] = kept[rows].reshape(8, 16, HALF)
                blocks = sent[rows].reshape(2, 4, 16, HALF).astype(far.dtype)
                far[:, place_at] = jnp.where(bit == 0, blocks[1], blocks[0])
                near[:, place_at] = jnp.where(bit == 0, blocks[0], blocks[1])


def halve_core_kernel(axis, keep, far, near, kept, sent):
    bit = place_bits()[axis]
    for target, came, first in ((kept, near, bit * 4), (sent, far, (1 - bit) * 4)):

        @pl.loop(0, 4)
        def _(block):
            total = keep[first + block] + came[block].astype(jnp.float32)
            target[block] = total.astype(target.dtype)


def halve_kernel(axis, keep, came, kept, sent):
    bit = place_bits()[axis]
    half = keep.shape[0] // 2
    for target, first in ((kept, bit * half), (sent, (1 - bit) * half)):
        for block in range(half):
            total = keep[first + block] + came[first + block].astype(jnp.float32)
            target[block] = total.astype(target.dtype)


def finish_kernel(scale, keep, came, total):
    total[...] = ((keep[...] + came[...].astype(jnp.float32)) * scale).astype(total.dtype)


def join_kernel(axis, own, came, target):
    bit = place_bits()[axis]
    half = own.shape[0]
    target[pl.ds(bit * half, half)] = own[...]
    target[pl.ds((1 - bit) * half, half)] = came[...]


def join_core_kernel(order, *refs):
    _, _, core = place()
    grad = refs[-1]
    first_tap = 0
    for own, came in zip(refs[0:-1:2], refs[1:-1:2]):
        base = first_tap
        first_tap += own.shape[1]

        @pl.loop(0, own.shape[1])
        def _(tap):
            for at, block in enumerate(order):
                rows = slice(block * 16, block * 16 + 16)
                first = jnp.where(core == 0, own[at, tap], came[at, tap])
                second = jnp.where(core == 0, came[at, tap], own[at, tap])
                grad[base + tap, rows, :HALF] = first.astype(jnp.float32)
                grad[base + tap, rows, HALF:] = second.astype(jnp.float32)


WEIGHT = {
    "sum_two_core": 0,
    "sum_two_z": 0,
    "sum_two_x": 2 * 10**9,
    "sum_a_core": 0,
    "sum_b_core": 0,
    "back_rim": 10**9,
    "sum_a_zz": 2 * 10**9,
    "sum_b_zz": 2 * 10**9,
    "join_a_zz": 2 * 10**9,
    "join_b_zz": 2 * 10**9,
    "join_a_z": 6 * 10**9,
    "join_b_x": 6 * 10**9,
    "join_a_x": 6 * 10**9,
    "join_b_z": 6 * 10**9,
}


def hint(flops):
    return pl.CostEstimate(flops=flops, bytes_accessed=0, transcendentals=0)


def small_call(kernel, outs, operands, name):
    return pl.pallas_call(
        kernel,
        out_shape=[jax.ShapeDtypeStruct(shape, dtype) for shape, dtype in outs],
        in_specs=[pl.BlockSpec(memory_space=pltpu.VMEM)] * len(operands),
        out_specs=[pl.BlockSpec(memory_space=pltpu.VMEM)] * len(outs),
        compiler_params=pltpu.CompilerParams(vmem_limit_bytes=VMEM_LIMIT),
        cost_estimate=hint(WEIGHT.get(name, SMALL)),
        name=name,
    )(*operands)


def halve_core(axis, keep, far, near, name):
    outs = [(far.shape, jnp.float32), (far.shape, jnp.bfloat16)]
    return small_call(functools.partial(halve_core_kernel, axis), outs, [keep, far, near], name)


def halve(axis, keep, came, name):
    shape = (keep.shape[0] // 2,) + keep.shape[1:]
    outs = [(shape, jnp.float32), (shape, jnp.bfloat16)]
    return small_call(functools.partial(halve_kernel, axis), outs, [keep, came], name)


def finish(scale, keep, came, name):
    outs = [(keep.shape, jnp.bfloat16)]
    return small_call(functools.partial(finish_kernel, scale), outs, [keep, came], name)[0]


def join(axis, own, came, name):
    outs = [((2 * own.shape[0],) + own.shape[1:], jnp.bfloat16)]
    return small_call(functools.partial(join_kernel, axis), outs, [own, came], name)[0]


def join_core(order, colours, name):
    outs = [((27, HALF, FULL), jnp.float32)]
    operands = [half for pair in colours for half in pair]
    return small_call(functools.partial(join_core_kernel, order), outs, operands, name)[0]


def conv_call(
    name, part, kind, finish, outs, planes, pieces, begun=(), extra=(), flipped=False,
    lane=0, lanes=None, row=0, unroll=True,
):
    lanes = lanes or planes[0].shape[3]
    height = {"own": HALF, "quarters": HALF, "both": FULL, "ready": pieces[0].shape[1]}[kind]
    ready = kind == "ready"
    if not ready:
        outs = outs + [((27, height, FULL), jnp.bfloat16)]
    operands = [*planes, *pieces, *begun, *extra]
    counts = (len(planes), len(pieces), len(begun), len(extra), len(outs))
    specs = [pl.BlockSpec(memory_space=pltpu.VMEM) for _ in operands]
    if not ready:
        for at in range(len(planes), len(planes) + len(pieces)):
            own = kind != "quarters" and at == len(planes)
            specs[at] = pl.BlockSpec(memory_space=pltpu.HBM if own else pl.ANY)
    scratch = [pltpu.VMEM((len(PARTS[part]["slots"]), VOX + 2, VOX, lanes), jnp.bfloat16)]
    if not ready:
        scratch.append(pltpu.SemaphoreType.DMA((20,)))
    return pl.pallas_call(
        functools.partial(conv_kernel, part, kind, flipped, finish, counts, lane, row, unroll),
        out_shape=[jax.ShapeDtypeStruct(shape, dtype) for shape, dtype in outs],
        in_specs=specs,
        out_specs=[pl.BlockSpec(memory_space=pltpu.VMEM)] * len(outs),
        scratch_shapes=scratch,
        compiler_params=pltpu.CompilerParams(vmem_limit_bytes=VMEM_LIMIT),
        cost_estimate=hint(WEIGHT.get(name, 0)),
        name=name,
    )(*operands)


def filter_call(colours, planes, mid_at, deltas, name):
    narrow = (1, VOX, VOX, HALF)
    specs = [
        pl.BlockSpec(narrow, functools.partial(lambda at, i: (at, 0, 0, 0), at)) for at in mid_at
    ]
    specs += [pl.BlockSpec((1, VOX, VOX, FULL), lambda i: (0, 0, 0, 0))] * 2
    outs = []
    for _, taps, _ in colours:
        for blocks, dtype in ((8, jnp.float32), (4, jnp.bfloat16), (4, jnp.bfloat16)):
            outs.append(jax.ShapeDtypeStruct((blocks, taps, 16, HALF), dtype))
    values = pl.pallas_call(
        functools.partial(filter_kernel, colours),
        grid=(1,),
        out_shape=outs,
        in_specs=specs,
        out_specs=[pl.BlockSpec(out.shape, lambda i: (0, 0, 0, 0)) for out in outs],
        scratch_shapes=[
            pltpu.VMEM((3 * HALF, 2 * VOX * VOX), jnp.bfloat16),
            pltpu.VMEM((3, 2, VOX + 2, VOX, FULL), jnp.bfloat16),
        ],
        compiler_params=pltpu.CompilerParams(vmem_limit_bytes=VMEM_LIMIT),
        cost_estimate=hint(0),
        name=name,
    )(*planes, *deltas)
    return [values[at : at + 3] for at in range(0, len(values), 3)]


def after(value, *earlier):
    return lax.optimization_barrier((value,) + earlier)[0]


def paired(volume, filter_one, filter_two, cotangent):
    count = lax.axis_size("dp")
    ahead = [(i, (i + 1) % count) for i in range(count)]
    behind = [(target, source) for source, target in ahead]
    scale = 1.0 / math.sqrt(count * 2 * VOX * VOX)
    one = filter_one.reshape(27, HALF, FULL)
    two = filter_two.reshape(27, HALF, FULL)
    _, side, core = place()

    def other(values):
        return lax.ppermute(values, "chan", [(0, 1), (1, 0)])

    def to_core(values):
        return lax.ppermute(values, "dp", [(i, i ^ 1) for i in range(count)])

    def to_side(values):
        return lax.ppermute(values, "dp", [(i, i ^ 2) for i in range(count)])

    def to_level(values):
        return lax.ppermute(values, "dp", [(i, i ^ 4) for i in range(count)])

    def to_far_level(values):
        return lax.ppermute(values, "dp", [(i, i ^ 8) for i in range(count)])

    def rims(first, last):
        return lax.ppermute(last, "dp", ahead), lax.ppermute(first, "dp", behind)

    wide = ((1, VOX, VOX, FULL), jnp.bfloat16)
    narrow = ((2, VOX, VOX, HALF), jnp.bfloat16)
    partial = ((2, VOX, VOX, FULL), jnp.float32)
    half_partial = ((2, VOX, VOX, HALF), jnp.float32)

    low_own, high_own = rims(volume[:1], volume[1:])
    one_0 = other(lax.dynamic_slice_in_dim(one, (2 * side + core) * 32, 32, axis=1))
    volume_other = other(after(volume, one_0, low_own, high_own))
    one_1 = to_side(one_0)
    one_2 = to_core(one_0)
    begun, own_ready = conv_call(
        "first_own", "all", "own", finish_partial, [partial], [low_own, volume, high_own], [one],
        unroll=False,
    )
    one_3 = to_core(after(one_1, begun))
    quarters = [one_0, one_1, one_2, one_3]
    volume_other = after(volume_other, begun)
    two_came = [
        other(after(lax.dynamic_slice_in_dim(two, core * 64 + at, 32, axis=1), volume_other))
        for at in (0, 32)
    ]
    low_other, high_other = rims(volume_other[:1], volume_other[1:])
    begun, ready = conv_call(
        "first_other", "local", "quarters", finish_partial, [partial], [volume_other], quarters,
        [begun],
    )
    act_0, act_1 = conv_call(
        "first_rim", "rim", "ready", finish_first, [wide, wide], [low_other, high_other],
        [ready], [begun],
    )
    low_act, high_act = rims(act_0, act_1)
    cot_other = other(after(cotangent, act_0))
    begun, _ = conv_call(
        "second_own", "local", "own", finish_partial, [partial], [act_0, act_1], [two], lanes=HALF,
        unroll=False,
    )
    two_came = [after(part, begun) for part in two_came]
    pieces = [two] + two_came + [to_core(part) for part in two_came]
    begun, ready = conv_call(
        "second_other", "local", "both", finish_partial, [partial], [act_0, act_1], pieces, [begun],
        lane=HALF, lanes=HALF, row=HALF,
    )
    output, delta_0, delta_1 = conv_call(
        "second_rim", "rim", "ready", finish_second, [narrow, wide, wide], [low_act, high_act],
        [ready], [begun], [cotangent, cot_other],
    )
    low_delta, high_delta = rims(delta_0, delta_1)
    ((keep, far, near),) = filter_call(
        ((0, 27, "z"),), [low_act, act_0, act_1, high_act], (0, 0, 0, 0), [delta_0, delta_1],
        "grad_two",
    )
    keep_two, sent = halve_core("z", keep, to_core(far), to_core(near), "sum_two_core")
    came_two = to_level(sent)
    (begun,) = conv_call(
        "back_local", "local", "ready", finish_partial, [partial], [delta_0, after(delta_1, keep_two)],
        [ready], flipped=True,
    )
    prior_0, prior_1 = conv_call(
        "back_rim", "rim", "ready", finish_back, [wide, wide], [low_delta, high_delta],
        [ready], [begun], [act_0, act_1], flipped=True,
    )
    low_prior, high_prior = rims(prior_0, prior_1)
    (keep_a, *sent_a), (keep_b, *sent_b) = filter_call(
        ((0, 14, "x"), (14, 13, "z")), [low_own, volume, volume, high_own], (0, 0, 1, 0),
        [prior_0, prior_1], "grad_one",
    )
    sent_a, sent_b = [to_core(half) for half in sent_a], [to_core(half) for half in sent_b]
    keep_two, sent = halve("x", after(keep_two, keep_a), came_two, "sum_two_z")
    came_two = to_side(sent)
    keep_a, sent = halve_core("x", after(keep_a, keep_two), *sent_a, "sum_a_core")
    came_a = to_side(sent)
    keep_b, sent = halve_core("z", after(keep_b, keep_a), *sent_b, "sum_b_core")
    came_b = to_level(sent)
    (begun,) = conv_call(
        "first_back_local", "local", "ready", finish_partial, [half_partial],
        [after(prior_0, keep_b), prior_1], [own_ready], flipped=True, unroll=False,
    )
    keep_two, sent = halve("zz", after(keep_two, begun, low_prior, high_prior), came_two, "sum_two_x")
    came_two = to_far_level(sent)
    keep_a, sent = halve("z", after(keep_a, keep_two), came_a, "sum_a_x")
    came_a = to_level(sent)
    keep_b, sent = halve("x", after(keep_b, keep_a), came_b, "sum_b_z")
    came_b = to_side(sent)
    own_two = finish(scale, after(keep_two, keep_b), came_two, "sum_two_zz")
    came_two = to_far_level(own_two)
    keep_a, sent = halve("zz", after(keep_a, own_two), came_a, "sum_a_z")
    came_a = to_far_level(sent)
    keep_b, sent = halve("zz", after(keep_b, keep_a), came_b, "sum_b_x")
    came_b = to_far_level(sent)
    own_two = join("zz", after(own_two, keep_b), came_two, "join_two_zz")
    came_two = to_level(own_two)
    own_a = finish(scale, after(keep_a, own_two), came_a, "sum_a_zz")
    came_a = to_far_level(own_a)
    own_b = finish(scale, after(keep_b, own_a), came_b, "sum_b_zz")
    came_b = to_far_level(own_b)
    own_two = join("z", after(own_two, own_b), came_two, "join_two_z")
    came_two = to_side(own_two)
    own_a = join("zz", after(own_a, own_two), came_a, "join_a_zz")
    came_a = to_level(own_a)
    own_b = join("zz", after(own_b, own_a), came_b, "join_b_zz")
    came_b = to_side(own_b)
    own_a = join("z", after(own_a, own_b), came_a, "join_a_z")
    came_a = to_side(own_a)
    own_b = join("x", after(own_b, own_a), came_b, "join_b_x")
    came_b = to_level(own_b)
    (input_grad,) = conv_call(
        "first_back_rim", "rim", "ready", finish_last, [narrow],
        [after(low_prior, own_b), high_prior], [own_ready], [begun], flipped=True,
    )
    own_two = join("x", after(own_two, input_grad), came_two, "join_two_x")
    came_two = to_core(own_two)
    own_a = join("x", after(own_a, own_two), came_a, "join_a_x")
    came_a = to_core(own_a)
    own_b = join("z", after(own_b, own_a), came_b, "join_b_z")
    came_b = to_core(own_b)
    summed_two = join_core(
        (0, 1, 4, 5, 2, 3, 6, 7), [(after(own_two, own_b), came_two)], "grads_two"
    )
    summed_one = join_core(
        tuple(range(8)), [(after(own_a, summed_two), came_a), (own_b, came_b)], "grads_one"
    )
    shape = filter_one.shape
    return output, input_grad, summed_one.reshape(shape), summed_two.reshape(shape)


def local(volume, filter_one, filter_two, cotangent):
    pair = lax.axis_size("chan") == 2 and lax.axis_size("dp") == 16
    if pair and volume.shape == (2, VOX, VOX, HALF):
        return paired(volume, filter_one, filter_two, cotangent)
    return plain(volume, filter_one, filter_two, cotangent)


def solution(mesh):
    in_specs = (
        P("dp", None, None, "chan"),
        P(None, None, None, "chan", None),
        P(None, None, None, "chan", None),
        P("dp", None, None, "chan"),
    )
    out_specs = (
        P("dp", None, None, "chan"),
        P("dp", None, None, "chan"),
        P(None, None, None, "chan", None),
        P(None, None, None, "chan", None),
    )
    return jax.shard_map(local, mesh=mesh, in_specs=in_specs, out_specs=out_specs, check_vma=False)
```
